32 devices in a mesh: doc: 4 (over y, x), seq: 8 (over z, core).
Axes of the slice: x: 2, y: 2, z: 4, core: 2. Of those that a mesh axis runs over, the one named last changes fastest.
Arguments:
- inputs: bfloat16 [16, 1024, 768], P('doc', 'seq'), may hold values from -6 to 6
- question_count: int32 [16], P('doc'), may hold values from 1 to 64, as said below
- question_at: int32 [16, 64], P('doc'), may hold values from 0 to 1023
- local_proj: bfloat16 [2, 768, 2304], replicated, may hold values from -0.21875 to 0.21875
- local_mixer: bfloat16 [2, 768, 768], replicated, may hold values from -1.25 to 1.25
- pooled_proj: bfloat16 [2, 768, 2304], replicated, may hold values from -0.21875 to 0.21875
- pool_taps: float32 [2, 2, 5, 768], replicated, may hold values from -3 to 3
- pooled_mixer: bfloat16 [2, 768, 768], replicated, may hold values from -2.5 to 2.5
- expand_weight: bfloat16 [2, 768, 3072], replicated, may hold values from -0.21875 to 0.21875
- reduce_weight: bfloat16 [2, 3072, 768], replicated, may hold values from -0.109375 to 0.109375
- norm_gain: float32 [2, 3, 768], replicated, may hold values from 0.5 to 1.5
- norm_shift: float32 [2, 3, 768], replicated, may hold values from -1 to 1
- output_grad: bfloat16 [16, 1024, 768], P('doc', 'seq'), may hold values from -6 to 6
Outputs:
- outputs: bfloat16 [16, 1024, 768], P('doc', 'seq')
- input_grad: float32 [16, 1024, 768], P('doc', 'seq')
- local_proj_grad: float32 [2, 768, 2304], P(None, None, 'seq')
- local_mixer_grad: float32 [2, 768, 768], P(None, 'seq')
- pooled_query_grad: float32 [2, 768, 768], P(None, None, 'seq')
- pooled_kv_grad: float32 [2, 768, 1536], P(None, None, 'seq')
- pool_taps_grad: float32 [2, 2, 5, 768], P(None, None, None, 'seq')
- pooled_mixer_grad: float32 [2, 768, 768], P(None, 'seq')
- expand_grad: float32 [2, 768, 3072], P(None, None, 'seq')
- reduce_grad: float32 [2, 3072, 768], P(None, 'seq')
- gain_grad: float32 [2, 3, 768], P(None, None, 'seq')
- shift_grad: float32 [2, 3, 768], P(None, None, 'seq')
The draws below stay inside these ranges and needn't reach their ends.
Inputs may be any that keep to these rules, and one draw needn't show every extreme that they name: `question_count`: each document has at least one and at most 64 question tokens, and some document has exactly 64. `question_at`: entries of a row past that document's question count are not read; positions may repeat.
All inputs are finite; a program needn't handle non-finite values.
Results may differ from the reference program's by a relative error of at most 0.022.
Values may be sent and summed in bfloat16 or wider, within the bound.
A program may use at most 512 MiB of HBM per device.

```python
import math
import jax
import jax.numpy as jnp
from jax import lax

D = 768
HD = 64
FF = 3072
NL = 2
LOCAL_WIN = 128
POOL_WIN = 512
QMAX = 64
DOCS = 16
LEN = 1024


def draw_question_count(key, part):
    key = jax.random.fold_in(key, 11)
    first_key, second_key = jax.random.split(key)
    counts = jax.random.randint(first_key, (DOCS,), 1, QMAX + 1)
    chosen = jax.random.randint(second_key, (), 0, DOCS)
    return jnp.where(jnp.arange(DOCS) == chosen, QMAX, counts).astype(jnp.int32)


def plant(result, own_key, smallest, high):
    index_at = [jax.random.randint(jax.random.fold_in(own_key, axis), (), 0, length) for axis, length in enumerate(result.shape)]
    main_axis = result.shape.index(max(result.shape))
    beside = index_at[:main_axis] + [(index_at[main_axis] + 1) % result.shape[main_axis]] + index_at[main_axis + 1:]
    return result.at[tuple(index_at)].set(smallest).at[tuple(beside)].set(high)


def shard_levels(key, dims, pieces, smallest, largest):
    level, own = 1.0, jax.random.fold_in(key, 6)
    for position, parts in pieces:
        draws = jnp.exp(jax.random.uniform(jax.random.fold_in(own, position), (parts,), jnp.float32, smallest / len(pieces), largest / len(pieces)))
        level = level * jnp.repeat(draws, dims[position] // parts).reshape([-1 if axis == position else 1 for axis in range(len(dims))])
    return level


def normal_values(stream_key, extent, scale, most, shards=(), kind=jnp.bfloat16):
    result = jax.random.normal(stream_key, extent, jnp.float32) * scale
    if len(shards) > 0:
        result = shard_levels(stream_key, extent, shards, -0.22, 0.18) * result
    return jnp.clip(result, min=-most, max=most).astype(kind)


def setup_inputs(seed: int = 0) -> dict:
    key_of = jax.random.split(jax.random.key(seed), 14)
    return {
        "inputs": normal_values(key_of[0], (DOCS, LEN, D), 1.0, 6.0, ((0, 4), (1, 8))),
        "question_count": draw_question_count(jax.random.fold_in(key_of[13], 71), 0),
        "question_at": plant(jax.random.randint(key_of[2], (DOCS, QMAX), 0, LEN), jax.random.fold_in(key_of[2], 1), 0, LEN - 1).astype(jnp.int32),
        "local_proj": normal_values(key_of[3], (NL, D, 3 * D), D ** -0.5, 0.21875),
        "local_mixer": normal_values(key_of[4], (NL, D, D), (D // 32) ** -0.5, 1.25),
        "pooled_proj": normal_values(key_of[5], (NL, D, 3 * D), D ** -0.5, 0.21875),
        "pool_taps": normal_values(key_of[6], (NL, 2, 5, D), 0.5, 3.0, (), jnp.float32),
        "pooled_mixer": normal_values(key_of[7], (NL, D, D), (max(D // 128, 1)) ** -0.5, 2.5),
        "expand_weight": normal_values(key_of[8], (NL, D, FF), D ** -0.5, 0.21875),
        "reduce_weight": normal_values(key_of[9], (NL, FF, D), FF ** -0.5, 0.109375),
        "norm_gain": jnp.clip(1.0 + 0.1 * jax.random.normal(key_of[10], (NL, 3, D), jnp.float32), 0.5, 1.5),
        "norm_shift": normal_values(key_of[11], (NL, 3, D), 0.2, 1.0, (), jnp.float32),
        "output_grad": normal_values(key_of[12], (DOCS, LEN, D), 1.0, 6.0, ((0, 4), (1, 8))),
    }


PRECISE = lax.Precision.HIGHEST
EPSILON = 1e-05
MASKED = -1e+30

@jax.custom_vjp
def low(v):
    return lax.optimization_barrier(v.astype(jnp.bfloat16)).astype(jnp.float32)

@jax.custom_vjp
def low_back(v):
    return v

def low_keep(v):
    return (low(v), None)

def low_pass(kept, grad):
    return (grad,)

def back_keep(v):
    return (v, None)

def back_low(kept, grad):
    return (low(grad),)
low.defvjp(low_keep, low_pass)
low_back.defvjp(back_keep, back_low)

def round_both(value):
    return low_back(low(value))

def layer_norm(summed, gain, shift_bias):
    centre = summed - lax.optimization_barrier(jnp.mean(summed, -1, keepdims=True))
    spread = lax.optimization_barrier(jnp.mean(centre * centre, -1, keepdims=True))
    return centre * lax.rsqrt(spread + EPSILON) * gain + shift_bias

def attend_rows(queries, key_rows, value_rows, allowed):
    factor = queries.shape[-1] ** (-0.5)
    scores = low_back(jnp.einsum('qhe,khe->hqk', queries, key_rows, precision=PRECISE) * factor)
    scores = jnp.where(allowed[None], scores, MASKED)
    row_top = lax.optimization_barrier(jnp.max(scores, -1, keepdims=True))
    raised = jnp.exp(scores - row_top)
    soft_weights = low(raised / lax.optimization_barrier(jnp.sum(raised, -1, keepdims=True)))
    return jnp.einsum('hqk,khe->qhe', soft_weights, value_rows, precision=PRECISE)

def local_attention(queries, key_rows, value_rows):
    length = queries.shape[0]
    half_win = LOCAL_WIN // 2
    block_rows = math.gcd(length, 512)
    pad_width = ((half_win, half_win), (0, 0), (0, 0))
    key_pad = jnp.pad(key_rows, pad_width)
    value_pad = jnp.pad(value_rows, pad_width)

    def one_block(first_row):
        query_block = lax.dynamic_slice_in_dim(queries, first_row, block_rows, 0)
        key_block = lax.dynamic_slice_in_dim(key_pad, first_row, block_rows + 2 * half_win, 0)
        value_block = lax.dynamic_slice_in_dim(value_pad, first_row, block_rows + 2 * half_win, 0)
        row_index = first_row + jnp.arange(block_rows, dtype=jnp.int32)
        col_index = first_row - half_win + jnp.arange(block_rows + 2 * half_win, dtype=jnp.int32)
        allowed = (jnp.abs(row_index[:, None] - col_index[None, :]) <= half_win) & (col_index[None, :] >= 0) & (col_index[None, :] < length)
        return attend_rows(query_block, key_block, value_block, allowed)
    starts = jnp.arange(0, length, block_rows, dtype=jnp.int32)
    return lax.map(jax.checkpoint(one_block), starts).reshape(queries.shape)

def pooled_attention(queries, pool_keys, pool_values, question):
    length = queries.shape[0]
    block_rows = math.gcd(length, 512)
    col_index = jnp.arange(pool_keys.shape[0], dtype=jnp.int32)

    def one_block(first_row):
        query_block = lax.dynamic_slice_in_dim(queries, first_row, block_rows, 0)
        row_index = first_row + jnp.arange(block_rows, dtype=jnp.int32)
        asking = lax.dynamic_slice_in_dim(question, first_row, block_rows, 0)
        allowed = (jnp.abs(col_index[None, :] - row_index[:, None] // 4) <= POOL_WIN // 2) | asking[:, None]
        return attend_rows(query_block, pool_keys, pool_values, allowed)
    starts = jnp.arange(0, length, block_rows, dtype=jnp.int32)
    return lax.map(jax.checkpoint(one_block), starts).reshape(queries.shape)

def pooling(token_rows, taps):
    length = token_rows.shape[0]
    padded = jnp.pad(token_rows, ((2, 2), (0, 0)))
    total = taps[0] * padded[0:length:4]
    for tap_at in range(1, 5):
        total = total + taps[tap_at] * padded[tap_at:tap_at + length:4]
    return total

def layer_forward(hidden_in, weight_set, layer_at, question):
    local_proj, local_mixer, pooled_proj, pool_taps, pooled_mixer, expand_weight, reduce_weight, norm_gain, norm_shift = weight_set
    length, width = hidden_in.shape
    heads = width // HD
    in_rows = low(hidden_in)
    local_heads = round_both(jnp.dot(in_rows, local_proj[layer_at], precision=PRECISE)).reshape(length, 3, heads, HD)
    local_result = local_attention(local_heads[:, 0], local_heads[:, 1], local_heads[:, 2])
    local_mix = round_both(local_result.reshape(length, width))
    first_sum = hidden_in + low_back(jnp.dot(local_mix, local_mixer[layer_at], precision=PRECISE))
    first_norm = layer_norm(first_sum, norm_gain[layer_at, 0], norm_shift[layer_at, 0])
    second_in = low(first_norm)
    pooled_heads = round_both(jnp.dot(second_in, pooled_proj[layer_at], precision=PRECISE)).reshape(length, 3, width)
    pool_keys = low(pooling(pooled_heads[:, 1], pool_taps[layer_at, 0])).reshape(length // 4, heads, HD)
    pool_values = low(pooling(pooled_heads[:, 2], pool_taps[layer_at, 1])).reshape(length // 4, heads, HD)
    pooled_result = pooled_attention(pooled_heads[:, 0].reshape(length, heads, HD), pool_keys, pool_values, question)
    pooled_mix = round_both(pooled_result.reshape(length, width))
    second_sum = first_norm + low_back(jnp.dot(pooled_mix, pooled_mixer[layer_at], precision=PRECISE))
    second_norm = layer_norm(second_sum, norm_gain[layer_at, 1], norm_shift[layer_at, 1])
    ffn_in = low(second_norm)
    up_proj = low_back(jnp.dot(ffn_in, expand_weight[layer_at], precision=PRECISE))
    activated = low(jax.nn.gelu(up_proj, approximate=False))
    third_sum = second_norm + low_back(jnp.dot(activated, reduce_weight[layer_at], precision=PRECISE))
    return layer_norm(third_sum, norm_gain[layer_at, 2], norm_shift[layer_at, 2])

def reference(inputs, question_count, question_at, local_proj, local_mixer, pooled_proj, pool_taps, pooled_mixer, expand_weight, reduce_weight, norm_gain, norm_shift, output_grad):
    weights = jax.tree.map(lambda weight_arr: weight_arr.astype(jnp.float32), (local_proj, local_mixer, pooled_proj, pool_taps, pooled_mixer, expand_weight, reduce_weight, norm_gain, norm_shift))
    length = inputs.shape[1]
    width = inputs.shape[2]
    positions = jnp.arange(length, dtype=jnp.int32)
    slots = jnp.arange(question_at.shape[1], dtype=jnp.int32)

    def one_doc(totals, doc_item):
        doc_in, doc_count, doc_places, doc_grad = doc_item
        question = jnp.any((doc_places[None, :] == positions[:, None]) & (slots[None, :] < doc_count), axis=1)

        def forward(hidden_in, weight_set):
            for layer_at in range(NL):
                hidden_in = layer_forward(hidden_in, weight_set, layer_at, question)
            return hidden_in
        doc_out, pull_back = jax.vjp(forward, doc_in.astype(jnp.float32), weights)
        grad_in, grad_weights = pull_back(doc_grad.astype(jnp.float32))
        totals = jax.tree.map(jnp.add, totals, grad_weights)
        return (totals, (doc_out.astype(jnp.bfloat16), grad_in))
    zero_grads = jax.tree.map(jnp.zeros_like, weights)
    totals, (outputs, grad_inputs) = lax.scan(one_doc, zero_grads, (inputs, question_count, question_at, output_grad))
    pooled_total = totals[2]
    return (outputs, grad_inputs, totals[0], totals[1], pooled_total[:, :, :width], pooled_total[:, :, width:], totals[3], totals[4], totals[5], totals[6], totals[7], totals[8])
```

```python
from types import SimpleNamespace

import jax
import jax.numpy as jnp
from jax import lax
from jax.experimental import pallas as pl
from jax.experimental.pallas import tpu as pltpu
from jax.sharding import PartitionSpec as P

HD = 64
LOCAL_WIN = 128
POOL_WIN = 512
EPSILON = 1e-05
MASKED = -1e30
F32 = jnp.float32
BF16 = jnp.bfloat16
MESH = pl.DeviceIdType.MESH
ANY = pl.BlockSpec(memory_space=pl.ANY)
VMEM = pl.BlockSpec(memory_space=pltpu.VMEM)
VMEM_LIMIT = 60 * 1024 * 1024


def dot_nn(left, right):
    return jnp.dot(left, right, preferred_element_type=F32)


def dot_nt(left, right):
    return lax.dot_general(left, right, (((1,), (1,)), ((), ())), preferred_element_type=F32)


def dot_tn(left, right):
    return lax.dot_general(left, right, (((0,), (0,)), ((), ())), preferred_element_type=F32)


def loop(count, body):
    def step(i, carry):
        body(i)
        return carry

    lax.fori_loop(0, count, step, 0)


def aligned(index, size):
    return pl.ds(pl.multiple_of(index * size, size), size)


class Copies:
    def __init__(self, sems):
        self.sems = sems
        self.used = 0

    def start(self, source, target):
        copy = pltpu.make_async_copy(source, target, self.sems.at[self.used])
        self.used += 1
        copy.start()
        return copy


class Links:
    def __init__(self, send, recv):
        self.send, self.recv = send, recv
        self.used = 0

    def take(self):
        self.used += 1
        return self.used - 1

    def start(self, source, target, device):
        at = self.take()
        copy = pltpu.make_async_remote_copy(
            src_ref=source,
            dst_ref=target,
            send_sem=self.send.at[at],
            recv_sem=self.recv.at[at],
            device_id=device,
            device_id_type=MESH,
        )
        copy.start()
        return copy


def greet(devices):
    barrier = pltpu.get_barrier_semaphore()
    for device in devices:
        pl.semaphore_signal(barrier, inc=1, device_id=device, device_id_type=MESH)
    pl.semaphore_wait(barrier, len(devices))


class Regroup:
    def __init__(self, copies, links, source, target, gather):
        self.doc, self.me = lax.axis_index("doc"), lax.axis_index("seq")
        self.source, self.target = source, target
        self.gather = gather
        self.copies, self.links = copies, links
        self.local = copies.used
        copies.used += 1
        self.first = links.used
        links.used += 4

    def _to(self, i):
        if self.gather:
            return 2 * i + self.me // 4, self.me % 4
        return 4 * (self.me % 2) + i, self.me // 2

    def _from(self, i):
        if self.gather:
            return 4 * (self.me % 2) + i
        return 2 * i + self.me // 4

    def _remote(self, i, slot, device):
        return pltpu.make_async_remote_copy(
            src_ref=self.source.at[i],
            dst_ref=self.target.at[slot],
            send_sem=self.links.send.at[self.first + i],
            recv_sem=self.links.recv.at[self.first + slot],
            device_id=(self.doc, device),
            device_id_type=MESH,
        )

    def _local(self, i, slot):
        return pltpu.make_async_copy(
            self.source.at[i], self.target.at[slot], self.copies.sems.at[self.local]
        )

    def start(self):
        for i in range(4):
            device, slot = self._to(i)

            @pl.when(device == self.me)
            def _():
                self._local(i, slot).start()

            @pl.when(device != self.me)
            def _():
                self._remote(i, slot, device).start()

    def wait(self):
        for i in range(4):
            device, slot = self._to(i)

            @pl.when(device == self.me)
            def _():
                self._local(i, slot).wait()

            @pl.when(device != self.me)
            def _():
                self._remote(i, slot, device).wait_send()

        for i in range(4):

            @pl.when(self._from(i) != self.me)
            def _():
                self._remote(i, i, self._from(i)).wait_recv()


def regroup_peers():
    me = lax.axis_index("seq")
    return [2 * i + me // 4 for i in range(4)], [4 * (me % 2) + i for i in range(4)]


def greet_regroup(others):
    doc, me = lax.axis_index("doc"), lax.axis_index("seq")
    barrier = pltpu.get_barrier_semaphore()
    to, back = regroup_peers()
    for device in to + back:

        @pl.when(device != me)
        def _():
            pl.semaphore_signal(barrier, inc=1, device_id=(doc, device), device_id_type=MESH)

    for device in others:
        pl.semaphore_signal(barrier, inc=1, device_id=device, device_id_type=MESH)
    inside = me // 4 == me % 2
    pl.semaphore_wait(barrier, len(others) + jnp.where(inside, 6, 8))


def split_masks(width):
    lane = lax.broadcasted_iota(jnp.int32, (1, 2 * HD), 1)
    low = (lane < HD).astype(F32)
    return low, 1.0 - low


def by_head(rows, low, high, factor):
    wide = rows.astype(F32) * factor
    return jnp.concatenate([wide * low, wide * high], 0).astype(BF16)


def from_heads(stacked, low, high):
    rows = stacked.shape[0] // 2
    return stacked[:rows] * low + stacked[rows:] * high


def attend_blocks(queries, key_rows, value_rows, bias):
    low, high = split_masks(2 * HD)
    wide_bias = jnp.concatenate([bias, bias], 0)
    scores = [
        dot_nt(by_head(query, low, high, HD**-0.5), key) + wide_bias
        for query, key in zip(queries, key_rows)
    ]
    soft = []
    for score in scores:
        raised = jnp.exp(score - jnp.max(score, -1, keepdims=True))
        soft.append((raised.astype(BF16), 1.0 / jnp.sum(raised, -1, keepdims=True)))
    return [
        from_heads(dot_nn(raised, value) * share, low, high).astype(BF16)
        for (raised, share), value in zip(soft, value_rows)
    ]


def local_bias(at, blocks, length_first, length_last, rows, half):
    shape = (rows, rows + 2 * half)
    query = lax.broadcasted_iota(jnp.int32, shape, 0)
    key = lax.broadcasted_iota(jnp.int32, shape, 1)
    first = jnp.where(length_first & (at == 0), half, 0)
    last = jnp.where(length_last & (at == blocks - 1), rows + half, rows + 2 * half)
    seen = (key >= query) & (key <= query + 2 * half) & (key >= first) & (key < last)
    return jnp.where(seen, 0.0, MASKED).astype(F32)


def norm_rows(summed, gain, shift):
    centre = summed - jnp.mean(summed, -1, keepdims=True)
    spread = jnp.mean(centre * centre, -1, keepdims=True)
    rate = lax.rsqrt(spread + EPSILON)
    plain = centre * rate
    return plain, rate, plain * gain + shift


def gelu_rows(u):
    z = jnp.abs(u) * (0.5**0.5)
    t = 1.0 / (1.0 + 0.3275911 * z)
    series = 1.061405429 * t - 1.453152027
    series = series * t + 1.421413741
    series = series * t - 0.284496736
    series = series * t + 0.254829592
    bell = jnp.exp(-(z * z))
    tail = 0.5 * series * t * bell
    share = jnp.where(u < 0, tail, 1.0 - tail)
    return u * share, share + u * bell * 0.3989422804014327


def vmem(shape, kind=BF16):
    return pltpu.VMEM(shape, kind)


class Scratch:
    def __init__(self):
        self.names, self.shapes = [], []

    def add(self, tag="", **shapes):
        for name, shape in shapes.items():
            self.names.append(tag + name)
            self.shapes.append(shape)

    def plane(self, tag, block):
        first = vmem((2, 2, 4, 2) + block)
        second, total = vmem((2, 2, 4) + block), vmem((2, 4, 2) + block)
        self.add(tag, kept=first, got1=first, got2=second, total=total)

    def line(self, tag, block):
        whole = vmem((2, 2, 2, 2) + block)
        self.add(tag, own=vmem((2, 2) + block), got=vmem((2, 3, 2) + block), whole=whole)

    def core(self, tag, block):
        group = vmem((2, 4, 2, 2, 2) + block)
        self.add(tag, send=group, mine=group, got=group)

    def sems(self, loads, saves, links):
        dma = pltpu.SemaphoreType.DMA
        self.add(load_sems=dma((loads,)), save_sems=dma((saves,)))
        self.add(send_sems=dma((links,)), recv_sems=dma((links,)))

    def bring(self, args, **arrays):
        for name, array in arrays.items():
            args[name] = (array, ANY)
            self.names.append("v_" + name)
            self.shapes.append(pltpu.VMEM(array.shape, array.dtype))


class Kernel:
    def __init__(self, names, refs):
        self.__dict__.update(zip(names, refs))
        assert len(names) == len(refs)
        self.loads = Copies(self.load_sems)
        self.saves = Copies(self.save_sems)
        self.links = Links(self.send_sems, self.recv_sems)
        self.waits = []

    def load(self, source, target):
        return self.loads.start(source, target)

    def load_all(self, names):
        return {name: self.load(getattr(self, name), getattr(self, "v_" + name)) for name in names}

    def save(self, source, target):
        self.waits.append(self.saves.start(source, target))

    def done(self):
        for wait in self.waits:
            wait.wait()


def run_kernel(body, name, collective, args, outs, scratch):
    names = list(args) + list(outs) + scratch.names

    def kernel(*refs):
        body(Kernel(names, refs))

    made = pl.pallas_call(
        kernel,
        out_shape=[jax.ShapeDtypeStruct(shape, kind) for shape, kind in outs.values()],
        in_specs=[spec for _, spec in args.values()],
        out_specs=[ANY] * len(outs),
        scratch_shapes=scratch.shapes,
        compiler_params=pltpu.CompilerParams(
            collective_id=collective,
            has_side_effects=collective is not None,
            vmem_limit_bytes=VMEM_LIMIT,
        ),
        name=name,
    )(*(array for array, _ in args.values()))
    return SimpleNamespace(**dict(zip(outs, made)))


def turn(source, target):
    for i in range(0, source.shape[1], 128):
        target[i : i + 128] = source[:, i : i + 128].T


GAIN, SHIFT, TAPS = 0, 3, 6


def small_row(k, layer, row, lane=None, count=None):
    lanes = slice(None) if lane is None else slice(lane, lane + count)
    return k.small[layer, row : row + 1, lanes]


def fill_pooled_bias(k, rows, core):
    doc = lax.axis_index("seq") // 2
    places = k.places[pl.ds(doc, 1)]
    slot = lax.broadcasted_iota(jnp.int32, (128, places.shape[1]), 1)
    column = lax.broadcasted_iota(jnp.int32, (128, rows // 2), 1)
    for i in range(0, rows, 128):
        here = core * rows + i
        position = lax.broadcasted_iota(jnp.int32, (128, places.shape[1]), 0) + here
        hit = (position == places) & (slot < k.counts[doc])
        question = jnp.max(hit.astype(F32), -1, keepdims=True)
        own = (lax.broadcasted_iota(jnp.int32, (128, rows // 2), 0) + here) // 4
        near = jnp.where(jnp.abs(column - own) <= POOL_WIN // 2, 1.0, 0.0)
        bias = jnp.where(near + question > 0.5, 0.0, MASKED).astype(F32)
        k.pbias[i : i + 128] = bias
        k.pbias_t[:, i : i + 128] = bias.T


def forward(k, layer, first, last, rows, width, ff):
    half = LOCAL_WIN // 2
    pool = rows // 4
    blocks = rows // 128
    pairs = width // (2 * HD)
    lanes_of = [slice(2 * HD * pair, 2 * HD * (pair + 1)) for pair in range(pairs)]
    values_of = [slice(width + s.start, width + s.stop) for s in lanes_of]
    core = lax.axis_index("seq") % 2
    sibling = axis_peers()[0]
    links = k.links

    def weight(source, target):
        return k.load(source.at[layer], target)

    got_small = k.load(k.small_in, k.small)
    if not first:
        got_x = k.load(k.x_in, k.xf)
    got = [weight(k.w_local, k.wl)]
    if first:
        greet_regroup([sibling])
        incoming = Regroup(k.loads, links, k.x_in, k.x, True)
        incoming.start()
        background = Regroup(k.loads, links, k.grad_in, k.grad_got, True)
        fill_pooled_bias(k, rows, core)
        k.save(k.pbias, k.o_pbias)
        k.save(k.pbias_t, k.o_pbias_t)
    else:
        greet([sibling])
    for i in range(blocks):
        k.lbias[i] = local_bias(i, blocks, core == 0, core == 1, 128, half)
    k.kvf[:, pl.ds(0, 8)] = jnp.zeros((2 * width // 128, 8, 128), F32)

    if first:
        incoming.wait()
        xrows = k.x.reshape(rows, width)
    else:
        got_x.wait()
        xrows = k.x
        for i in range(0, rows, 128):
            k.x[i : i + 128] = k.xf[i : i + 128].astype(BF16)
    k.save(k.x, k.o_x)
    got += [weight(k.w_mix, k.wm), weight(k.w_pooled, k.wp)]
    if not first:
        got_bias = k.load(k.pbias_in, k.pbias)

    got[0].wait()
    for i in range(0, 2 * width, 256):
        k.kv[half : half + rows, i : i + 256] = dot_nn(
            xrows[...], k.wl[:, width + i : width + i + 256]
        ).astype(BF16)
    rim = links.start(
        k.kv.at[pl.ds(pl.multiple_of(half + (rows - half) * (1 - core), half), half)],
        k.halo,
        sibling,
    )
    for i in range(0, width, 256):
        k.q[:, i : i + 256] = dot_nn(xrows[...], k.wl[:, i : i + 256]).astype(BF16)
    k.save(k.q, k.o_q)
    rim.wait()
    k.kv[pl.ds(pl.multiple_of((rows + half) * (1 - core), half), half)] = k.halo[...]
    k.kv[pl.ds(pl.multiple_of((rows + half) * core, half), half)] = jnp.zeros_like(k.halo)
    k.save(k.kv, k.o_kv)

    def attend_local(i):
        here, seen = aligned(i, 128), pl.ds(pl.multiple_of(i * 128, 128), 128 + 2 * half)
        mixed = attend_blocks(
            [k.q[here, lanes] for lanes in lanes_of],
            [k.kv[seen, lanes] for lanes in lanes_of],
            [k.kv[seen, lanes] for lanes in values_of],
            k.lbias[i],
        )
        for lanes, part in zip(lanes_of, mixed):
            k.a[here, lanes] = part

    loop(blocks, attend_local)
    k.save(k.a, k.o_a)
    got += [weight(k.w_mix2, k.wm2), weight(k.w_up, k.wu), weight(k.w_down, k.wd)]
    if first:
        background.start()
    got_small.wait()

    def mix_norm(at_norm, mixed, weight, residual, plain_ref, rate_ref, full_ref, narrow_ref):
        gain, shift = small_row(k, layer, GAIN + at_norm), small_row(k, layer, SHIFT + at_norm)
        for i in range(0, rows, 128):
            at = slice(i, i + 128)
            update = k.acc[at] if weight is None else dot_nn(mixed[at], weight[...])
            plain, rate, full = norm_rows(residual[at].astype(F32) + update, gain, shift)
            plain_ref[at] = plain.astype(BF16)
            rate_ref[at] = jnp.broadcast_to(rate, (128, 128))
            if full_ref is not None:
                full_ref[at] = full
            if narrow_ref is not None:
                narrow_ref[at] = full.astype(BF16)

    got[1].wait()
    mix_norm(0, k.a, k.wm, xrows if first else k.xf, k.xh, k.rt, k.x1f, k.x1)
    k.save(k.xh, k.o_xh1)
    k.save(k.rt, k.o_r1)
    k.save(k.x1, k.o_x1)

    got[2].wait()
    for i in range(0, 2 * width, 256):
        part = dot_nn(k.x1[...], k.wp[:, width + i : width + i + 256]).astype(BF16)
        k.kv2[:, i : i + 256] = part
        k.kvf[i // 128, 8 : 8 + rows] = part[:, :128].astype(F32)
        k.kvf[i // 128 + 1, 8 : 8 + rows] = part[:, 128:].astype(F32)
    k.save(k.kv2, k.o_kv2)
    for chunk in range(2 * width // 128):
        side, lane = chunk * 128 // width, chunk * 128 % width
        lanes = slice(chunk * 128, chunk * 128 + 128)
        total = jnp.zeros((pool, 128), F32)
        tail = jnp.zeros((1, 128), F32)
        for t in range(5):
            tap = small_row(k, layer, TAPS + 5 * side + t, lane, 128)
            total = total + k.kvf[chunk, pl.ds(6 + t, pool, stride=4)] * tap
            if t < 2:
                tail = tail + k.kvf[chunk, pl.ds(6 + rows + t, 1)] * tap
        k.kp_own[:, lanes] = total.astype(BF16)
        k.aux_own[0:8, lanes] = jnp.broadcast_to(tail, (8, 128))
        k.aux_own[8:16, lanes] = total[:8]
    pooled_out = links.start(k.kp_own, k.kp_got, sibling)
    aux_out = links.start(k.aux_own, k.aux_got, sibling)
    for i in range(0, width, 256):
        k.q2[:, i : i + 256] = dot_nn(k.x1[...], k.wp[:, i : i + 256]).astype(BF16)
    k.save(k.q2, k.o_q2)
    if not first:
        got_bias.wait()
    pooled_out.wait()
    aux_out.wait()
    k.pk[pl.ds(pl.multiple_of(core * pool, pool), pool)] = k.kp_own[...]
    k.pk[pl.ds(pl.multiple_of((1 - core) * pool, pool), pool)] = k.kp_got[...]
    tail = jnp.where(core == 0, k.aux_own[0:1], k.aux_got[0:1])
    head = jnp.where(core == 0, k.aux_got[8:9], k.aux_own[8:9])
    edge = lax.broadcasted_iota(jnp.int32, (16, 1), 0) == 0
    k.pk[pool : pool + 16] = jnp.where(
        edge, jnp.broadcast_to(head + tail, (16, 2 * width)), k.pk[pool : pool + 16].astype(F32)
    ).astype(BF16)
    k.save(k.pk, k.o_pk)

    def attend_pooled(i):
        here = aligned(i, 128)
        mixed = attend_blocks(
            [k.q2[here, lanes] for lanes in lanes_of],
            [k.pk[:, lanes] for lanes in lanes_of],
            [k.pk[:, lanes] for lanes in values_of],
            k.pbias[here],
        )
        for lanes, part in zip(lanes_of, mixed):
            k.b[here, lanes] = part

    loop(blocks, attend_pooled)
    k.save(k.b, k.o_b)
    got[3].wait()
    mix_norm(1, k.b, k.wm2, k.x1f, k.xh2, k.rt2, k.x1f, k.x2)
    k.save(k.xh2, k.o_xh2)
    k.save(k.rt2, k.o_r2)
    k.save(k.x2, k.o_x2)

    got[4].wait()
    got[5].wait()
    part, up = 512, (k.up_a, k.up_b)
    count = ff // part

    def expand(i):
        up[i % 2][...] = dot_nn(k.x2[...], k.wu[:, i * part : (i + 1) * part])

    expand(0)
    for i in range(count):
        if i + 1 < count:
            expand(i + 1)
        lanes = slice(i * part, (i + 1) * part)
        full, slope = gelu_rows(up[i % 2][...])
        k.g[:, lanes] = full.astype(BF16)
        k.gp[:, lanes] = slope.astype(BF16)
        k.save(k.g.at[:, lanes], k.o_g.at[:, lanes])
        k.save(k.gp.at[:, lanes], k.o_gp.at[:, lanes])
        product = dot_nn(full.astype(BF16), k.wd[lanes])
        if i == 0:
            k.acc[...] = product
        else:
            k.acc[...] += product
    result = k.out16 if last else k.xf
    mix_norm(
        2, None, None, k.x1f, k.xh3, k.rt3, None if last else result, result if last else None
    )
    k.save(k.xh3, k.o_xh3)
    k.save(k.rt3, k.o_r3)
    k.save(result, k.o_out)
    if first:
        background.wait()
        k.save(k.grad_got, k.o_grad)
    k.done()


def forward_call(layer, first, last, x_in, small, weights, extra):
    width, ff = weights[0].shape[1], weights[4].shape[2]
    rows = x_in.shape[0] * x_in.shape[1] if first else x_in.shape[0]
    half, pool = LOCAL_WIN // 2, rows // 4
    x_shape = (4, rows // 4, width) if first else (rows, width)
    local, mixer, pooled, mixer2, up, down = ((weight, ANY) for weight in weights)
    args = dict(x_in=(x_in, ANY), small_in=(small, ANY), w_local=local, w_mix=mixer)
    args.update(w_pooled=pooled, w_mix2=mixer2, w_up=up, w_down=down)
    wide, kv = ((rows, width), BF16), ((rows + 2 * half, 2 * width), BF16)
    rate, feed, full = ((rows, 128), F32), ((rows, ff), BF16), ((rows, width), F32)
    outs = dict(o_x=(x_shape, BF16), o_q=wide, o_kv=kv, o_a=wide, o_xh1=wide, o_r1=rate)
    outs.update(o_x1=wide, o_q2=wide, o_kv2=((rows, 2 * width), BF16))
    outs.update(o_pk=((2 * pool, 2 * width), BF16), o_b=wide, o_xh2=wide, o_r2=rate)
    outs.update(o_x2=wide, o_g=feed, o_gp=feed, o_xh3=wide, o_r3=rate)
    outs.update(o_out=wide if last else full)
    s = Scratch()
    wl, wm, wp, wm2, wu, wd = (vmem(weight.shape[1:]) for weight in weights)
    s.add(wl=wl, wm=wm, wp=wp, wm2=wm2, wu=wu, wd=wd)
    wide, full, rate, feed = (vmem(*shape) for shape in (wide, full, rate, feed))
    s.add(small=vmem(small.shape, F32), x=vmem(x_shape))
    s.add(q=wide, a=wide, xh=wide, x1=wide, q2=wide, b=wide, xh2=wide, x2=wide, xh3=wide)
    s.add(xf=full, x1f=full, acc=full, rt=rate, rt2=rate, rt3=rate, g=feed, gp=feed)
    part, pooled = vmem((rows, 512), F32), vmem((pool, 2 * width))
    s.add(up_a=part, up_b=part, kv=vmem(*kv), kv2=vmem((rows, 2 * width)))
    s.add(kvf=vmem((2 * width // 128, rows + 8, 128), F32), pk=vmem((2 * pool, 2 * width)))
    aux = vmem((16, 2 * width), F32)
    s.add(halo=vmem((half, 2 * width)), kp_own=pooled, kp_got=pooled, aux_own=aux, aux_got=aux)
    s.add(lbias=vmem((rows // 128, 128, 128 + 2 * half), F32))
    s.add(pbias=vmem((rows, 2 * pool), F32))
    if last:
        s.add(out16=wide)
    if first:
        counts, places, grad_in = extra
        args.update(counts=(counts, pl.BlockSpec(memory_space=pltpu.SMEM)))
        args.update(places=(places, VMEM), grad_in=(grad_in, ANY))
        outs.update(o_grad=(grad_in.shape, BF16))
        outs.update(o_pbias=((rows, 2 * pool), F32), o_pbias_t=((2 * pool, rows), F32))
        s.add(grad_got=vmem(grad_in.shape), pbias_t=vmem((2 * pool, rows), F32))
    else:
        args.update(pbias_in=(extra, ANY))
    s.sems(16, 40, 12)
    return run_kernel(
        lambda k: forward(k, layer, first, last, rows, width, ff),
        "forward_%d" % layer,
        layer,
        args,
        outs,
        s,
    )


def axis_peers():
    doc, me = lax.axis_index("doc"), lax.axis_index("seq")
    core, z = me % 2, me // 2
    along = (z + 1 - 2 * (z % 2), z + 2 - 4 * (z // 2), 3 - z)
    return (
        (doc, me + 1 - 2 * core),
        (doc + 1 - 2 * (doc % 2), me),
        (doc + 2 - 4 * (doc // 2), me),
        [(doc, 2 * other + core) for other in along],
        along,
    )


BOTH = (0, 1)


class CoreSum:
    def __init__(self, k, tag):
        self.links = k.links
        self.send, self.own, self.got = (getattr(k, tag + part) for part in ("send", "mine", "got"))
        self.copy = {}

    def start(self, part):
        self.copy[part] = self.links.start(
            self.send.at[part], self.got.at[part], axis_peers()[0]
        )

    def finish(self, *parts):
        for part in parts or BOTH:
            self.copy[part].wait()

            def add(z):
                self.own[part, z] += self.got[part, z]

            loop(4, add)


class PlaneSum:
    def __init__(self, k, tag, source):
        self.links, self.copies, self.source = k.links, k.loads, source
        self.kept, self.got1, self.got2, self.total = (
            getattr(k, tag + part) for part in ("kept", "got1", "got2", "total")
        )
        doc = lax.axis_index("doc")
        self.x, self.y = doc % 2, doc // 2
        self.copy = {}

    def start(self, *parts):
        _, across, up, _, _ = axis_peers()
        x, y = self.x, self.y
        for part in parts or BOTH:
            source, got = self.source.at[part], self.got1.at[part]
            self.copy[part] = [
                self.links.start(source.at[:, 0, :, 1 - x], got.at[0], across),
                self.links.start(source.at[:, 1, 1 - y], got.at[1], up),
                self.copies.start(source.at[:, 0, :, x], self.kept.at[part, 0]),
                self.copies.start(source.at[:, 1, y], self.kept.at[part, 1]),
            ]

    def middle(self, *parts):
        _, across, up, _, _ = axis_peers()
        for part in parts or BOTH:
            for copy in self.copy[part]:
                copy.wait()

            def add(half):
                self.kept[part, half] += self.got1[part, half]

            loop(2, add)
            kept, got = self.kept.at[part], self.got2.at[part]
            self.copy[part] = [
                self.links.start(kept.at[0, :, 1 - self.y], got.at[0], up),
                self.links.start(kept.at[1, :, 1 - self.x], got.at[1], across),
            ]

    def finish(self, *parts):
        for part in parts or BOTH:
            for copy in self.copy[part]:
                copy.wait()
            for z in range(4):
                self.total[part, z, 0] = self.kept[part, 0, z, self.y] + self.got2[part, 0, z]
                self.total[part, z, 1] = self.kept[part, 1, z, self.x] + self.got2[part, 1, z]


class LineSum:
    def __init__(self, k, tag, source):
        self.links, self.copies, self.source = k.links, k.loads, source
        self.whole = getattr(k, tag + "whole")
        if hasattr(k, tag + "own"):
            self.own, self.got = getattr(k, tag + "own"), getattr(k, tag + "got")
        doc = lax.axis_index("doc")
        self.x, self.y = doc % 2, doc // 2
        self.copy = {}

    def start(self, *parts):
        _, _, _, line, along = axis_peers()
        for part in parts or BOTH:
            source = self.source.at[part]
            self.copy[part] = [
                self.links.start(source.at[other], self.got.at[part, i], device)
                for i, (other, device) in enumerate(zip(along, line))
            ]
            self.copy[part].append(
                self.copies.start(source.at[lax.axis_index("seq") // 2], self.own.at[part])
            )

    def settle(self, *parts):
        for part in parts or BOTH:
            for copy in self.copy[part]:
                copy.wait()
            for half in range(2):
                total = self.own[part, half].astype(F32)
                for i in range(3):
                    total = total + self.got[part, i, half].astype(F32)
                self.whole[part, half, self.y, self.x] = total.astype(BF16)

    def take(self):
        return [
            self.copies.start(self.source.at[part, half], self.whole.at[part, half, self.y, self.x])
            for part in range(2)
            for half in range(2)
        ]

    def give(self, k, target):
        for part in range(2):
            for half in range(2):
                k.save(self.whole.at[part, half, self.y, self.x], target.at[part, half])

    def gather(self, *parts):
        _, across, up, _, _ = axis_peers()
        for part in parts or BOTH:
            first = self.whole.at[part, 0, self.y, self.x]
            second = self.whole.at[part, 1, self.y, self.x]
            self.copy[part] = [
                self.links.start(first, first, across),
                self.links.start(second, second, up),
            ]

    def middle(self, *parts):
        for part in parts or BOTH:
            self.settle(part)
            self.gather(part)

    def spread(self, *parts):
        _, across, up, _, _ = axis_peers()
        for part in parts or BOTH:
            for copy in self.copy[part]:
                copy.wait()
            first = self.whole.at[part, 0, self.y]
            second = self.whole.at[part, 1, :, self.x]
            self.copy[part] = [
                self.links.start(first, first, up),
                self.links.start(second, second, across),
            ]

    def finish(self, *parts):
        for part in parts or BOTH:
            for copy in self.copy[part]:
                copy.wait()


def norm_back(k, rows, incoming, plain_ref, rate_ref, gain, full, narrow, sums, at_sum):
    for i in range(0, rows, 128):
        at = slice(i, i + 128)
        grad = incoming(at)
        plain = plain_ref[at].astype(F32)
        rate = rate_ref[at][:, :1]
        scaled = grad * gain
        even = jnp.mean(scaled, -1, keepdims=True)
        tilt = jnp.mean(scaled * plain, -1, keepdims=True)
        result = rate * (scaled - even - plain * tilt)
        full[at] = result
        narrow[at] = result.astype(BF16)
        for j, part in enumerate((grad * plain, grad)):
            part = jnp.sum(part.reshape(16, 8, -1), 0)
            if i == 0:
                sums[at_sum + j] = part
            else:
                sums[at_sum + j] += part


def attend_back_blocks(queries, key_rows, value_rows, grads_mixed, bias):
    low, high = split_masks(2 * HD)
    wide_bias = jnp.concatenate([bias, bias], 1)
    first = []
    for query, key, value, grad in zip(queries, key_rows, value_rows, grads_mixed):
        stacked, grads = by_head(query, low, high, HD**-0.5), by_head(grad, low, high, 1.0)
        first.append((stacked, grads, dot_nt(key, stacked) + wide_bias, dot_nt(value, grads)))
    second = []
    for _, _, scores, grad_soft in first:
        raised = jnp.exp(scores - jnp.max(scores, 0, keepdims=True))
        soft = raised * (1.0 / jnp.sum(raised, 0, keepdims=True))
        inner = jnp.sum(soft * grad_soft, 0, keepdims=True)
        second.append((soft.astype(BF16), (soft * (grad_soft - inner)).astype(BF16)))
    result = []
    for (stacked, grads, _, _), (soft, grad_scores), key in zip(first, second, key_rows):
        grad_queries = from_heads(dot_tn(grad_scores, key), low, high) * HD**-0.5
        result.append(
            (grad_queries.astype(BF16), dot_nn(grad_scores, stacked), dot_nn(soft, grads))
        )
    return result


def local_bias_turned(at, blocks, length_first, length_last, rows, half):
    shape = (rows + 2 * half, rows)
    key = lax.broadcasted_iota(jnp.int32, shape, 0)
    query = lax.broadcasted_iota(jnp.int32, shape, 1)
    first = jnp.where(length_first & (at == 0), half, 0)
    last = jnp.where(length_last & (at == blocks - 1), rows + half, rows + 2 * half)
    seen = (key >= query) & (key <= query + 2 * half) & (key >= first) & (key < last)
    return jnp.where(seen, 0.0, MASKED).astype(F32)


def place_piece(target, part, z, top, bottom):
    block = target.shape[5:]
    target[part, z, 0] = top[: 4 * block[0]].reshape((2, 2) + block).astype(BF16)
    target[part, z, 1, 0] = top[4 * block[0] :].reshape((2,) + block).astype(BF16)
    target[part, z, 1, 1] = bottom.reshape((2,) + block).astype(BF16)


def whole_piece(target, part, z, value):
    target[part, z] = value.reshape(target.shape[2:]).astype(BF16)


def feed_back(k, layer, rows, width, ff, last):
    core = lax.axis_index("seq") % 2
    sibling, across, up, line_peers, _ = axis_peers()
    shard = ff // 8
    got = k.load_all("dy xh3 r3".split())
    got_small = k.load(k.small_in, k.small)
    if not last:
        greet([sibling, across, up] + line_peers)
        before, line = PlaneSum(k, "x_", k.x_in), LineSum(k, "z_", k.z_in)
        before.start()
        line.start()
    got.update(k.load_all(["g"]))
    for name in ("dy", "xh3", "r3"):
        got[name].wait()
    got_small.wait()
    incoming = k.v_dy.reshape(rows, width) if last else k.v_dy
    norm_back(
        k,
        rows,
        lambda at: incoming[at].astype(F32),
        k.v_xh3,
        k.v_r3,
        small_row(k, layer, GAIN + 2),
        k.res,
        k.dn,
        k.sums,
        0,
    )
    got.update(k.load_all(["gp"]))
    got_down = k.load(k.w_down.at[layer], k.v_down)
    turn(k.dn, k.dn_t)
    got["g"].wait()
    reduced, expanded = CoreSum(k, "r_"), CoreSum(k, "e_")
    middle = width // 2

    def reduce_part(part, which, target):
        rows_of = slice(part * middle, (part + 1) * middle)
        for z in range(4):
            lanes = aligned(2 * z + which, shard)
            whole_piece(target, part, z, dot_nn(k.dn_t[rows_of], k.v_g[:, lanes]))

    def slope_part(first):
        for i in range(first, first + ff // 2, 512):
            k.du[:, i : i + 512] = (
                dot_nt(k.dn[...], k.v_down[i : i + 512]) * k.v_gp[:, i : i + 512].astype(F32)
            ).astype(BF16)

    reduce_part(0, 1 - core, k.r_send)
    if last:
        greet_regroup([sibling, across, up] + line_peers)
    reduced.start(0)
    reduce_part(1, 1 - core, k.r_send)
    reduced.start(1)
    got.update(k.load_all("x2 xh2 r2".split()))
    got_up = k.load(k.w_up.at[layer], k.v_up)
    reduce_part(0, core, k.r_mine)
    reduce_part(1, core, k.r_mine)
    if last:
        outward = Regroup(k.loads, k.links, k.x3, k.regrouped, False)
        outward.start()
    got["gp"].wait()
    got_down.wait()
    plane = PlaneSum(k, "r_", k.r_mine)
    if last:
        reduced.finish(0)
        plane.start(0)
    else:
        before.middle(0)
    slope_part(0)
    reduced.finish(*((1,) if last else BOTH))
    if not last:
        line.middle()
        before.middle(1)
    plane.start(*((1,) if last else BOTH))
    slope_part(ff // 2)
    got["x2"].wait()
    turn(k.v_x2, k.x2_t)

    def expand_part(part, which, target):
        rows_of = slice(part * middle, (part + 1) * middle)
        for z in range(4):
            lanes = aligned(2 * z + which, shard)
            whole_piece(target, part, z, dot_nn(k.x2_t[rows_of], k.du[:, lanes]))

    for part in BOTH:
        expand_part(part, 1 - core, k.e_send)
        expanded.start(part)
    for part in BOTH:
        expand_part(part, core, k.e_mine)
    if not last:
        line.spread()
        before.finish()
        late = LineSum(k, "y_", k.x_total)
        late.start()
    else:
        plane.middle(0)
    got_up.wait()
    for i in range(0, width, 256):
        k.res[:, i : i + 256] += dot_nt(k.du[...], k.v_up[i : i + 256])
    got["xh2"].wait()
    got["r2"].wait()
    norm_back(
        k,
        rows,
        lambda at: k.res[at],
        k.v_xh2,
        k.v_r2,
        small_row(k, layer, GAIN + 1),
        k.res,
        k.dn2,
        k.sums,
        2,
    )
    k.save(k.res, k.o_mid)
    k.save(k.dn2, k.o_dy2)
    save_sums(k, 4)
    expanded.finish()
    k.save(k.e_mine, k.o_e)
    plane.middle(*((1,) if last else BOTH))
    if last:
        outward.wait()
        k.save(k.regrouped, k.o_out)
    else:
        line.finish()
        k.save(k.z_whole, k.o_z)
        late.settle()
        late.give(k, k.o_y)
    plane.finish()
    k.save(k.r_total, k.o_r)
    k.done()


def pooled_back(k, layer, rows, width):
    core = lax.axis_index("seq") % 2
    sibling, across, up, line_peers, _ = axis_peers()
    pool = rows // 4
    pairs, blocks = width // (2 * HD), rows // 128
    shard = width // 8
    got = k.load_all(["dy2"])
    got_mix = k.load(k.w_mix2.at[layer], k.v_mix2)
    got_small = k.load(k.small_in, k.small)
    late = LineSum(k, "y_", k.y_in) if hasattr(k, "y_in") else None
    if late:
        got_late = late.take()
    greet([sibling, across, up] + line_peers)
    plane, line = PlaneSum(k, "x_", k.x_in), LineSum(k, "z_", k.z_in)
    if late:
        for copy in got_late:
            copy.wait()
        late.gather()
    plane.start()
    line.start()
    got.update(k.load_all("q2 pk".split()))
    got_bias = k.load(k.pbias, k.v_pbias)
    got["dy2"].wait()
    got_mix.wait()
    got.update(k.load_all("kv2 b".split()))
    for i in range(0, width, 256):
        k.do[:, i : i + 256] = dot_nt(k.v_dy2[...], k.v_mix2[i : i + 256]).astype(BF16)
    for name in ("q2", "pk"):
        got[name].wait()
    k.dkv[...] = jnp.zeros_like(k.dkv)
    got_bias.wait()
    got.update(k.load_all("x1 mid xh1 r1".split()))
    got_proj = k.load(k.w_pooled.at[layer], k.v_pooled)
    lanes_of = [slice(2 * HD * pair, 2 * HD * (pair + 1)) for pair in range(pairs)]
    values_of = [slice(width + part.start, width + part.stop) for part in lanes_of]

    def attend_part(i):
        here = aligned(i, 128)
        parts = attend_back_blocks(
            [k.v_q2[here, lanes] for lanes in lanes_of],
            [k.v_pk[:, lanes] for lanes in lanes_of],
            [k.v_pk[:, lanes] for lanes in values_of],
            [k.do[here, lanes] for lanes in lanes_of],
            k.v_pbias[:, here],
        )
        for lanes, values, (grad_q, grad_k, grad_v) in zip(lanes_of, values_of, parts):
            k.dqkv[here, lanes] = grad_q
            k.dkv[:, lanes] += grad_k
            k.dkv[:, values] += grad_v

    loop(blocks, attend_part)
    k.rim_out[...] = k.dkv[pl.ds(pl.multiple_of((pool - 16) * (1 - core), 16), pool + 16)].astype(
        BF16
    )
    rim = k.links.start(k.rim_out, k.rim_got, sibling)
    got["b"].wait()
    turn(k.v_b, k.b_t)
    got["kv2"].wait()
    for c in range(2 * width // 128):
        k.kvf[c] = k.v_kv2[:, pl.ds(c * 128, 128)].astype(F32)
    got_small.wait()
    rim.wait()
    k.total[pl.ds(0, pool)] = (
        k.dkv[pl.ds(pl.multiple_of(core * pool, pool), pool)]
        + k.rim_got[pl.ds(pl.multiple_of(core * 16, 16), pool)].astype(F32)
    )
    k.total[pl.ds(pool, 8)] = jnp.where(
        core == 0, k.dkv[pl.ds(pool, 8)] + k.rim_got[pl.ds(pool, 16)].astype(F32)[:8], 0.0
    )

    for c in range(2 * width // 128):
        side, lane = c * 128 // width, c * 128 % width
        lanes = pl.ds(c * 128, 128)
        own, after = k.total[pl.ds(0, pool), lanes], k.total[pl.ds(1, pool), lanes]
        rows_at = [pl.ds(j, pool, stride=4) for j in range(4)]
        kept = [k.kvf[c, at] for at in rows_at]
        taps = [small_row(k, layer, TAPS + 5 * side + t, lane, 128) for t in range(5)]
        pairs_of = ((kept[2], after), (kept[3], after), (kept[0], own), (kept[1], own), (kept[2], own))
        for t, (token, grad) in enumerate(pairs_of):
            k.tap_sums[side, 8 * t : 8 * t + 8, lane : lane + 128] = jnp.sum(
                (token * grad).reshape(pool // 8, 8, 128), 0
            )
        k.kvf[c, rows_at[0]] = own * taps[2]
        k.kvf[c, rows_at[1]] = own * taps[3]
        k.kvf[c, rows_at[2]] = own * taps[4] + after * taps[0]
        k.kvf[c, rows_at[3]] = after * taps[1]
        k.dqkv[:, pl.ds(width + c * 128, 128)] = k.kvf[c].astype(BF16)
    turn(k.dqkv, k.dqkv_t)
    got["x1"].wait()
    if late:
        late.spread()
    line.middle()
    plane.middle()
    summed = CoreSum(k, "p_")
    middle = width // 2

    def grad_part(part, which, target):
        lanes = slice(part * middle, (part + 1) * middle)
        mixers = jnp.concatenate(
            [k.b_t[aligned(2 * z + which, shard)] for z in range(4)], 0
        )
        k.mixed[...] = dot_nn(mixers, k.v_dy2[:, lanes])

        for z in range(4):
            at = 2 * z + which
            mine = jnp.concatenate(
                [
                    k.dqkv_t[aligned(at, shard)],
                    k.dqkv_t[pl.ds(pl.multiple_of(width + at * 2 * shard, 2 * shard), 2 * shard)],
                ],
                0,
            )
            place_piece(
                target, part, z, dot_nn(mine, k.v_x1[:, lanes]), k.mixed[z * shard : (z + 1) * shard]
            )

    for part in BOTH:
        grad_part(part, 1 - core, k.p_send)
        summed.start(part)
    for part in BOTH:
        grad_part(part, core, k.p_mine)
    got["mid"].wait()
    got_proj.wait()

    for i in range(0, width, 256):
        k.v_mid[:, i : i + 256] += dot_nt(k.dqkv[...], k.v_pooled[i : i + 256])
    got["xh1"].wait()
    got["r1"].wait()
    norm_back(
        k,
        rows,
        lambda at: k.v_mid[at],
        k.v_xh1,
        k.v_r1,
        small_row(k, layer, GAIN),
        k.v_mid,
        k.dn,
        k.sums,
        0,
    )
    k.save(k.v_mid, k.o_low)
    k.save(k.dn, k.o_dy1)
    save_sums(k, 2, k.tap_sums)
    line.spread()
    plane.finish()
    k.save(k.x_total, k.o_x)
    summed.finish()
    k.save(k.p_mine, k.o_p)
    if late:
        late.finish()
        k.save(k.y_whole, k.o_y)
    line.finish()
    k.save(k.z_whole, k.o_z)
    k.done()


def local_back(k, layer, rows, width, final):
    core = lax.axis_index("seq") % 2
    sibling, across, up, line_peers, _ = axis_peers()
    half = LOCAL_WIN // 2
    pairs, blocks = width // (2 * HD), rows // 128
    shard = width // 8
    got = k.load_all(["dy1"])
    got_mix = k.load(k.w_mix.at[layer], k.v_mix)
    if final:
        greet_regroup([sibling, across, up] + line_peers)
    else:
        greet([sibling, across, up] + line_peers)
    plane, line = PlaneSum(k, "x_", k.x_in), LineSum(k, "z_", k.z_in)
    plane.start()
    line.start()
    got.update(k.load_all("q kv".split()))
    if final:
        small = SmallSum(k)
        small.load()
    for i in range(blocks):
        k.lbias[i] = local_bias_turned(i, blocks, core == 0, core == 1, 128, half)
    got["dy1"].wait()
    got_mix.wait()
    for i in range(0, width, 256):
        k.do[:, i : i + 256] = dot_nt(k.v_dy1[...], k.v_mix[i : i + 256]).astype(BF16)
    got.update(k.load_all("a x low".split()))
    got_proj = k.load(k.w_local.at[layer], k.v_local)
    for name in ("q", "kv"):
        got[name].wait()
    if final:
        small.step()
    k.dkv[...] = jnp.zeros_like(k.dkv)
    lanes_of = [slice(2 * HD * pair, 2 * HD * (pair + 1)) for pair in range(pairs)]
    values_of = [slice(width + part.start, width + part.stop) for part in lanes_of]

    def attend_part(i):
        here, seen = aligned(i, 128), pl.ds(pl.multiple_of(i * 128, 128), 128 + 2 * half)
        parts = attend_back_blocks(
            [k.v_q[here, lanes] for lanes in lanes_of],
            [k.v_kv[seen, lanes] for lanes in lanes_of],
            [k.v_kv[seen, lanes] for lanes in values_of],
            [k.do[here, lanes] for lanes in lanes_of],
            k.lbias[i],
        )
        for lanes, values, (grad_q, grad_k, grad_v) in zip(lanes_of, values_of, parts):
            k.dqkv[here, lanes] = grad_q
            k.dkv[seen, lanes] += grad_k
            k.dkv[seen, values] += grad_v

    loop(blocks, attend_part)
    k.rim_out[...] = k.dkv[pl.ds(pl.multiple_of((rows + half) * (1 - core), half), half)].astype(
        BF16
    )
    rim = k.links.start(k.rim_out, k.rim_got, sibling)
    got["a"].wait()
    turn(k.v_a, k.a_t)
    rim.wait()
    edge = pl.ds(pl.multiple_of(half + (rows - half) * (1 - core), half), half)
    k.dkv[edge] += k.rim_got[...].astype(F32)
    k.dqkv[:, width:] = k.dkv[half : half + rows].astype(BF16)
    turn(k.dqkv, k.dqkv_t)
    got["x"].wait()
    inputs = k.v_x.reshape(rows, width) if len(k.v_x.shape) == 3 else k.v_x
    summed = CoreSum(k, "l_")
    middle = width // 2

    def grad_part(part, which, target):
        lanes = slice(part * middle, (part + 1) * middle)
        mixers = jnp.concatenate(
            [k.a_t[aligned(2 * z + which, shard)] for z in range(4)], 0
        )
        k.mixed[...] = dot_nn(mixers, k.v_dy1[:, lanes])
        for z in range(4):
            mine = k.dqkv_t[aligned(2 * z + which, 3 * shard)]
            place_piece(
                target, part, z, dot_nn(mine, inputs[:, lanes]), k.mixed[z * shard : (z + 1) * shard]
            )

    def residual():
        got["low"].wait()
        got_proj.wait()
        for i in range(0, width, 256):
            k.v_low[:, i : i + 256] += dot_nt(k.dqkv[...], k.v_local[i : i + 256])

    if not final:
        for part in BOTH:
            grad_part(part, 1 - core, k.l_send)
            summed.start(part)
        line.middle()
        plane.middle()
        for part in BOTH:
            grad_part(part, core, k.l_mine)
        residual()
        k.save(k.v_low, k.o_dx)
        line.spread()
        plane.finish()
        k.save(k.x_total, k.o_x)
        summed.finish()
        k.save(k.l_mine, k.o_l)
        line.finish()
        k.save(k.z_whole, k.o_z)
        k.done()
        return
    small.step()
    residual()
    for i in range(0, rows, 128):
        k.narrow[i // 128] = k.v_low[i : i + 128].astype(BF16)
    outward = Regroup(k.loads, k.links, k.narrow, k.regrouped, False)
    outward.start()
    line.middle()
    plane.middle()
    for part in BOTH:
        grad_part(part, 1 - core, k.l_send)
        summed.start(part)
    small.step()
    last_plane, last_line = PlaneSum(k, "l_", k.l_mine), LineSum(k, "f_", k.l_total)
    for part in BOTH:
        grad_part(part, core, k.l_mine)
    for part in BOTH:
        summed.finish(part)
        last_plane.start(part)
    plane.finish()
    before = LineSum(k, "p_", k.x_total)
    before.start()
    small.step()
    line.spread()
    last_plane.middle(0)
    last_plane.middle(1)
    line.finish()
    k.save(k.z_whole, k.o_z)
    before.middle()
    for part in BOTH:
        last_plane.finish(part)
        last_line.start(part)
    small.finish()
    before.spread()
    outward.wait()
    k.save(k.regrouped, k.o_dx)
    last_line.middle(0)
    before.finish()
    k.save(k.p_whole, k.o_p)
    last_line.middle(1)
    last_line.spread(0)
    last_line.spread(1)
    last_line.finish()
    k.save(k.f_whole, k.o_f)
    k.done()


class SmallSum:
    def __init__(self, k):
        self.k = k
        sibling, across, up, line, _ = axis_peers()
        self.order = [[sibling], [across], [up], line]
        self.at, self.slot = 0, 0

    def load(self):
        k = self.k
        self.copies = []
        for i in range(k.s_sum.shape[0]):
            for source, first, last in ((k.s_feed[i], 0, 8), (k.s_pool[i], 8, 24)):
                self.copies.append(k.load(source, k.s_sum.at[i, first:last]))

    def step(self):
        k = self.k
        for copy in self.copies:
            copy.wait()
        if self.at > 0:
            for _ in self.copies:
                k.s_sum[...] += k.s_got[self.slot]
                self.slot += 1
        if self.at < len(self.order):
            self.copies = [
                k.links.start(k.s_sum, k.s_got.at[self.slot + i], device)
                for i, device in enumerate(self.order[self.at])
            ]
        self.at += 1

    def finish(self):
        self.step()
        self.k.save(self.k.s_sum, self.k.o_small)


def save_sums(k, count, taps=None):
    for i in range(count):
        k.row_sums[i : i + 1] = jnp.sum(k.sums[i], 0, keepdims=True)
    at = count
    if taps is not None:
        for side in range(2):
            for t in range(5):
                k.row_sums[at : at + 1] = jnp.sum(
                    taps[side, 8 * t : 8 * t + 8], 0, keepdims=True
                )
                at += 1
    k.row_sums[at:] = jnp.zeros((k.row_sums.shape[0] - at, k.row_sums.shape[1]), F32)
    k.save(k.row_sums, k.o_sums)


def block_of(width):
    return (width // 16, width // 2)


def group_shape(block):
    return (2, 4, 2, 2, 2) + block


def total_shape(block):
    return (2, 4, 2) + block


def whole_shape(block):
    return (2, 2, 2, 2) + block


def feed_back_call(layer, last, dy, small, kept, w_down, w_up, x_in, z_in, outputs):
    rows, width = kept.o_xh3.shape
    ff = kept.o_g.shape[1]
    block = block_of(width)
    full, wide = (rows, width), vmem((rows, width))
    s = Scratch()
    args = dict(small_in=(small, ANY), w_down=(w_down, ANY), w_up=(w_up, ANY))
    s.bring(args, dy=dy, xh3=kept.o_xh3, r3=kept.o_r3, g=kept.o_g, gp=kept.o_gp)
    s.bring(args, x2=kept.o_x2, xh2=kept.o_xh2, r2=kept.o_r2)
    outs = dict(o_mid=(full, F32), o_dy2=(full, BF16), o_sums=((8, width), F32))
    outs.update(o_r=(total_shape(block), BF16), o_e=(group_shape(block), BF16))
    s.add(small=vmem(small.shape, F32), sums=vmem((4, 8, width), F32))
    s.add(v_down=vmem(w_down.shape[1:]), v_up=vmem(w_up.shape[1:]))
    s.add(row_sums=vmem((8, width), F32), res=vmem(full, F32), dn=wide, dn2=wide)
    s.add(dn_t=vmem((width, rows)), x2_t=vmem((width, rows)), du=vmem((rows, ff)))
    s.core("r_", block)
    s.core("e_", block)
    s.plane("r_", block)
    if last:
        by_doc = (4, rows // 4, width)
        args.update(x3=(outputs.reshape(by_doc), ANY))
        outs.update(o_out=(by_doc, BF16))
        s.add(regrouped=vmem(by_doc))
    else:
        args.update(x_in=(x_in, ANY), z_in=(z_in, ANY))
        outs.update(o_y=((2, 2) + block, BF16), o_z=(whole_shape(block), BF16))
        s.plane("x_", block)
        s.line("y_", block)
        s.line("z_", block)
    s.sems(40, 16, 48)
    return run_kernel(
        lambda k: feed_back(k, layer, rows, width, ff, last),
        "feed_back_%d" % layer,
        2 + layer,
        args,
        outs,
        s,
    )


def pooled_back_call(layer, mid, dy2, small, pbias, kept, w_mix2, w_pooled, x_in, z_in, y_in):
    rows, width = mid.shape
    pool = rows // 4
    block = block_of(width)
    full, wide = (rows, width), vmem((rows, width))
    s = Scratch()
    args = dict(small_in=(small, ANY), w_mix2=(w_mix2, ANY), w_pooled=(w_pooled, ANY))
    args.update(x_in=(x_in, ANY), z_in=(z_in, ANY))
    s.bring(args, mid=mid, dy2=dy2, b=kept.o_b, q2=kept.o_q2, kv2=kept.o_kv2, pk=kept.o_pk)
    s.bring(args, x1=kept.o_x1, xh1=kept.o_xh1, r1=kept.o_r1, pbias=pbias)
    outs = dict(o_low=(full, F32), o_dy1=(full, BF16), o_sums=((16, width), F32))
    outs.update(o_p=(group_shape(block), BF16), o_x=(total_shape(block), BF16))
    outs.update(o_z=(whole_shape(block), BF16))
    s.add(small=vmem(small.shape, F32), v_mix2=vmem(w_mix2.shape[1:]))
    s.add(v_pooled=vmem(w_pooled.shape[1:]), sums=vmem((2, 8, width), F32))
    s.add(row_sums=vmem((16, width), F32), tap_sums=vmem((2, 40, width), F32), do=wide, dn=wide)
    rim, turned = vmem((pool + 16, 2 * width)), vmem((width, rows))
    s.add(dkv=vmem((2 * pool, 2 * width), F32), rim_out=rim, rim_got=rim)
    s.add(total=vmem((pool + 8, 2 * width), F32), kvf=vmem((2 * width // 128, rows, 128), F32))
    s.add(dqkv=vmem((rows, 3 * width)), dqkv_t=vmem((3 * width, rows)), b_t=turned)
    s.add(mixed=vmem((width // 2, width // 2), F32))
    s.core("p_", block)
    s.plane("x_", block)
    s.line("z_", block)
    if y_in is not None:
        args.update(y_in=(y_in, ANY))
        outs.update(o_y=(whole_shape(block), BF16))
        s.add(y_whole=vmem(whole_shape(block)))
    s.sems(40, 16, 48)
    return run_kernel(
        lambda k: pooled_back(k, layer, rows, width),
        "pooled_back_%d" % layer,
        4 + layer,
        args,
        outs,
        s,
    )


def local_back_call(layer, final, low, dy1, kept, w_mix, w_local, x_in, z_in, sums):
    rows, width = low.shape
    half = LOCAL_WIN // 2
    block = block_of(width)
    s = Scratch()
    args = dict(w_mix=(w_mix, ANY), w_local=(w_local, ANY), x_in=(x_in, ANY), z_in=(z_in, ANY))
    s.bring(args, low=low, dy1=dy1, a=kept.o_a, q=kept.o_q, kv=kept.o_kv, x=kept.o_x)
    outs = dict(o_z=(whole_shape(block), BF16))
    by_doc, total = (4, rows // 4, width), (len(sums), 24, width)
    if final:
        whole = (whole_shape(block), BF16)
        for i, (feed, pooled) in enumerate(sums):
            args["s_feed%d" % i], args["s_pool%d" % i] = (feed, ANY), (pooled, ANY)
        outs.update(o_dx=(by_doc, BF16), o_p=whole, o_f=whole, o_small=(total, F32))
    else:
        outs.update(o_dx=((rows, width), F32), o_l=(group_shape(block), BF16))
        outs.update(o_x=(total_shape(block), BF16))
    s.add(v_mix=vmem(w_mix.shape[1:]), v_local=vmem(w_local.shape[1:]))
    s.add(lbias=vmem((rows // 128, 128 + 2 * half, 128), F32), do=vmem((rows, width)))
    s.add(dkv=vmem((rows + 2 * half, 2 * width), F32))
    s.add(rim_out=vmem((half, 2 * width)), rim_got=vmem((half, 2 * width)))
    s.add(dqkv=vmem((rows, 3 * width)), dqkv_t=vmem((3 * width, rows)))
    s.add(a_t=vmem((width, rows)), mixed=vmem((width // 2, width // 2), F32))
    s.core("l_", block)
    s.plane("x_", block)
    s.line("z_", block)
    if final:
        s.add(narrow=vmem(by_doc), regrouped=vmem(by_doc))
        s.add(s_sum=vmem(total, F32), s_got=vmem((6,) + total, F32))
        s.plane("l_", block)
        s.line("p_", block)
        s.line("f_", block)
    s.sems(48, 16, 72)

    def body(k):
        if final:
            k.s_feed = [getattr(k, "s_feed%d" % i) for i in range(len(sums))]
            k.s_pool = [getattr(k, "s_pool%d" % i) for i in range(len(sums))]
        local_back(k, layer, rows, width, final)

    return run_kernel(
        body,
        "local_back_%d" % layer,
        6 + layer,
        args,
        outs,
        s,
    )


def by_chip(
    inputs,
    question_count,
    question_at,
    local_proj,
    local_mixer,
    pooled_proj,
    pool_taps,
    pooled_mixer,
    expand_weight,
    reduce_weight,
    norm_gain,
    norm_shift,
    output_grad,
):
    docs_here, tok_here, width = inputs.shape
    layers, ff = local_proj.shape[0], expand_weight.shape[2]
    small = jnp.concatenate([norm_gain, norm_shift, pool_taps.reshape(layers, 10, width)], 1)
    weights = (local_proj, local_mixer, pooled_proj, pooled_mixer, expand_weight, reduce_weight)
    hidden, kept, bias = inputs, [], None
    for layer in range(layers):
        first, last = layer == 0, layer == layers - 1
        extra = (question_count, question_at, output_grad) if first else bias
        made = forward_call(layer, first, last, hidden, small, weights, extra)
        if first:
            grad, bias, bias_t = made.o_grad, made.o_pbias, made.o_pbias_t
        kept.append(made)
        hidden = made.o_out
    x_in = z_in = None
    reduced, expanded, pooled_sums, local_sums, sums = {}, {}, {}, {}, []
    for layer in reversed(range(layers)):
        last = layer == layers - 1
        saved = kept[layer]
        fed = feed_back_call(
            layer, last, grad, small, saved, reduce_weight, expand_weight, x_in, z_in, hidden
        )
        if last:
            outputs = fed.o_out
        else:
            pooled_sums[layer + 1] = fed.o_z
        pooled = pooled_back_call(
            layer,
            fed.o_mid,
            fed.o_dy2,
            small,
            bias_t,
            saved,
            pooled_mixer,
            pooled_proj,
            fed.o_e,
            fed.o_r,
            None if last else fed.o_y,
        )
        reduced[layer] = pooled.o_z
        if not last:
            local_sums[layer + 1] = pooled.o_y
        sums.insert(0, (fed.o_sums, pooled.o_sums))
        local = local_back_call(
            layer,
            layer == 0,
            pooled.o_low,
            pooled.o_dy1,
            saved,
            local_mixer,
            local_proj,
            pooled.o_p,
            pooled.o_x,
            sums,
        )
        expanded[layer] = local.o_z
        if layer > 0:
            grad, x_in, z_in = local.o_dx, local.o_l, local.o_x
    pooled_sums[0], local_sums[0] = local.o_p, local.o_f
    groups = [[group[i] for i in range(layers)] for group in (reduced, expanded, local_sums, pooled_sums)]
    return finish_call(outputs, local.o_dx, local.o_small, groups, layers, width, ff)


def finish(k, layers, width, ff):
    part, feed = width // 8, ff // 8
    me = lax.axis_index("seq")
    order = list(reversed(range(layers)))
    names = ["g%d" % i for i in range(4 * layers)]
    got = [k.load(getattr(k, name), getattr(k, "v_" + name)) for name in names]
    got_dx, got_small = k.load(k.dx, k.v_dx), k.load(k.small_sum, k.v_small_sum)
    got_out = k.load(k.outputs, k.v_outputs)

    def whole(group, layer, axis):
        got[group * layers + layer].wait()
        block = getattr(k, "v_" + names[group * layers + layer])
        parts = [block[i].reshape(-1, block.shape[-1]).astype(F32) for i in BOTH]
        return jnp.concatenate(parts, axis)

    def put(layer, source, target, value):
        source[layer] = value
        k.save(source.at[layer], target.at[layer])

    for layer in order:
        put(layer, k.v_down, k.o_down, whole(0, layer, 0).T)
        put(layer, k.v_up, k.o_up, whole(1, layer, 0))
    got_out.wait()
    k.save(k.v_outputs, k.o_outputs)
    got_dx.wait()
    for i in range(4):
        k.v_dx32[i] = k.v_dx[i].astype(F32)
    k.save(k.v_dx32, k.o_dx)
    for layer in order:
        local = whole(2, layer, 1)
        put(layer, k.v_local, k.o_local, local[: 3 * part])
        put(layer, k.v_mix, k.o_mix, local[3 * part :])
        pooled = whole(3, layer, 1)
        put(layer, k.v_query, k.o_query, pooled[:part])
        put(layer, k.v_kv, k.o_kv, pooled[part : 3 * part])
        put(layer, k.v_mix2, k.o_mix2, pooled[3 * part :])
    got_small.wait()
    small = k.v_small_sum[...]
    mine = jnp.zeros(small.shape[:2] + (part,), F32)
    for i in range(8):
        mine = jnp.where(me == i, small[:, :, i * part : (i + 1) * part], mine)
    for layer in range(layers):
        rows = mine[layer]
        for i, (gain, shift) in enumerate(((8, 9), (2, 3), (0, 1))):
            k.v_gain[i, layer : layer + 1] = rows[gain : gain + 1]
            k.v_shift[i, layer : layer + 1] = rows[shift : shift + 1]
        for side in range(2):
            for t in range(5):
                at = 10 + 5 * side + t
                k.v_taps[layer, t, side : side + 1] = rows[at : at + 1]
    k.save(k.v_gain, k.o_gain)
    k.save(k.v_shift, k.o_shift)
    k.save(k.v_taps, k.o_taps)
    k.done()


def finish_call(outputs, dx, small_sum, groups, layers, width, ff):
    part, feed = width // 8, ff // 8
    args = {}
    s = Scratch()
    s.bring(args, outputs=outputs, dx=dx, small_sum=small_sum)
    s.add(v_dx32=vmem(dx.shape, F32))
    for i, array in enumerate(array for group in groups for array in group):
        s.bring(args, **{"g%d" % i: array})
    mixer, few = (layers, part, width), (3, layers, part)
    shapes = dict(local=(layers, 3 * part, width), mix=mixer, query=mixer)
    shapes.update(kv=(layers, 2 * part, width), taps=(layers, 5, 2, part), mix2=mixer)
    shapes.update(up=(layers, width, feed), down=(layers, feed, width), gain=few, shift=few)
    outs = dict(o_outputs=(outputs.shape, BF16), o_dx=(dx.shape, F32))
    for name, shape in shapes.items():
        outs["o_" + name] = (shape, F32)
        s.add("v_", **{name: vmem(shape, F32)})
    s.sems(16, 32, 1)
    made = run_kernel(lambda k: finish(k, layers, width, ff), "finish", None, args, outs, s)
    made.o_local, made.o_query, made.o_kv = (
        jnp.swapaxes(array, 1, 2) for array in (made.o_local, made.o_query, made.o_kv)
    )
    made.o_taps = jnp.swapaxes(made.o_taps, 1, 2)
    made.o_gain, made.o_shift = jnp.swapaxes(made.o_gain, 0, 1), jnp.swapaxes(made.o_shift, 0, 1)
    return tuple(vars(made).values())


def with_halo(array, sides, width):
    for axis, dim in sides:
        peers, length = (lax.axis_size(axis), array.shape[dim])
        up = [(i, (i + 1) % peers) for i in range(peers - 1)]
        down = [(j, i) for i, j in up]
        last = lax.slice_in_dim(array, length - width, length, axis=dim)
        first = lax.slice_in_dim(array, 0, width, axis=dim)
        before = lax.ppermute(last, axis, up)
        after = lax.ppermute(first, axis, down)
        array = jnp.concatenate([before, array, after], axis=dim)
    return array


def from_behind(value, axis, steps):
    count = lax.axis_size(axis)
    first, last = (max(0, -steps), min(count, count - steps))
    return lax.ppermute(value, axis, [(source, source + steps) for source in range(first, last)])


def layer_norm(summed, gain, shift_bias):
    centre = summed - jnp.mean(summed, -1, keepdims=True)
    spread = jnp.mean(centre * centre, -1, keepdims=True)
    return centre * lax.rsqrt(spread + EPSILON) * gain + shift_bias


def exact_gelu(value):
    return jax.nn.gelu(value, approximate=False)


def mul_plain(left_rows, right_mat):
    return jnp.dot(left_rows, right_mat, preferred_element_type=jnp.float32)


def mul_last(left_rows, right_mat):
    return lax.dot_general(
        left_rows, right_mat, (((1,), (1,)), ((), ())), preferred_element_type=jnp.float32
    )


def mul_first(left_rows, right_rows):
    return lax.dot_general(
        left_rows, right_rows, (((0,), (0,)), ((), ())), preferred_element_type=jnp.float32
    )


def as_rows(array_in):
    return array_in.reshape(-1, array_in.shape[-1])


def masked_scores(queries, key_rows, allowed):
    factor = queries.shape[-1] ** (-0.5)
    scores = (
        jnp.einsum("nqhe,nkhe->nhqk", queries, key_rows, preferred_element_type=jnp.float32)
        * factor
    )
    return (jnp.where(allowed[:, None], scores, MASKED), factor)


def attend(queries, key_rows, value_rows, allowed):
    scores, factor = masked_scores(queries, key_rows, allowed)
    row_top = jnp.max(scores, -1, keepdims=True)
    raised = jnp.exp(scores - row_top)
    row_total = jnp.sum(raised, -1, keepdims=True)
    soft_weights = (raised / row_total).astype(jnp.bfloat16)
    mixed = jnp.einsum(
        "nhqk,nkhe->nqhe", soft_weights, value_rows, preferred_element_type=jnp.float32
    )
    return (mixed, row_top + jnp.log(row_total))


def attend_back(queries, key_rows, value_rows, allowed, log_total, grad_mixed):
    scores, factor = masked_scores(queries, key_rows, allowed)
    soft_full = jnp.exp(scores - log_total)
    soft_weights = soft_full.astype(jnp.bfloat16)
    grad_values = jnp.einsum(
        "nhqk,nqhe->nkhe", soft_weights, grad_mixed, preferred_element_type=jnp.float32
    )
    grad_soft = jnp.einsum(
        "nqhe,nkhe->nhqk", grad_mixed, value_rows, preferred_element_type=jnp.float32
    )
    row_inner = jnp.sum(soft_full * grad_soft, -1, keepdims=True)
    grad_scores = (soft_full * (grad_soft - row_inner)).astype(jnp.bfloat16)
    grad_queries = (
        jnp.einsum("nhqk,nkhe->nqhe", grad_scores, key_rows, preferred_element_type=jnp.float32)
        * factor
    )
    grad_keys = (
        jnp.einsum("nhqk,nqhe->nkhe", grad_scores, queries, preferred_element_type=jnp.float32)
        * factor
    )
    return (grad_queries, grad_keys, grad_values)


def apply_taps(extended, taps):
    pool_rows = (extended.shape[1] - 2) // 4
    total = extended[:, 0 : 4 * pool_rows : 4] * taps[:, 0]
    for tap_at in range(1, 5):
        total = total + extended[:, tap_at : tap_at + 4 * pool_rows : 4] * taps[:, tap_at]
    return total


def taps_back(extended, taps, grad_pool):
    pool_rows = grad_pool.shape[1]
    grad_ext = jnp.zeros(extended.shape, jnp.float32)
    tap_grads = []
    for tap_at in range(5):
        tap_rows = extended[:, tap_at : tap_at + 4 * pool_rows : 4]
        tap_grads.append(jnp.sum(tap_rows * grad_pool, axis=(0, 1)))
        grad_ext = grad_ext.at[:, tap_at : tap_at + 4 * pool_rows : 4].add(
            grad_pool * taps[:, tap_at]
        )
    return (grad_ext, jnp.stack(tap_grads, 1))


def by_sequence(
    inputs,
    question_count,
    question_at,
    local_proj,
    local_mixer,
    pooled_proj,
    pool_taps,
    pooled_mixer,
    expand_weight,
    reduce_weight,
    norm_gain,
    norm_shift,
    output_grad,
):
    docs_here, tok_here, width = inputs.shape
    layers = local_proj.shape[0]
    heads = width // HD
    half_win = LOCAL_WIN // 2
    seq_count = lax.axis_size("seq")
    seq_at = lax.axis_index("seq")
    length = tok_here * seq_count
    positions = seq_at * tok_here + jnp.arange(tok_here, dtype=jnp.int32)
    slots = jnp.arange(question_at.shape[1], dtype=jnp.int32)
    question = jnp.any(
        (question_at[:, :, None] == positions[None, None, :])
        & (slots[None, :, None] < question_count[:, None, None]),
        axis=1,
    )
    near_cols = seq_at * tok_here - half_win + jnp.arange(tok_here + 2 * half_win, dtype=jnp.int32)
    local_allowed = (
        (jnp.abs(positions[:, None] - near_cols[None, :]) <= half_win)
        & (near_cols[None, :] >= 0)
        & (near_cols[None, :] < length)
    )[None]
    pool_cols = jnp.arange(length // 4, dtype=jnp.int32)
    pool_allowed = (
        jnp.abs(pool_cols[None, None, :] - (positions // 4)[None, :, None]) <= POOL_WIN // 2
    ) | question[:, :, None]
    head_shape = (docs_here, tok_here, heads, HD)
    hidden_now = inputs.astype(jnp.float32)
    saved_all = []
    for layer_at in range(layers):
        in_rows = hidden_now.astype(jnp.bfloat16)
        local_heads = (
            mul_plain(as_rows(in_rows), local_proj[layer_at])
            .astype(jnp.bfloat16)
            .reshape(docs_here, tok_here, 3, heads, HD)
        )
        forward_near_kv = with_halo(local_heads[:, :, 1:], (("seq", 1),), half_win)
        local_result, local_lse = attend(
            local_heads[:, :, 0], forward_near_kv[:, :, 0], forward_near_kv[:, :, 1], local_allowed
        )
        local_mix = local_result.astype(jnp.bfloat16).reshape(docs_here, tok_here, width)
        first_sum = hidden_now + mul_plain(as_rows(local_mix), local_mixer[layer_at]).reshape(
            hidden_now.shape
        )
        first_norm = layer_norm(first_sum, norm_gain[layer_at, 0], norm_shift[layer_at, 0])
        second_in = first_norm.astype(jnp.bfloat16)
        pooled_heads = (
            mul_plain(as_rows(second_in), pooled_proj[layer_at])
            .astype(jnp.bfloat16)
            .reshape(docs_here, tok_here, 3, heads, HD)
        )
        prior_kv = from_behind(pooled_heads[:, tok_here - 2 :, 1:], "seq", 1)
        extended = jnp.concatenate([prior_kv, pooled_heads[:, :, 1:]], 1).astype(jnp.float32)
        forward_taps = pool_taps[layer_at].reshape(2, 5, heads, HD)
        pooled = apply_taps(extended, forward_taps).astype(jnp.bfloat16)
        forward_all_pooled = lax.all_gather(pooled, "seq", axis=1, tiled=True)
        pooled_result, pooled_lse = attend(
            pooled_heads[:, :, 0],
            forward_all_pooled[:, :, 0],
            forward_all_pooled[:, :, 1],
            pool_allowed,
        )
        pooled_mix = pooled_result.astype(jnp.bfloat16).reshape(docs_here, tok_here, width)
        second_sum = first_norm + mul_plain(as_rows(pooled_mix), pooled_mixer[layer_at]).reshape(
            hidden_now.shape
        )
        second_norm = layer_norm(second_sum, norm_gain[layer_at, 1], norm_shift[layer_at, 1])
        ffn_in = second_norm.astype(jnp.bfloat16)
        up_proj = mul_plain(as_rows(ffn_in), expand_weight[layer_at])
        activated = exact_gelu(up_proj).astype(jnp.bfloat16)
        third_sum = second_norm + mul_plain(activated, reduce_weight[layer_at]).reshape(
            hidden_now.shape
        )
        result = layer_norm(third_sum, norm_gain[layer_at, 2], norm_shift[layer_at, 2])
        forward_saved = SimpleNamespace(
            in_rows=in_rows,
            local_heads=local_heads,
            near_kv=forward_near_kv,
            local_lse=local_lse,
            local_mix=local_mix,
            first_sum=first_sum,
            second_in=second_in,
            pooled_heads=pooled_heads,
            extended=extended,
            saved_pool=forward_all_pooled,
            pooled_lse=pooled_lse,
            pooled_mix=pooled_mix,
            second_sum=second_sum,
            ffn_in=ffn_in,
            up_proj=up_proj,
            activated=activated,
            third_sum=third_sum,
        )
        hidden_now = result
        saved_all.append(forward_saved)
    outputs = hidden_now.astype(jnp.bfloat16)
    grad_now = output_grad.astype(jnp.float32)
    grads_list = [None] * layers
    for layer_at in reversed(range(layers)):
        backward_saved = saved_all[layer_at]
        gain_row = norm_gain[layer_at]
        bias_row = norm_shift[layer_at]
        taps = pool_taps[layer_at].reshape(2, 5, heads, HD)
        unused_third, pull_third = jax.vjp(
            layer_norm, backward_saved.third_sum, gain_row[2], bias_row[2]
        )
        grad_third, gain_third, bias_third = pull_third(grad_now)
        grad_down_in = as_rows(grad_third.astype(jnp.bfloat16))
        down_grad = mul_first(backward_saved.activated, grad_down_in)
        grad_act = mul_last(grad_down_in, reduce_weight[layer_at])
        unused_gelu, pull_gelu = jax.vjp(exact_gelu, backward_saved.up_proj)
        grad_up = pull_gelu(grad_act)[0].astype(jnp.bfloat16)
        up_grad = mul_first(as_rows(backward_saved.ffn_in), grad_up)
        grad_second = grad_third + mul_last(grad_up, expand_weight[layer_at]).reshape(
            grad_now.shape
        )
        unused_second, pull_second = jax.vjp(
            layer_norm, backward_saved.second_sum, gain_row[1], bias_row[1]
        )
        grad_mid, gain_second, bias_second = pull_second(grad_second)
        grad_pool_mix = as_rows(grad_mid.astype(jnp.bfloat16))
        out2_grad = mul_first(as_rows(backward_saved.pooled_mix), grad_pool_mix)
        grad_pool_out = (
            mul_last(grad_pool_mix, pooled_mixer[layer_at]).astype(jnp.bfloat16).reshape(head_shape)
        )
        all_pooled = backward_saved.saved_pool
        grad_pool_query, grad_pool_key, grad_pool_value = attend_back(
            backward_saved.pooled_heads[:, :, 0],
            all_pooled[:, :, 0],
            all_pooled[:, :, 1],
            pool_allowed,
            backward_saved.pooled_lse,
            grad_pool_out,
        )
        own_key = lax.psum_scatter(
            grad_pool_key.astype(jnp.bfloat16), "seq", scatter_dimension=1, tiled=True
        ).astype(jnp.float32)
        own_value = lax.psum_scatter(
            grad_pool_value.astype(jnp.bfloat16), "seq", scatter_dimension=1, tiled=True
        ).astype(jnp.float32)
        grad_ext, taps_grad = taps_back(
            backward_saved.extended, taps, jnp.stack([own_key, own_value], 2)
        )
        from_next = from_behind(grad_ext[:, :2].astype(jnp.bfloat16), "seq", -1).astype(jnp.float32)
        grad_kv_second = grad_ext[:, 2:].at[:, tok_here - 2 :].add(from_next)
        grad_heads_two = (
            jnp.concatenate([grad_pool_query[:, :, None], grad_kv_second], 2)
            .astype(jnp.bfloat16)
            .reshape(-1, 3 * width)
        )
        proj2_grad = mul_first(as_rows(backward_saved.second_in), grad_heads_two)
        grad_first = grad_mid + mul_last(grad_heads_two, pooled_proj[layer_at]).reshape(
            grad_now.shape
        )
        unused_first, pull_first = jax.vjp(
            layer_norm, backward_saved.first_sum, gain_row[0], bias_row[0]
        )
        grad_low, gain_first, bias_first = pull_first(grad_first)
        grad_local_mix = as_rows(grad_low.astype(jnp.bfloat16))
        out1_grad = mul_first(as_rows(backward_saved.local_mix), grad_local_mix)
        grad_local_out = (
            mul_last(grad_local_mix, local_mixer[layer_at]).astype(jnp.bfloat16).reshape(head_shape)
        )
        near_kv = backward_saved.near_kv
        grad_local_query, grad_near_key, grad_near_value = attend_back(
            backward_saved.local_heads[:, :, 0],
            near_kv[:, :, 0],
            near_kv[:, :, 1],
            local_allowed,
            backward_saved.local_lse,
            grad_local_out,
        )
        grad_near = jnp.stack([grad_near_key, grad_near_value], 2)
        rim_rows = jnp.concatenate(
            [grad_near[:, :half_win], grad_near[:, tok_here + half_win :]], 1
        )
        came_back = with_halo(rim_rows.astype(jnp.bfloat16), (("seq", 1),), half_win).astype(
            rim_rows.dtype
        )
        grad_kv_first = grad_near[:, half_win : half_win + tok_here]
        grad_kv_first = grad_kv_first.at[:, :half_win].add(came_back[:, :half_win])
        grad_kv_first = grad_kv_first.at[:, tok_here - half_win :].add(came_back[:, 3 * half_win :])
        grad_heads_one = (
            jnp.concatenate([grad_local_query[:, :, None], grad_kv_first], 2)
            .astype(jnp.bfloat16)
            .reshape(-1, 3 * width)
        )
        proj1_grad = mul_first(as_rows(backward_saved.in_rows), grad_heads_one)
        grad_bottom = grad_low + mul_last(grad_heads_one, local_proj[layer_at]).reshape(
            grad_now.shape
        )
        layer_grads = (
            proj1_grad,
            out1_grad,
            proj2_grad[:, :width],
            proj2_grad[:, width:],
            taps_grad.reshape(2, 5, width),
            out2_grad,
            up_grad,
            down_grad,
            jnp.stack([gain_first, gain_second, gain_third]),
            jnp.stack([bias_first, bias_second, bias_third]),
        )
        grad_now, layer_grads = (grad_bottom, layer_grads)
        grads_list[layer_at] = layer_grads
    stacked = [jnp.stack([layer_set[member] for layer_set in grads_list]) for member in range(10)]
    shards_all = (
        lax.psum_scatter(
            stacked[0].astype(jnp.bfloat16), "seq", scatter_dimension=2, tiled=True
        ).astype(jnp.float32),
        lax.psum_scatter(
            stacked[1].astype(jnp.bfloat16), "seq", scatter_dimension=1, tiled=True
        ).astype(jnp.float32),
        lax.psum_scatter(
            stacked[2].astype(jnp.bfloat16), "seq", scatter_dimension=2, tiled=True
        ).astype(jnp.float32),
        lax.psum_scatter(
            stacked[3].astype(jnp.bfloat16), "seq", scatter_dimension=2, tiled=True
        ).astype(jnp.float32),
        lax.psum_scatter(
            stacked[4].astype(jnp.bfloat16), "seq", scatter_dimension=3, tiled=True
        ).astype(jnp.float32),
        lax.psum_scatter(
            stacked[5].astype(jnp.bfloat16), "seq", scatter_dimension=1, tiled=True
        ).astype(jnp.float32),
        lax.psum_scatter(
            stacked[6].astype(jnp.bfloat16), "seq", scatter_dimension=2, tiled=True
        ).astype(jnp.float32),
        lax.psum_scatter(
            stacked[7].astype(jnp.bfloat16), "seq", scatter_dimension=1, tiled=True
        ).astype(jnp.float32),
        lax.psum_scatter(
            stacked[8].astype(jnp.bfloat16), "seq", scatter_dimension=2, tiled=True
        ).astype(jnp.float32),
        lax.psum_scatter(
            stacked[9].astype(jnp.bfloat16), "seq", scatter_dimension=2, tiled=True
        ).astype(jnp.float32),
    )
    stacked = (
        lax.psum(shards_all[0].astype(jnp.bfloat16), "doc").astype(jnp.float32),
        lax.psum(shards_all[1].astype(jnp.bfloat16), "doc").astype(jnp.float32),
        lax.psum(shards_all[2].astype(jnp.bfloat16), "doc").astype(jnp.float32),
        lax.psum(shards_all[3].astype(jnp.bfloat16), "doc").astype(jnp.float32),
        lax.psum(shards_all[4].astype(jnp.bfloat16), "doc").astype(jnp.float32),
        lax.psum(shards_all[5].astype(jnp.bfloat16), "doc").astype(jnp.float32),
        lax.psum(shards_all[6].astype(jnp.bfloat16), "doc").astype(jnp.float32),
        lax.psum(shards_all[7].astype(jnp.bfloat16), "doc").astype(jnp.float32),
        lax.psum(shards_all[8].astype(jnp.bfloat16), "doc").astype(jnp.float32),
        lax.psum(shards_all[9].astype(jnp.bfloat16), "doc").astype(jnp.float32),
    )
    return (
        outputs,
        grad_now,
        stacked[0],
        stacked[1],
        stacked[2],
        stacked[3],
        stacked[4],
        stacked[5],
        stacked[6],
        stacked[7],
        stacked[8],
        stacked[9],
    )


def solution(mesh):
    planes, places = mesh.shape["doc"], mesh.shape["seq"]

    def per_device(inputs, *others):
        docs_here, tok_here, _ = inputs.shape
        whole = docs_here == 4 and 2 * docs_here == places and planes == 4 and tok_here == 128
        return (by_chip if whole else by_sequence)(inputs, *others)

    return jax.shard_map(
        per_device,
        mesh=mesh,
        in_specs=(
            P("doc", "seq", None),
            P("doc"),
            P("doc", None),
            P(),
            P(),
            P(),
            P(),
            P(),
            P(),
            P(),
            P(),
            P(),
            P("doc", "seq", None),
        ),
        out_specs=(
            P("doc", "seq", None),
            P("doc", "seq", None),
            P(None, None, "seq"),
            P(None, "seq", None),
            P(None, None, "seq"),
            P(None, None, "seq"),
            P(None, None, None, "seq"),
            P(None, "seq", None),
            P(None, None, "seq"),
            P(None, "seq", None),
            P(None, None, "seq"),
            P(None, None, "seq"),
        ),
        check_vma=False,
    )
```

```python
from types import SimpleNamespace

import jax
import jax.numpy as jnp
from jax import lax
from jax.experimental import pallas as pl
from jax.experimental.pallas import tpu as pltpu
from jax.sharding import PartitionSpec as P

HD = 64
LOCAL_WIN = 128
POOL_WIN = 512
EPSILON = 1e-05
MASKED = -1e30
F32 = jnp.float32
BF16 = jnp.bfloat16
MESH = pl.DeviceIdType.MESH
ANY = pl.BlockSpec(memory_space=pl.ANY)
VMEM = pl.BlockSpec(memory_space=pltpu.VMEM)
VMEM_LIMIT = 60 * 1024 * 1024


def dot_nn(left, right):
    return jnp.dot(left, right, preferred_element_type=F32)


def dot_nt(left, right):
    return lax.dot_general(left, right, (((1,), (1,)), ((), ())), preferred_element_type=F32)


def dot_tn(left, right):
    return lax.dot_general(left, right, (((0,), (0,)), ((), ())), preferred_element_type=F32)


def loop(count, body):
    def step(i, carry):
        body(i)
        return carry

    lax.fori_loop(0, count, step, 0)


def aligned(index, size):
    return pl.ds(pl.multiple_of(index * size, size), size)


class Copies:
    def __init__(self, sems):
        self.sems = sems
        self.used = 0

    def start(self, source, target):
        copy = pltpu.make_async_copy(source, target, self.sems.at[self.used])
        self.used += 1
        copy.start()
        return copy


class Links:
    def __init__(self, send, recv):
        self.send, self.recv = send, recv
        self.used = 0

    def take(self):
        self.used += 1
        return self.used - 1

    def start(self, source, target, device):
        at = self.take()
        copy = pltpu.make_async_remote_copy(
            src_ref=source,
            dst_ref=target,
            send_sem=self.send.at[at],
            recv_sem=self.recv.at[at],
            device_id=device,
            device_id_type=MESH,
        )
        copy.start()
        return copy


def greet(devices):
    barrier = pltpu.get_barrier_semaphore()
    for device in devices:
        pl.semaphore_signal(barrier, inc=1, device_id=device, device_id_type=MESH)
    pl.semaphore_wait(barrier, len(devices))


class Regroup:
    def __init__(self, copies, links, source, target, gather):
        self.doc, self.me = lax.axis_index("doc"), lax.axis_index("seq")
        self.source, self.target = source, target
        self.gather = gather
        self.copies, self.links = copies, links
        self.local = copies.used
        copies.used += 1
        self.first = links.used
        links.used += 4

    def _to(self, i):
        if self.gather:
            return 2 * i + self.me // 4, self.me % 4
        return 4 * (self.me % 2) + i, self.me // 2

    def _from(self, i):
        if self.gather:
            return 4 * (self.me % 2) + i
        return 2 * i + self.me // 4

    def _remote(self, i, slot, device):
        return pltpu.make_async_remote_copy(
            src_ref=self.source.at[i],
            dst_ref=self.target.at[slot],
            send_sem=self.links.send.at[self.first + i],
            recv_sem=self.links.recv.at[self.first + slot],
            device_id=(self.doc, device),
            device_id_type=MESH,
        )

    def _local(self, i, slot):
        return pltpu.make_async_copy(
            self.source.at[i], self.target.at[slot], self.copies.sems.at[self.local]
        )

    def start(self):
        for i in range(4):
            device, slot = self._to(i)

            @pl.when(device == self.me)
            def _():
                self._local(i, slot).start()

            @pl.when(device != self.me)
            def _():
                self._remote(i, slot, device).start()

    def wait(self):
        for i in range(4):
            device, slot = self._to(i)

            @pl.when(device == self.me)
            def _():
                self._local(i, slot).wait()

            @pl.when(device != self.me)
            def _():
                self._remote(i, slot, device).wait_send()

        for i in range(4):

            @pl.when(self._from(i) != self.me)
            def _():
                self._remote(i, i, self._from(i)).wait_recv()


def regroup_peers():
    me = lax.axis_index("seq")
    return [2 * i + me // 4 for i in range(4)], [4 * (me % 2) + i for i in range(4)]


def greet_regroup(others):
    doc, me = lax.axis_index("doc"), lax.axis_index("seq")
    barrier = pltpu.get_barrier_semaphore()
    to, back = regroup_peers()
    for device in to + back:

        @pl.when(device != me)
        def _():
            pl.semaphore_signal(barrier, inc=1, device_id=(doc, device), device_id_type=MESH)

    for device in others:
        pl.semaphore_signal(barrier, inc=1, device_id=device, device_id_type=MESH)
    inside = me // 4 == me % 2
    pl.semaphore_wait(barrier, len(others) + jnp.where(inside, 6, 8))


def split_masks(width):
    lane = lax.broadcasted_iota(jnp.int32, (1, 2 * HD), 1)
    low = (lane < HD).astype(F32)
    return low, 1.0 - low


def by_head(rows, low, high, factor):
    wide = rows.astype(F32) * factor
    return jnp.concatenate([wide * low, wide * high], 0).astype(BF16)


def from_heads(stacked, low, high):
    rows = stacked.shape[0] // 2
    return stacked[:rows] * low + stacked[rows:] * high


def attend_blocks(queries, key_rows, value_rows, bias):
    low, high = split_masks(2 * HD)
    wide_bias = jnp.concatenate([bias, bias], 0)
    scores = [
        dot_nt(by_head(query, low, high, HD**-0.5), key) + wide_bias
        for query, key in zip(queries, key_rows)
    ]
    soft = []
    for score in scores:
        raised = jnp.exp(score - jnp.max(score, -1, keepdims=True))
        soft.append((raised.astype(BF16), 1.0 / jnp.sum(raised, -1, keepdims=True)))
    return [
        from_heads(dot_nn(raised, value) * share, low, high).astype(BF16)
        for (raised, share), value in zip(soft, value_rows)
    ]


def local_bias(at, blocks, length_first, length_last, rows, half):
    shape = (rows, rows + 2 * half)
    query = lax.broadcasted_iota(jnp.int32, shape, 0)
    key = lax.broadcasted_iota(jnp.int32, shape, 1)
    first = jnp.where(length_first & (at == 0), half, 0)
    last = jnp.where(length_last & (at == blocks - 1), rows + half, rows + 2 * half)
    seen = (key >= query) & (key <= query + 2 * half) & (key >= first) & (key < last)
    return jnp.where(seen, 0.0, MASKED).astype(F32)


def norm_rows(summed, gain, shift):
    centre = summed - jnp.mean(summed, -1, keepdims=True)
    spread = jnp.mean(centre * centre, -1, keepdims=True)
    rate = lax.rsqrt(spread + EPSILON)
    plain = centre * rate
    return plain, rate, plain * gain + shift


def gelu_rows(u):
    t = 1.0 / (1.0 + (0.3275911 * 0.5**0.5) * jnp.abs(u))
    series = 0.5307027145 * t - 0.7265760135
    series = series * t + 0.7107068705
    series = series * t - 0.142248368
    series = series * t + 0.127414796
    bell = jnp.exp2((u * u) * -0.7213475204444817)
    tail = series * t * bell
    share = jnp.where(u < 0, tail, 1.0 - tail)
    return u * share, share + (u * 0.3989422804014327) * bell


def vmem(shape, kind=BF16):
    return pltpu.VMEM(shape, kind)


class Scratch:
    def __init__(self):
        self.names, self.shapes = [], []

    def add(self, tag="", **shapes):
        for name, shape in shapes.items():
            self.names.append(tag + name)
            self.shapes.append(shape)

    def plane(self, tag, block):
        first = vmem((2, 2, 4, 2) + block)
        second, total = vmem((2, 2, 4) + block), vmem((2, 4, 2) + block)
        self.add(tag, kept=first, got1=first, got2=second, total=total)

    def line(self, tag, block):
        whole = vmem((2, 2, 2, 2) + block)
        self.add(tag, own=vmem((2, 2) + block), got=vmem((2, 4, 2) + block), whole=whole)

    def core(self, tag, block):
        group = vmem((2, 4, 2, 2, 2) + block)
        self.add(tag, send=group, mine=group, got=group)

    def sems(self, loads, saves, links):
        dma = pltpu.SemaphoreType.DMA
        self.add(load_sems=dma((loads,)), save_sems=dma((saves,)))
        self.add(send_sems=dma((links,)), recv_sems=dma((links,)))

    def bring(self, args, **arrays):
        for name, array in arrays.items():
            args[name] = (array, ANY)
            self.names.append("v_" + name)
            self.shapes.append(pltpu.VMEM(array.shape, array.dtype))


class Kernel:
    def __init__(self, names, refs):
        self.__dict__.update(zip(names, refs))
        assert len(names) == len(refs)
        self.loads = Copies(self.load_sems)
        self.saves = Copies(self.save_sems)
        self.links = Links(self.send_sems, self.recv_sems)
        self.waits = []

    def load(self, source, target):
        return self.loads.start(source, target)

    def load_all(self, names):
        return {name: self.load(getattr(self, name), getattr(self, "v_" + name)) for name in names}

    def save(self, source, target):
        self.waits.append(self.saves.start(source, target))

    def done(self):
        for wait in self.waits:
            wait.wait()


def run_kernel(body, name, collective, args, outs, scratch):
    names = list(args) + list(outs) + scratch.names

    def kernel(*refs):
        k = Kernel(names, refs)
        body(k)
        for used, sems in ((k.loads, k.load_sems), (k.saves, k.save_sems), (k.links, k.send_sems)):
            assert used.used <= sems.shape[0]

    made = pl.pallas_call(
        kernel,
        out_shape=[jax.ShapeDtypeStruct(shape, kind) for shape, kind in outs.values()],
        in_specs=[spec for _, spec in args.values()],
        out_specs=[ANY] * len(outs),
        scratch_shapes=scratch.shapes,
        compiler_params=pltpu.CompilerParams(
            collective_id=collective,
            has_side_effects=collective is not None,
            vmem_limit_bytes=VMEM_LIMIT,
        ),
        name=name,
    )(*(array for array, _ in args.values()))
    return SimpleNamespace(**dict(zip(outs, made)))


def turn(source, target):
    for i in range(0, source.shape[1], 128):
        target[i : i + 128] = source[:, i : i + 128].T


GAIN, SHIFT, TAPS = 0, 3, 6


def small_row(k, layer, row, lane=None, count=None):
    lanes = slice(None) if lane is None else slice(lane, lane + count)
    return k.small[layer, row : row + 1, lanes]


def fill_pooled_bias(k, rows, core):
    doc = lax.axis_index("seq") // 2
    places = k.places[pl.ds(doc, 1)]
    slot = lax.broadcasted_iota(jnp.int32, (128, places.shape[1]), 1)
    column = lax.broadcasted_iota(jnp.int32, (128, rows // 2), 1)
    for i in range(0, rows, 128):
        here = core * rows + i
        position = lax.broadcasted_iota(jnp.int32, (128, places.shape[1]), 0) + here
        hit = (position == places) & (slot < k.counts[doc])
        question = jnp.max(hit.astype(F32), -1, keepdims=True)
        own = (lax.broadcasted_iota(jnp.int32, (128, rows // 2), 0) + here) // 4
        near = jnp.where(jnp.abs(column - own) <= POOL_WIN // 2, 1.0, 0.0)
        bias = jnp.where(near + question > 0.5, 0.0, MASKED).astype(F32)
        k.pbias[i : i + 128] = bias
        k.pbias_t[:, i : i + 128] = bias.T


def forward(k, layer, first, last, rows, width, ff):
    half = LOCAL_WIN // 2
    pool = rows // 4
    blocks = rows // 128
    pairs = width // (2 * HD)
    lanes_of = [slice(2 * HD * pair, 2 * HD * (pair + 1)) for pair in range(pairs)]
    values_of = [slice(width + s.start, width + s.stop) for s in lanes_of]
    core = lax.axis_index("seq") % 2
    sibling = axis_peers()[0]
    links = k.links

    def weight(source, target):
        return k.load(source.at[layer], target)

    got_small = k.load(k.small_in, k.small)
    if not first:
        got_x = k.load(k.x_in, k.xf)
    got = [weight(k.w_local, k.wl)]
    if first:
        greet_regroup([sibling])
        incoming = Regroup(k.loads, links, k.x_in, k.x, True)
        incoming.start()
        background = Regroup(k.loads, links, k.grad_in, k.grad_got, True)
        fill_pooled_bias(k, rows, core)
        k.save(k.pbias, k.o_pbias)
        k.save(k.pbias_t, k.o_pbias_t)
    else:
        greet([sibling])
    for i in range(blocks):
        k.lbias[i] = local_bias(i, blocks, core == 0, core == 1, 128, half)
    k.kvf[:, pl.ds(0, 8)] = jnp.zeros((2 * width // 128, 8, 128), F32)

    if first:
        incoming.wait()
        xrows = k.x.reshape(rows, width)
    else:
        got_x.wait()
        xrows = k.x
        for i in range(0, rows, 128):
            k.x[i : i + 128] = k.xf[i : i + 128].astype(BF16)
    k.save(k.x, k.o_x)
    got += [weight(k.w_mix, k.wm), weight(k.w_pooled, k.wp)]
    if not first:
        got_bias = k.load(k.pbias_in, k.pbias)

    got[0].wait()
    for i in range(0, 2 * width, 256):
        k.kv[half : half + rows, i : i + 256] = dot_nn(
            xrows[...], k.wl[:, width + i : width + i + 256]
        ).astype(BF16)
    rim = links.start(
        k.kv.at[pl.ds(pl.multiple_of(half + (rows - half) * (1 - core), half), half)],
        k.halo,
        sibling,
    )
    for i in range(0, width, 256):
        k.q[:, i : i + 256] = dot_nn(xrows[...], k.wl[:, i : i + 256]).astype(BF16)
    k.save(k.q, k.o_q)
    rim.wait()
    k.kv[pl.ds(pl.multiple_of((rows + half) * (1 - core), half), half)] = k.halo[...]
    k.kv[pl.ds(pl.multiple_of((rows + half) * core, half), half)] = jnp.zeros_like(k.halo)
    k.save(k.kv, k.o_kv)

    def attend_local(i):
        here, seen = aligned(i, 128), pl.ds(pl.multiple_of(i * 128, 128), 128 + 2 * half)
        mixed = attend_blocks(
            [k.q[here, lanes] for lanes in lanes_of],
            [k.kv[seen, lanes] for lanes in lanes_of],
            [k.kv[seen, lanes] for lanes in values_of],
            k.lbias[i],
        )
        for lanes, part in zip(lanes_of, mixed):
            k.a[here, lanes] = part

    loop(blocks, attend_local)
    k.save(k.a, k.o_a)
    got += [weight(k.w_mix2, k.wm2), weight(k.w_up, k.wu), weight(k.w_down, k.wd)]
    if first:
        background.start()
    got_small.wait()

    def mix_norm(at_norm, mixed, weight, residual, plain_ref, rate_ref, full_ref, narrow_ref):
        gain, shift = small_row(k, layer, GAIN + at_norm), small_row(k, layer, SHIFT + at_norm)
        for i in range(0, rows, 128):
            at = slice(i, i + 128)
            update = k.acc[at] if weight is None else dot_nn(mixed[at], weight[...])
            plain, rate, full = norm_rows(residual[at].astype(F32) + update, gain, shift)
            plain_ref[at] = plain.astype(BF16)
            rate_ref[at] = jnp.broadcast_to(rate, (128, 128))
            if full_ref is not None:
                full_ref[at] = full
            if narrow_ref is not None:
                narrow_ref[at] = full.astype(BF16)

    got[1].wait()
    mix_norm(0, k.a, k.wm, xrows if first else k.xf, k.xh, k.rt, k.x1f, k.x1)
    k.save(k.xh, k.o_xh1)
    k.save(k.rt, k.o_r1)
    k.save(k.x1, k.o_x1)

    got[2].wait()
    for i in range(0, 2 * width, 256):
        part = dot_nn(k.x1[...], k.wp[:, width + i : width + i + 256]).astype(BF16)
        k.kv2[:, i : i + 256] = part
        k.kvf[i // 128, 8 : 8 + rows] = part[:, :128].astype(F32)
        k.kvf[i // 128 + 1, 8 : 8 + rows] = part[:, 128:].astype(F32)
    k.save(k.kv2, k.o_kv2)
    for chunk in range(2 * width // 128):
        side, lane = chunk * 128 // width, chunk * 128 % width
        lanes = slice(chunk * 128, chunk * 128 + 128)
        total = jnp.zeros((pool, 128), F32)
        tail = jnp.zeros((1, 128), F32)
        for t in range(5):
            tap = small_row(k, layer, TAPS + 5 * side + t, lane, 128)
            total = total + k.kvf[chunk, pl.ds(6 + t, pool, stride=4)] * tap
            if t < 2:
                tail = tail + k.kvf[chunk, pl.ds(6 + rows + t, 1)] * tap
        k.kp_own[:, lanes] = total.astype(BF16)
        k.aux_own[0:8, lanes] = jnp.broadcast_to(tail, (8, 128))
        k.aux_own[8:16, lanes] = total[:8]
    pooled_out = links.start(k.kp_own, k.kp_got, sibling)
    aux_out = links.start(k.aux_own, k.aux_got, sibling)
    for i in range(0, width, 256):
        k.q2[:, i : i + 256] = dot_nn(k.x1[...], k.wp[:, i : i + 256]).astype(BF16)
    k.save(k.q2, k.o_q2)
    if not first:
        got_bias.wait()
    pooled_out.wait()
    aux_out.wait()
    k.pk[pl.ds(pl.multiple_of(core * pool, pool), pool)] = k.kp_own[...]
    k.pk[pl.ds(pl.multiple_of((1 - core) * pool, pool), pool)] = k.kp_got[...]
    tail = jnp.where(core == 0, k.aux_own[0:1], k.aux_got[0:1])
    head = jnp.where(core == 0, k.aux_got[8:9], k.aux_own[8:9])
    edge = lax.broadcasted_iota(jnp.int32, (16, 1), 0) == 0
    k.pk[pool : pool + 16] = jnp.where(
        edge, jnp.broadcast_to(head + tail, (16, 2 * width)), k.pk[pool : pool + 16].astype(F32)
    ).astype(BF16)
    k.save(k.pk, k.o_pk)

    def attend_pooled(i):
        here = aligned(i, 128)
        mixed = attend_blocks(
            [k.q2[here, lanes] for lanes in lanes_of],
            [k.pk[:, lanes] for lanes in lanes_of],
            [k.pk[:, lanes] for lanes in values_of],
            k.pbias[here],
        )
        for lanes, part in zip(lanes_of, mixed):
            k.b[here, lanes] = part

    loop(blocks, attend_pooled)
    k.save(k.b, k.o_b)
    got[3].wait()
    mix_norm(1, k.b, k.wm2, k.x1f, k.xh2, k.rt2, k.x1f, k.x2)
    k.save(k.xh2, k.o_xh2)
    k.save(k.rt2, k.o_r2)
    k.save(k.x2, k.o_x2)

    got[4].wait()
    got[5].wait()
    part, up = 512, (k.up_a, k.up_b)
    count = ff // part

    def expand(i):
        up[i % 2][...] = dot_nn(k.x2[...], k.wu[:, i * part : (i + 1) * part])

    expand(0)
    for i in range(count):
        if i + 1 < count:
            expand(i + 1)
        lanes = slice(i * part, (i + 1) * part)
        full, slope = gelu_rows(up[i % 2][...])
        k.g[:, lanes] = full.astype(BF16)
        k.gp[:, lanes] = slope.astype(BF16)
        k.save(k.g.at[:, lanes], k.o_g.at[:, lanes])
        k.save(k.gp.at[:, lanes], k.o_gp.at[:, lanes])
        product = dot_nn(full.astype(BF16), k.wd[lanes])
        if i == 0:
            k.acc[...] = product
        else:
            k.acc[...] += product
    result = k.out16 if last else k.xf
    mix_norm(
        2, None, None, k.x1f, k.xh3, k.rt3, None if last else result, result if last else None
    )
    k.save(k.xh3, k.o_xh3)
    k.save(k.rt3, k.o_r3)
    k.save(result, k.o_out)
    if first:
        background.wait()
        k.save(k.grad_got, k.o_grad)
    k.done()


def forward_call(layer, first, last, x_in, small, weights, extra):
    width, ff = weights[0].shape[1], weights[4].shape[2]
    rows = x_in.shape[0] * x_in.shape[1] if first else x_in.shape[0]
    half, pool = LOCAL_WIN // 2, rows // 4
    x_shape = (4, rows // 4, width) if first else (rows, width)
    local, mixer, pooled, mixer2, up, down = ((weight, ANY) for weight in weights)
    args = dict(x_in=(x_in, ANY), small_in=(small, ANY), w_local=local, w_mix=mixer)
    args.update(w_pooled=pooled, w_mix2=mixer2, w_up=up, w_down=down)
    wide, kv = ((rows, width), BF16), ((rows + 2 * half, 2 * width), BF16)
    rate, feed, full = ((rows, 128), F32), ((rows, ff), BF16), ((rows, width), F32)
    outs = dict(o_x=(x_shape, BF16), o_q=wide, o_kv=kv, o_a=wide, o_xh1=wide, o_r1=rate)
    outs.update(o_x1=wide, o_q2=wide, o_kv2=((rows, 2 * width), BF16))
    outs.update(o_pk=((2 * pool, 2 * width), BF16), o_b=wide, o_xh2=wide, o_r2=rate)
    outs.update(o_x2=wide, o_g=feed, o_gp=feed, o_xh3=wide, o_r3=rate)
    outs.update(o_out=wide if last else full)
    s = Scratch()
    wl, wm, wp, wm2, wu, wd = (vmem(weight.shape[1:]) for weight in weights)
    s.add(wl=wl, wm=wm, wp=wp, wm2=wm2, wu=wu, wd=wd)
    wide, full, rate, feed = (vmem(*shape) for shape in (wide, full, rate, feed))
    s.add(small=vmem(small.shape, F32), x=vmem(x_shape))
    s.add(q=wide, a=wide, xh=wide, x1=wide, q2=wide, b=wide, xh2=wide, x2=wide, xh3=wide)
    s.add(xf=full, x1f=full, acc=full, rt=rate, rt2=rate, rt3=rate, g=feed, gp=feed)
    part, pooled = vmem((rows, 512), F32), vmem((pool, 2 * width))
    s.add(up_a=part, up_b=part, kv=vmem(*kv), kv2=vmem((rows, 2 * width)))
    s.add(kvf=vmem((2 * width // 128, rows + 16, 128), F32), pk=vmem((2 * pool, 2 * width)))
    aux = vmem((16, 2 * width), F32)
    s.add(halo=vmem((half, 2 * width)), kp_own=pooled, kp_got=pooled, aux_own=aux, aux_got=aux)
    s.add(lbias=vmem((rows // 128, 128, 128 + 2 * half), F32))
    s.add(pbias=vmem((rows, 2 * pool), F32))
    if last:
        s.add(out16=wide)
    if first:
        counts, places, grad_in = extra
        args.update(counts=(counts, pl.BlockSpec(memory_space=pltpu.SMEM)))
        args.update(places=(places, VMEM), grad_in=(grad_in, ANY))
        outs.update(o_grad=(grad_in.shape, BF16))
        outs.update(o_pbias=((rows, 2 * pool), F32), o_pbias_t=((2 * pool, rows), F32))
        s.add(grad_got=vmem(grad_in.shape), pbias_t=vmem((2 * pool, rows), F32))
    else:
        args.update(pbias_in=(extra, ANY))
    s.sems(16, 40, 12)
    return run_kernel(
        lambda k: forward(k, layer, first, last, rows, width, ff),
        "forward_%d" % layer,
        layer,
        args,
        outs,
        s,
    )


def axis_peers():
    doc, me = lax.axis_index("doc"), lax.axis_index("seq")
    core, z = me % 2, me // 2
    along = (z + 1 - 2 * (z % 2), z + 2 - 4 * (z // 2), 3 - z)
    return (
        (doc, me + 1 - 2 * core),
        (doc + 1 - 2 * (doc % 2), me),
        (doc + 2 - 4 * (doc // 2), me),
        [(doc, 2 * other + core) for other in along],
        along,
    )


BOTH = (0, 1)


class CoreSum:
    def __init__(self, k, tag):
        self.links = k.links
        self.send, self.own, self.got = (getattr(k, tag + part) for part in ("send", "mine", "got"))
        self.copy = {}

    def start(self, part):
        self.copy[part] = self.links.start(
            self.send.at[part], self.got.at[part], axis_peers()[0]
        )

    def finish(self, *parts):
        for part in parts or BOTH:
            self.copy[part].wait()

            def add(z):
                self.own[part, z] += self.got[part, z]

            loop(4, add)


class PlaneSum:
    def __init__(self, k, tag, source):
        self.links, self.copies, self.source = k.links, k.loads, source
        self.kept, self.got1, self.got2, self.total = (
            getattr(k, tag + part) for part in ("kept", "got1", "got2", "total")
        )
        doc = lax.axis_index("doc")
        self.x, self.y = doc % 2, doc // 2
        self.copy = {}

    def start(self, *parts):
        _, across, up, _, _ = axis_peers()
        x, y = self.x, self.y
        for part in parts or BOTH:
            source, got = self.source.at[part], self.got1.at[part]
            self.copy[part] = [
                self.links.start(source.at[:, 0, :, 1 - x], got.at[0], across),
                self.links.start(source.at[:, 1, 1 - y], got.at[1], up),
                self.copies.start(source.at[:, 0, :, x], self.kept.at[part, 0]),
                self.copies.start(source.at[:, 1, y], self.kept.at[part, 1]),
            ]

    def middle(self, *parts):
        _, across, up, _, _ = axis_peers()
        for part in parts or BOTH:
            for copy in self.copy[part]:
                copy.wait()

            def add(half):
                self.kept[part, half] += self.got1[part, half]

            loop(2, add)
            kept, got = self.kept.at[part], self.got2.at[part]
            self.copy[part] = [
                self.links.start(kept.at[0, :, 1 - self.y], got.at[0], up),
                self.links.start(kept.at[1, :, 1 - self.x], got.at[1], across),
            ]

    def finish(self, *parts):
        for part in parts or BOTH:
            for copy in self.copy[part]:
                copy.wait()
            for z in range(4):
                self.total[part, z, 0] = self.kept[part, 0, z, self.y] + self.got2[part, 0, z]
                self.total[part, z, 1] = self.kept[part, 1, z, self.x] + self.got2[part, 1, z]


class LineSum:
    def __init__(self, k, tag, source):
        self.links, self.copies, self.source = k.links, k.loads, source
        self.whole = getattr(k, tag + "whole")
        if hasattr(k, tag + "own"):
            self.own, self.got = getattr(k, tag + "own"), getattr(k, tag + "got")
        doc = lax.axis_index("doc")
        self.x, self.y = doc % 2, doc // 2
        self.copy = {}

    def start(self, *parts):
        _, _, _, line, along = axis_peers()
        for part in parts or BOTH:
            source = self.source.at[part]
            self.copy[part] = [
                self.links.start(source.at[other], self.got.at[part, i], device)
                for i, (other, device) in enumerate(zip(along, line))
            ]
            self.copy[part].append(
                self.copies.start(source.at[lax.axis_index("seq") // 2], self.own.at[part])
            )

    def settle(self, *parts):
        for part in parts or BOTH:
            for copy in self.copy[part]:
                copy.wait()
            for half in range(2):
                total = self.own[part, half].astype(F32)
                for i in range(3):
                    total = total + self.got[part, i, half].astype(F32)
                self.whole[part, half, self.y, self.x] = total.astype(BF16)

    def take(self):
        return [
            self.copies.start(self.source.at[part, half], self.whole.at[part, half, self.y, self.x])
            for part in range(2)
            for half in range(2)
        ]

    def give(self, k, target):
        for part in range(2):
            for half in range(2):
                k.save(self.whole.at[part, half, self.y, self.x], target.at[part, half])

    def gather(self, *parts):
        _, across, up, _, _ = axis_peers()
        for part in parts or BOTH:
            first = self.whole.at[part, 0, self.y, self.x]
            second = self.whole.at[part, 1, self.y, self.x]
            self.copy[part] = [
                self.links.start(first, first, across),
                self.links.start(second, second, up),
            ]

    def middle(self, *parts):
        for part in parts or BOTH:
            self.settle(part)
            self.gather(part)

    def spread(self, *parts):
        _, across, up, _, _ = axis_peers()
        for part in parts or BOTH:
            for copy in self.copy[part]:
                copy.wait()
            first = self.whole.at[part, 0, self.y]
            second = self.whole.at[part, 1, :, self.x]
            self.copy[part] = [
                self.links.start(first, first, up),
                self.links.start(second, second, across),
            ]

    def finish(self, *parts):
        for part in parts or BOTH:
            for copy in self.copy[part]:
                copy.wait()


class RelaySum(LineSum):
    def __init__(self, k, tag, source):
        super().__init__(k, tag, source)
        self.doc, me = lax.axis_index("doc"), lax.axis_index("seq")
        self.core, self.z = me % 2, me // 2
        self.near = self.z + 1 - 2 * (self.z % 2)
        self.far = [2 - 2 * (self.z // 2) + i for i in range(2)]
        self.inner = (self.z == 1) | (self.z == 2)
        self.first = {}

    def _send(self, part, source, slot, send, recv, z):
        at = self.first[part]
        return pltpu.make_async_remote_copy(
            src_ref=source,
            dst_ref=self.got.at[part, slot],
            send_sem=self.links.send.at[at + send],
            recv_sem=self.links.recv.at[at + recv],
            device_id=(self.doc, 2 * z + self.core),
            device_id_type=MESH,
        )

    def _beside(self, part):
        return self._send(part, self.source.at[part, self.near], 0, 0, 0, self.near)

    def _past(self, part, i):
        return self._send(part, self.source.at[part, self.far[i]], 2 + i, 1 + i, 1 + i, self.near)

    def _across(self, part, i):
        return self._send(part, self.got.at[part, 2 + i], 1, 3 + i, 3, self.far[i])

    def start(self, *parts):
        for part in parts or BOTH:
            self.first[part] = self.links.used
            self.links.used += 5

            @pl.when(jnp.logical_not(self.inner))
            def _():
                for i in range(2):
                    self._past(part, i).start()

            self._beside(part).start()

    def relay(self, part):
        @pl.when(self.inner)
        def _():
            for i in range(2):
                self._past(part, i).wait_recv()
                self.got[part, 2 + i] += self.source[part, self.far[i]]
                self._across(part, i).start()

    def settle(self, *parts):
        for part in parts or BOTH:
            self._beside(part).wait()
            self._across(part, 0).wait_recv()

            @pl.when(self.inner)
            def _():
                for i in range(2):
                    self._across(part, i).wait_send()

            @pl.when(jnp.logical_not(self.inner))
            def _():
                for i in range(2):
                    self._past(part, i).wait_send()

            for half in range(2):
                total = self.source[part, self.z, half].astype(F32)
                for i in range(2):
                    total = total + self.got[part, i, half].astype(F32)
                self.whole[part, half, self.y, self.x] = total.astype(BF16)


def norm_back(k, rows, incoming, plain_ref, rate_ref, gain, full, narrow, sums, at_sum):
    for i in range(0, rows, 128):
        at = slice(i, i + 128)
        grad = incoming(at)
        plain = plain_ref[at].astype(F32)
        rate = rate_ref[at][:, :1]
        scaled = grad * gain
        even = jnp.mean(scaled, -1, keepdims=True)
        tilt = jnp.mean(scaled * plain, -1, keepdims=True)
        result = rate * (scaled - even - plain * tilt)
        full[at] = result
        narrow[at] = result.astype(BF16)
        for j, part in enumerate((grad * plain, grad)):
            part = jnp.sum(part.reshape(16, 8, -1), 0)
            if i == 0:
                sums[at_sum + j] = part
            else:
                sums[at_sum + j] += part


def attend_back_blocks(queries, key_rows, value_rows, grads_mixed, bias):
    low, high = split_masks(2 * HD)
    wide_bias = jnp.concatenate([bias, bias], 1)
    first = []
    for query, key, value, grad in zip(queries, key_rows, value_rows, grads_mixed):
        stacked, grads = by_head(query, low, high, HD**-0.5), by_head(grad, low, high, 1.0)
        first.append((stacked, grads, dot_nt(key, stacked) + wide_bias, dot_nt(value, grads)))
    second = []
    for _, _, scores, grad_soft in first:
        raised = jnp.exp(scores - jnp.max(scores, 0, keepdims=True))
        soft = raised * (1.0 / jnp.sum(raised, 0, keepdims=True))
        inner = jnp.sum(soft * grad_soft, 0, keepdims=True)
        second.append((soft.astype(BF16), (soft * (grad_soft - inner)).astype(BF16)))
    result = []
    for (stacked, grads, _, _), (soft, grad_scores), key in zip(first, second, key_rows):
        grad_queries = from_heads(dot_tn(grad_scores, key), low, high) * HD**-0.5
        result.append(
            (grad_queries.astype(BF16), dot_nn(grad_scores, stacked), dot_nn(soft, grads))
        )
    return result


def local_bias_turned(at, blocks, length_first, length_last, rows, half):
    shape = (rows + 2 * half, rows)
    key = lax.broadcasted_iota(jnp.int32, shape, 0)
    query = lax.broadcasted_iota(jnp.int32, shape, 1)
    first = jnp.where(length_first & (at == 0), half, 0)
    last = jnp.where(length_last & (at == blocks - 1), rows + half, rows + 2 * half)
    seen = (key >= query) & (key <= query + 2 * half) & (key >= first) & (key < last)
    return jnp.where(seen, 0.0, MASKED).astype(F32)


def place_piece(target, part, z, top, bottom):
    block = target.shape[5:]
    target[part, z, 0] = top[: 4 * block[0]].reshape((2, 2) + block).astype(BF16)
    target[part, z, 1, 0] = top[4 * block[0] :].reshape((2,) + block).astype(BF16)
    target[part, z, 1, 1] = bottom.reshape((2,) + block).astype(BF16)


def whole_piece(target, part, z, value):
    target[part, z] = value.reshape(target.shape[2:]).astype(BF16)


def feed_back(k, layer, rows, width, ff, last):
    core = lax.axis_index("seq") % 2
    sibling, across, up, line_peers, _ = axis_peers()
    shard = ff // 8
    got = k.load_all("dy xh3 r3".split())
    got_small = k.load(k.small_in, k.small)
    if not last:
        greet([sibling, across, up] + line_peers)
        before, line = PlaneSum(k, "x_", k.x_in), LineSum(k, "z_", k.z_in)
        before.start()
        line.start()
    got.update(k.load_all(["g"]))
    for name in ("dy", "xh3", "r3"):
        got[name].wait()
    got_small.wait()
    incoming = k.v_dy.reshape(rows, width) if last else k.v_dy
    norm_back(
        k,
        rows,
        lambda at: incoming[at].astype(F32),
        k.v_xh3,
        k.v_r3,
        small_row(k, layer, GAIN + 2),
        k.res,
        k.dn,
        k.sums,
        0,
    )
    got.update(k.load_all(["gp"]))
    got_down = k.load(k.w_down.at[layer], k.v_down)
    turn(k.dn, k.dn_t)
    got["g"].wait()
    reduced, expanded = CoreSum(k, "r_"), CoreSum(k, "e_")
    middle = width // 2

    def reduce_part(part, which, target):
        rows_of = slice(part * middle, (part + 1) * middle)
        for z in range(4):
            lanes = aligned(2 * z + which, shard)
            whole_piece(target, part, z, dot_nn(k.dn_t[rows_of], k.v_g[:, lanes]))

    def slope_part(first):
        for i in range(first, first + ff // 2, 512):
            k.du[:, i : i + 512] = (
                dot_nt(k.dn[...], k.v_down[i : i + 512]) * k.v_gp[:, i : i + 512].astype(F32)
            ).astype(BF16)

    reduce_part(0, 1 - core, k.r_send)
    if last:
        greet_regroup([sibling, across, up] + line_peers)
    reduced.start(0)
    reduce_part(1, 1 - core, k.r_send)
    reduced.start(1)
    got.update(k.load_all("x2 xh2 r2".split()))
    got_up = k.load(k.w_up.at[layer], k.v_up)
    reduce_part(0, core, k.r_mine)
    reduce_part(1, core, k.r_mine)
    if last:
        outward = Regroup(k.loads, k.links, k.x3, k.regrouped, False)
        outward.start()
    got["gp"].wait()
    got_down.wait()
    plane = PlaneSum(k, "r_", k.r_mine)
    if last:
        reduced.finish(0)
        plane.start(0)
    else:
        before.middle(0)
    slope_part(0)
    reduced.finish(*((1,) if last else BOTH))
    if not last:
        before.middle(1)
    plane.start(*((1,) if last else BOTH))
    slope_part(ff // 2)
    got["x2"].wait()
    turn(k.v_x2, k.x2_t)

    def expand_part(part, which, target):
        rows_of = slice(part * middle, (part + 1) * middle)
        for z in range(4):
            lanes = aligned(2 * z + which, shard)
            whole_piece(target, part, z, dot_nn(k.x2_t[rows_of], k.du[:, lanes]))

    for part in BOTH:
        expand_part(part, 1 - core, k.e_send)
        expanded.start(part)
    for part in BOTH:
        expand_part(part, core, k.e_mine)
    if not last:
        before.finish()
        late = LineSum(k, "y_", k.x_total)
        late.start()
        line.settle()
        line.give(k, k.o_z)
    else:
        plane.middle(0)
    got_up.wait()
    for i in range(0, width, 256):
        k.res[:, i : i + 256] += dot_nt(k.du[...], k.v_up[i : i + 256])
    got["xh2"].wait()
    got["r2"].wait()
    norm_back(
        k,
        rows,
        lambda at: k.res[at],
        k.v_xh2,
        k.v_r2,
        small_row(k, layer, GAIN + 1),
        k.res,
        k.dn2,
        k.sums,
        2,
    )
    k.save(k.res, k.o_mid)
    k.save(k.dn2, k.o_dy2)
    save_sums(k, 4)
    expanded.finish()
    k.save(k.e_mine, k.o_e)
    plane.middle(*((1,) if last else BOTH))
    if last:
        outward.wait()
        k.save(k.regrouped, k.o_out)
    else:
        late.settle()
        late.give(k, k.o_y)
    plane.finish()
    k.save(k.r_total, k.o_r)
    k.done()


def pooled_back(k, layer, rows, width, last):
    core = lax.axis_index("seq") % 2
    sibling, across, up, line_peers, _ = axis_peers()
    pool = rows // 4
    pairs, blocks = width // (2 * HD), rows // 128
    shard = width // 8
    got = k.load_all(["dy2"])
    got_mix = k.load(k.w_mix2.at[layer], k.v_mix2)
    got_small = k.load(k.small_in, k.small)
    late = [] if last else [LineSum(k, "y_", k.y_in), LineSum(k, "w_", k.w_in)]
    got_late = [copy for each in late for copy in each.take()]
    greet([sibling, across, up] + line_peers)
    plane, line = PlaneSum(k, "x_", k.x_in), LineSum(k, "z_", k.z_in)
    for copy in got_late:
        copy.wait()
    for each in late:
        each.gather()
    plane.start()
    line.start()
    got.update(k.load_all("q2 pk".split()))
    got_bias = k.load(k.pbias, k.v_pbias)
    got["dy2"].wait()
    got_mix.wait()
    got.update(k.load_all("kv2 b".split()))
    for i in range(0, width, 256):
        k.do[:, i : i + 256] = dot_nt(k.v_dy2[...], k.v_mix2[i : i + 256]).astype(BF16)
    for name in ("q2", "pk"):
        got[name].wait()
    k.dkv[...] = jnp.zeros_like(k.dkv)
    got_bias.wait()
    got.update(k.load_all("x1 mid xh1 r1".split()))
    got_proj = k.load(k.w_pooled.at[layer], k.v_pooled)
    lanes_of = [slice(2 * HD * pair, 2 * HD * (pair + 1)) for pair in range(pairs)]
    values_of = [slice(width + part.start, width + part.stop) for part in lanes_of]

    def attend_part(i):
        here = aligned(i, 128)
        parts = attend_back_blocks(
            [k.v_q2[here, lanes] for lanes in lanes_of],
            [k.v_pk[:, lanes] for lanes in lanes_of],
            [k.v_pk[:, lanes] for lanes in values_of],
            [k.do[here, lanes] for lanes in lanes_of],
            k.v_pbias[:, here],
        )
        for lanes, values, (grad_q, grad_k, grad_v) in zip(lanes_of, values_of, parts):
            k.dqkv[here, lanes] = grad_q
            k.dkv[:, lanes] += grad_k
            k.dkv[:, values] += grad_v

    loop(blocks, attend_part)
    k.rim_out[...] = k.dkv[pl.ds(pl.multiple_of((pool - 16) * (1 - core), 16), pool + 16)].astype(
        BF16
    )
    rim = k.links.start(k.rim_out, k.rim_got, sibling)
    got["b"].wait()
    turn(k.v_b, k.b_t)
    got["kv2"].wait()
    for c in range(2 * width // 128):
        k.kvf[c, :rows] = k.v_kv2[:, pl.ds(c * 128, 128)].astype(F32)
    got_small.wait()
    rim.wait()
    k.total[pl.ds(0, pool)] = (
        k.dkv[pl.ds(pl.multiple_of(core * pool, pool), pool)]
        + k.rim_got[pl.ds(pl.multiple_of(core * 16, 16), pool)].astype(F32)
    )
    k.total[pl.ds(pool, 8)] = jnp.where(
        core == 0, k.dkv[pl.ds(pool, 8)] + k.rim_got[pl.ds(pool, 16)].astype(F32)[:8], 0.0
    )

    for c in range(2 * width // 128):
        side, lane = c * 128 // width, c * 128 % width
        lanes = pl.ds(c * 128, 128)
        own, after = k.total[pl.ds(0, pool), lanes], k.total[pl.ds(1, pool), lanes]
        rows_at = [pl.ds(j, pool, stride=4) for j in range(4)]
        kept = [k.kvf[c, at] for at in rows_at]
        taps = [small_row(k, layer, TAPS + 5 * side + t, lane, 128) for t in range(5)]
        pairs_of = ((kept[2], after), (kept[3], after), (kept[0], own), (kept[1], own), (kept[2], own))
        for t, (token, grad) in enumerate(pairs_of):
            k.tap_sums[side, 8 * t : 8 * t + 8, lane : lane + 128] = jnp.sum(
                (token * grad).reshape(pool // 8, 8, 128), 0
            )
        k.kvf[c, rows_at[0]] = own * taps[2]
        k.kvf[c, rows_at[1]] = own * taps[3]
        k.kvf[c, rows_at[2]] = own * taps[4] + after * taps[0]
        k.kvf[c, rows_at[3]] = after * taps[1]
        k.dqkv[:, pl.ds(width + c * 128, 128)] = k.kvf[c, :rows].astype(BF16)
    turn(k.dqkv, k.dqkv_t)
    got["x1"].wait()
    for each in late:
        each.spread()
    line.settle()
    if last:
        line.gather()
    else:
        line.give(k, k.o_z)
    plane.middle()
    summed = CoreSum(k, "p_")
    middle = width // 2

    def grad_part(part, which, target):
        lanes = slice(part * middle, (part + 1) * middle)
        mixers = jnp.concatenate(
            [k.b_t[aligned(2 * z + which, shard)] for z in range(4)], 0
        )
        k.mixed[...] = dot_nn(mixers, k.v_dy2[:, lanes])

        for z in range(4):
            at = 2 * z + which
            mine = jnp.concatenate(
                [
                    k.dqkv_t[aligned(at, shard)],
                    k.dqkv_t[pl.ds(pl.multiple_of(width + at * 2 * shard, 2 * shard), 2 * shard)],
                ],
                0,
            )
            place_piece(
                target, part, z, dot_nn(mine, k.v_x1[:, lanes]), k.mixed[z * shard : (z + 1) * shard]
            )

    for part in BOTH:
        grad_part(part, 1 - core, k.p_send)
        summed.start(part)
    for part in BOTH:
        grad_part(part, core, k.p_mine)
    got["mid"].wait()
    got_proj.wait()

    for i in range(0, width, 256):
        k.v_mid[:, i : i + 256] += dot_nt(k.dqkv[...], k.v_pooled[i : i + 256])
    got["xh1"].wait()
    got["r1"].wait()
    norm_back(
        k,
        rows,
        lambda at: k.v_mid[at],
        k.v_xh1,
        k.v_r1,
        small_row(k, layer, GAIN),
        k.v_mid,
        k.dn,
        k.sums,
        0,
    )
    k.save(k.v_mid, k.o_low)
    k.save(k.dn, k.o_dy1)
    save_sums(k, 2, k.tap_sums)
    if last:
        line.spread()
    plane.finish()
    k.save(k.x_total, k.o_x)
    summed.finish()
    k.save(k.p_mine, k.o_p)
    if last:
        line.finish()
        k.save(k.z_whole, k.o_z)
    else:
        for each, target in zip(late, (k.o_y, k.o_w)):
            each.finish()
            k.save(each.whole, target)
    k.done()


def local_back(k, layer, rows, width, final):
    core = lax.axis_index("seq") % 2
    sibling, across, up, line_peers, _ = axis_peers()
    half = LOCAL_WIN // 2
    pairs, blocks = width // (2 * HD), rows // 128
    shard = width // 8
    got = k.load_all(["dy1"])
    got_mix = k.load(k.w_mix.at[layer], k.v_mix)
    if final:
        greet_regroup([sibling, across, up] + line_peers)
    else:
        greet([sibling, across, up] + line_peers)
    plane, line = PlaneSum(k, "x_", k.x_in), LineSum(k, "z_", k.z_in)
    plane.start()
    line.start()
    got.update(k.load_all("q kv".split()))
    if final:
        small = SmallSum(k)
        small.load()
        early = LineSum(k, "r_", k.r_in)
        got_early = early.take()
    for i in range(blocks):
        k.lbias[i] = local_bias_turned(i, blocks, core == 0, core == 1, 128, half)
    got["dy1"].wait()
    got_mix.wait()
    for i in range(0, width, 256):
        k.do[:, i : i + 256] = dot_nt(k.v_dy1[...], k.v_mix[i : i + 256]).astype(BF16)
    got.update(k.load_all("a x low".split()))
    got_proj = k.load(k.w_local.at[layer], k.v_local)
    for name in ("q", "kv"):
        got[name].wait()
    if final:
        small.step()
    k.dkv[...] = jnp.zeros_like(k.dkv)
    lanes_of = [slice(2 * HD * pair, 2 * HD * (pair + 1)) for pair in range(pairs)]
    values_of = [slice(width + part.start, width + part.stop) for part in lanes_of]

    def attend_part(i):
        here, seen = aligned(i, 128), pl.ds(pl.multiple_of(i * 128, 128), 128 + 2 * half)
        parts = attend_back_blocks(
            [k.v_q[here, lanes] for lanes in lanes_of],
            [k.v_kv[seen, lanes] for lanes in lanes_of],
            [k.v_kv[seen, lanes] for lanes in values_of],
            [k.do[here, lanes] for lanes in lanes_of],
            k.lbias[i],
        )
        for lanes, values, (grad_q, grad_k, grad_v) in zip(lanes_of, values_of, parts):
            k.dqkv[here, lanes] = grad_q
            k.dkv[seen, lanes] += grad_k
            k.dkv[seen, values] += grad_v

    loop(blocks, attend_part)
    k.rim_out[...] = k.dkv[pl.ds(pl.multiple_of((rows + half) * (1 - core), half), half)].astype(
        BF16
    )
    rim = k.links.start(k.rim_out, k.rim_got, sibling)
    got["a"].wait()
    turn(k.v_a, k.a_t)
    rim.wait()
    edge = pl.ds(pl.multiple_of(half + (rows - half) * (1 - core), half), half)
    k.dkv[edge] += k.rim_got[...].astype(F32)
    k.dqkv[:, width:] = k.dkv[half : half + rows].astype(BF16)
    turn(k.dqkv, k.dqkv_t)
    got["x"].wait()
    inputs = k.v_x.reshape(rows, width) if len(k.v_x.shape) == 3 else k.v_x
    summed = CoreSum(k, "l_")
    middle = width // 2

    def grad_part(part, which, target):
        lanes = slice(part * middle, (part + 1) * middle)
        mixers = jnp.concatenate(
            [k.a_t[aligned(2 * z + which, shard)] for z in range(4)], 0
        )
        k.mixed[...] = dot_nn(mixers, k.v_dy1[:, lanes])
        for z in range(4):
            mine = k.dqkv_t[aligned(2 * z + which, 3 * shard)]
            place_piece(
                target, part, z, dot_nn(mine, inputs[:, lanes]), k.mixed[z * shard : (z + 1) * shard]
            )

    def residual():
        got["low"].wait()
        got_proj.wait()
        for i in range(0, width, 256):
            k.v_low[:, i : i + 256] += dot_nt(k.dqkv[...], k.v_local[i : i + 256])

    if not final:
        line.middle()
        plane.middle()
        for part in BOTH:
            grad_part(part, 1 - core, k.l_send)
            summed.start(part)
        for part in BOTH:
            grad_part(part, core, k.l_mine)
        residual()
        k.save(k.v_low, k.o_dx)
        line.spread()
        plane.finish()
        k.save(k.x_total, k.o_x)
        summed.finish()
        k.save(k.l_mine, k.o_l)
        line.finish()
        k.save(k.z_whole, k.o_z)
        k.done()
        return
    small.step()
    residual()
    for i in range(0, rows, 128):
        k.narrow[i // 128] = k.v_low[i : i + 128].astype(BF16)
    outward = Regroup(k.loads, k.links, k.narrow, k.regrouped, False)
    outward.start()
    plane.middle()
    line.settle()
    for part in BOTH:
        grad_part(part, 1 - core, k.l_send)
        summed.start(part)
    small.step()
    last_plane, last_line = PlaneSum(k, "l_", k.l_mine), RelaySum(k, "f_", k.l_total)
    for part in BOTH:
        grad_part(part, core, k.l_mine)
    for part in BOTH:
        summed.finish(part)
        last_plane.start(part)
    plane.finish()
    before = RelaySum(k, "p_", k.x_total)
    before.start()
    small.step()
    last_plane.middle(0)
    for copy in got_early:
        copy.wait()
    last_plane.middle(1)
    before.relay(0)
    before.relay(1)
    line.gather()
    early.gather()
    for part in BOTH:
        last_plane.finish(part)
        last_line.start(part)
    before.settle()
    line.spread()
    early.spread()
    last_line.relay(0)
    before.gather()
    last_line.relay(1)
    small.finish()
    for each, target in ((line, k.o_z), (early, k.o_r)):
        each.finish()
        k.save(each.whole, target)
    before.spread()
    outward.wait()
    k.save(k.regrouped, k.o_dx)
    last_line.middle(0)
    before.finish()
    k.save(k.p_whole, k.o_p)
    last_line.middle(1)
    last_line.spread(0)
    last_line.spread(1)
    last_line.finish()
    k.save(k.f_whole, k.o_f)
    k.done()


class SmallSum:
    def __init__(self, k):
        self.k = k
        sibling, across, up, self.line, self.along = axis_peers()
        self.order = [sibling, across, up]
        self.at = 0

    def load(self):
        k = self.k
        self.copies = []
        for i, (feed, pooled) in enumerate(zip(k.s_feed, k.s_pool)):
            self.copies.append(k.load(feed, k.s_sum.at[24 * i : 24 * i + 8]))
            self.copies.append(k.load(pooled, k.s_sum.at[24 * i + 8 : 24 * i + 24]))

    def window(self, z):
        return pl.ds(pl.multiple_of(3 * z // 2 * 128, 128), 256)

    def step(self):
        k = self.k
        for copy in self.copies:
            copy.wait()
        if self.at > 0:
            k.s_sum[...] += k.s_got[self.at - 1].astype(F32)
        k.s_out[...] = k.s_sum[...].astype(BF16)
        if self.at < len(self.order):
            self.copies = [k.links.start(k.s_out, k.s_got.at[self.at], self.order[self.at])]
        else:
            self.copies = [
                k.links.start(k.s_out.at[:, self.window(z)], k.s_line.at[i], device)
                for i, (z, device) in enumerate(zip(self.along, self.line))
            ]
        self.at += 1

    def finish(self):
        k = self.k
        for copy in self.copies:
            copy.wait()
        mine = self.window(lax.axis_index("seq") // 2)
        total = k.s_sum[:, mine]
        for i in range(3):
            total = total + k.s_line[i].astype(F32)
        k.s_sum[:, mine] = total
        k.save(k.s_sum, k.o_small)


def save_sums(k, count, taps=None):
    for i in range(count):
        k.row_sums[i : i + 1] = jnp.sum(k.sums[i], 0, keepdims=True)
    at = count
    if taps is not None:
        for side in range(2):
            for t in range(5):
                k.row_sums[at : at + 1] = jnp.sum(
                    taps[side, 8 * t : 8 * t + 8], 0, keepdims=True
                )
                at += 1
    k.row_sums[at:] = jnp.zeros((k.row_sums.shape[0] - at, k.row_sums.shape[1]), F32)
    k.save(k.row_sums, k.o_sums)


def block_of(width):
    return (width // 16, width // 2)


def group_shape(block):
    return (2, 4, 2, 2, 2) + block


def total_shape(block):
    return (2, 4, 2) + block


def whole_shape(block):
    return (2, 2, 2, 2) + block


def feed_back_call(layer, last, dy, small, kept, w_down, w_up, x_in, z_in, outputs):
    rows, width = kept.o_xh3.shape
    ff = kept.o_g.shape[1]
    block = block_of(width)
    full, wide = (rows, width), vmem((rows, width))
    s = Scratch()
    args = dict(small_in=(small, ANY), w_down=(w_down, ANY), w_up=(w_up, ANY))
    s.bring(args, dy=dy, xh3=kept.o_xh3, r3=kept.o_r3, g=kept.o_g, gp=kept.o_gp)
    s.bring(args, x2=kept.o_x2, xh2=kept.o_xh2, r2=kept.o_r2)
    outs = dict(o_mid=(full, F32), o_dy2=(full, BF16), o_sums=((8, width), F32))
    outs.update(o_r=(total_shape(block), BF16), o_e=(group_shape(block), BF16))
    s.add(small=vmem(small.shape, F32), sums=vmem((4, 8, width), F32))
    s.add(v_down=vmem(w_down.shape[1:]), v_up=vmem(w_up.shape[1:]))
    s.add(row_sums=vmem((8, width), F32), res=vmem(full, F32), dn=wide, dn2=wide)
    s.add(dn_t=vmem((width, rows)), x2_t=vmem((width, rows)), du=vmem((rows, ff)))
    s.core("r_", block)
    s.core("e_", block)
    s.plane("r_", block)
    if last:
        by_doc = (4, rows // 4, width)
        args.update(x3=(outputs.reshape(by_doc), ANY))
        outs.update(o_out=(by_doc, BF16))
        s.add(regrouped=vmem(by_doc))
    else:
        args.update(x_in=(x_in, ANY), z_in=(z_in, ANY))
        outs.update(o_y=((2, 2) + block, BF16), o_z=((2, 2) + block, BF16))
        s.plane("x_", block)
        s.line("y_", block)
        s.line("z_", block)
    s.sems(40, 16, 48)
    return run_kernel(
        lambda k: feed_back(k, layer, rows, width, ff, last),
        "feed_back_%d" % layer,
        2 + layer,
        args,
        outs,
        s,
    )


def pooled_back_call(
    layer, last, mid, dy2, small, pbias, kept, w_mix2, w_pooled, x_in, z_in, y_in, w_in
):
    rows, width = mid.shape
    pool = rows // 4
    block = block_of(width)
    full, wide = (rows, width), vmem((rows, width))
    s = Scratch()
    args = dict(small_in=(small, ANY), w_mix2=(w_mix2, ANY), w_pooled=(w_pooled, ANY))
    args.update(x_in=(x_in, ANY), z_in=(z_in, ANY))
    s.bring(args, mid=mid, dy2=dy2, b=kept.o_b, q2=kept.o_q2, kv2=kept.o_kv2, pk=kept.o_pk)
    s.bring(args, x1=kept.o_x1, xh1=kept.o_xh1, r1=kept.o_r1, pbias=pbias)
    outs = dict(o_low=(full, F32), o_dy1=(full, BF16), o_sums=((16, width), F32))
    outs.update(o_p=(group_shape(block), BF16), o_x=(total_shape(block), BF16))
    outs.update(o_z=(whole_shape(block) if last else (2, 2) + block, BF16))
    s.add(small=vmem(small.shape, F32), v_mix2=vmem(w_mix2.shape[1:]))
    s.add(v_pooled=vmem(w_pooled.shape[1:]), sums=vmem((2, 8, width), F32))
    s.add(row_sums=vmem((16, width), F32), tap_sums=vmem((2, 40, width), F32), do=wide, dn=wide)
    rim, turned = vmem((pool + 16, 2 * width)), vmem((width, rows))
    s.add(dkv=vmem((2 * pool, 2 * width), F32), rim_out=rim, rim_got=rim)
    s.add(total=vmem((pool + 8, 2 * width), F32), kvf=vmem((2 * width // 128, rows + 8, 128), F32))
    s.add(dqkv=vmem((rows, 3 * width)), dqkv_t=vmem((3 * width, rows)), b_t=turned)
    s.add(mixed=vmem((width // 2, width // 2), F32))
    s.core("p_", block)
    s.plane("x_", block)
    s.line("z_", block)
    if not last:
        args.update(y_in=(y_in, ANY), w_in=(w_in, ANY))
        whole = whole_shape(block)
        outs.update(o_y=(whole, BF16), o_w=(whole, BF16))
        s.add(y_whole=vmem(whole), w_whole=vmem(whole))
    s.sems(40, 16, 48)
    return run_kernel(
        lambda k: pooled_back(k, layer, rows, width, last),
        "pooled_back_%d" % layer,
        4 + layer,
        args,
        outs,
        s,
    )


def local_back_call(layer, final, low, dy1, kept, w_mix, w_local, x_in, z_in, r_in, sums):
    rows, width = low.shape
    half = LOCAL_WIN // 2
    block = block_of(width)
    s = Scratch()
    args = dict(w_mix=(w_mix, ANY), w_local=(w_local, ANY), x_in=(x_in, ANY), z_in=(z_in, ANY))
    s.bring(args, low=low, dy1=dy1, a=kept.o_a, q=kept.o_q, kv=kept.o_kv, x=kept.o_x)
    outs = dict(o_z=(whole_shape(block), BF16))
    by_doc, total = (4, rows // 4, width), (len(sums) * 24, width)
    if final:
        whole = (whole_shape(block), BF16)
        for i, (feed, pooled) in enumerate(sums):
            args["s_feed%d" % i], args["s_pool%d" % i] = (feed, ANY), (pooled, ANY)
        args.update(r_in=(r_in, ANY))
        outs.update(o_dx=(by_doc, BF16), o_p=whole, o_f=whole, o_r=whole, o_small=(total, F32))
        s.add(r_whole=vmem(whole_shape(block)))
    else:
        outs.update(o_dx=((rows, width), F32), o_l=(group_shape(block), BF16))
        outs.update(o_x=(total_shape(block), BF16))
    s.add(v_mix=vmem(w_mix.shape[1:]), v_local=vmem(w_local.shape[1:]))
    s.add(lbias=vmem((rows // 128, 128 + 2 * half, 128), F32), do=vmem((rows, width)))
    s.add(dkv=vmem((rows + 2 * half, 2 * width), F32))
    s.add(rim_out=vmem((half, 2 * width)), rim_got=vmem((half, 2 * width)))
    s.add(dqkv=vmem((rows, 3 * width)), dqkv_t=vmem((3 * width, rows)))
    s.add(a_t=vmem((width, rows)), mixed=vmem((width // 2, width // 2), F32))
    s.core("l_", block)
    s.plane("x_", block)
    s.line("z_", block)
    if final:
        s.add(narrow=vmem(by_doc), regrouped=vmem(by_doc))
        s.add(s_sum=vmem(total, F32), s_out=vmem(total), s_got=vmem((3,) + total))
        s.add(s_line=vmem((3, len(sums) * 24, 256)))
        s.plane("l_", block)
        s.line("p_", block)
        s.line("f_", block)
    s.sems(48, 16, 96)

    def body(k):
        if final:
            k.s_feed = [getattr(k, "s_feed%d" % i) for i in range(len(sums))]
            k.s_pool = [getattr(k, "s_pool%d" % i) for i in range(len(sums))]
        local_back(k, layer, rows, width, final)

    return run_kernel(
        body,
        "local_back_%d" % layer,
        6 + layer,
        args,
        outs,
        s,
    )


def by_chip(
    inputs,
    question_count,
    question_at,
    local_proj,
    local_mixer,
    pooled_proj,
    pool_taps,
    pooled_mixer,
    expand_weight,
    reduce_weight,
    norm_gain,
    norm_shift,
    output_grad,
):
    docs_here, tok_here, width = inputs.shape
    layers, ff = local_proj.shape[0], expand_weight.shape[2]
    small = jnp.concatenate([norm_gain, norm_shift, pool_taps.reshape(layers, 10, width)], 1)
    weights = (local_proj, local_mixer, pooled_proj, pooled_mixer, expand_weight, reduce_weight)
    hidden, kept, bias = inputs, [], None
    for layer in range(layers):
        first, last = layer == 0, layer == layers - 1
        extra = (question_count, question_at, output_grad) if first else bias
        made = forward_call(layer, first, last, hidden, small, weights, extra)
        if first:
            grad, bias, bias_t = made.o_grad, made.o_pbias, made.o_pbias_t
        kept.append(made)
        hidden = made.o_out
    x_in = z_in = None
    reduced, expanded, pooled_sums, local_sums, sums = {}, {}, {}, {}, []
    for layer in reversed(range(layers)):
        last = layer == layers - 1
        saved = kept[layer]
        fed = feed_back_call(
            layer, last, grad, small, saved, reduce_weight, expand_weight, x_in, z_in, hidden
        )
        if last:
            outputs = fed.o_out
        pooled = pooled_back_call(
            layer,
            last,
            fed.o_mid,
            fed.o_dy2,
            small,
            bias_t,
            saved,
            pooled_mixer,
            pooled_proj,
            fed.o_e,
            fed.o_r,
            None if last else fed.o_y,
            None if last else fed.o_z,
        )
        if not last:
            local_sums[layer + 1], pooled_sums[layer + 1] = pooled.o_y, pooled.o_w
        sums.insert(0, (fed.o_sums, pooled.o_sums))
        local = local_back_call(
            layer,
            layer == 0,
            pooled.o_low,
            pooled.o_dy1,
            saved,
            local_mixer,
            local_proj,
            pooled.o_p,
            pooled.o_x,
            None if last else pooled.o_z,
            sums,
        )
        reduced[layer] = pooled.o_z if last else local.o_r
        expanded[layer] = local.o_z
        if layer > 0:
            grad, x_in, z_in = local.o_dx, local.o_l, local.o_x
    pooled_sums[0], local_sums[0] = local.o_p, local.o_f
    groups = [[group[i] for i in range(layers)] for group in (reduced, expanded, local_sums, pooled_sums)]
    return finish_call(outputs, local.o_dx, local.o_small, groups, layers, width, ff)


def finish(k, layers, width, ff):
    part, feed = width // 8, ff // 8
    me = lax.axis_index("seq")
    order = list(reversed(range(layers)))
    names = ["g%d" % i for i in range(4 * layers)]
    got = [k.load(getattr(k, name), getattr(k, "v_" + name)) for name in names]
    got_dx, got_small = k.load(k.dx, k.v_dx), k.load(k.small_sum, k.v_small_sum)
    got_out = k.load(k.outputs, k.v_outputs)

    def whole(group, layer, axis):
        got[group * layers + layer].wait()
        block = getattr(k, "v_" + names[group * layers + layer])
        parts = [block[i].reshape(-1, block.shape[-1]).astype(F32) for i in BOTH]
        return jnp.concatenate(parts, axis)

    def put(layer, source, target, value):
        source[layer] = value
        k.save(source.at[layer], target.at[layer])

    for layer in order:
        put(layer, k.v_down, k.o_down, whole(0, layer, 0).T)
        put(layer, k.v_up, k.o_up, whole(1, layer, 0))
    got_out.wait()
    k.save(k.v_outputs, k.o_outputs)
    got_dx.wait()
    for i in range(4):
        k.v_dx32[i] = k.v_dx[i].astype(F32)
    k.save(k.v_dx32, k.o_dx)
    for layer in order:
        local = whole(2, layer, 1)
        put(layer, k.v_local, k.o_local, local[: 3 * part])
        put(layer, k.v_mix, k.o_mix, local[3 * part :])
        pooled = whole(3, layer, 1)
        put(layer, k.v_query, k.o_query, pooled[:part])
        put(layer, k.v_kv, k.o_kv, pooled[part : 3 * part])
        put(layer, k.v_mix2, k.o_mix2, pooled[3 * part :])
    got_small.wait()
    small = k.v_small_sum[...]
    mine = jnp.zeros((small.shape[0], part), F32)
    for i in range(8):
        mine = jnp.where(me == i, small[:, i * part : (i + 1) * part], mine)
    for layer in range(layers):
        rows = mine[24 * layer : 24 * layer + 24]
        for i, (gain, shift) in enumerate(((8, 9), (2, 3), (0, 1))):
            k.v_gain[i, layer : layer + 1] = rows[gain : gain + 1]
            k.v_shift[i, layer : layer + 1] = rows[shift : shift + 1]
        for side in range(2):
            for t in range(5):
                at = 10 + 5 * side + t
                k.v_taps[layer, t, side : side + 1] = rows[at : at + 1]
    k.save(k.v_gain, k.o_gain)
    k.save(k.v_shift, k.o_shift)
    k.save(k.v_taps, k.o_taps)
    k.done()


def finish_call(outputs, dx, small_sum, groups, layers, width, ff):
    part, feed = width // 8, ff // 8
    args = {}
    s = Scratch()
    s.bring(args, outputs=outputs, dx=dx, small_sum=small_sum)
    s.add(v_dx32=vmem(dx.shape, F32))
    for i, array in enumerate(array for group in groups for array in group):
        s.bring(args, **{"g%d" % i: array})
    mixer, few = (layers, part, width), (3, layers, part)
    shapes = dict(local=(layers, 3 * part, width), mix=mixer, query=mixer)
    shapes.update(kv=(layers, 2 * part, width), taps=(layers, 5, 2, part), mix2=mixer)
    shapes.update(up=(layers, width, feed), down=(layers, feed, width), gain=few, shift=few)
    outs = dict(o_outputs=(outputs.shape, BF16), o_dx=(dx.shape, F32))
    for name, shape in shapes.items():
        outs["o_" + name] = (shape, F32)
        s.add("v_", **{name: vmem(shape, F32)})
    s.sems(16, 32, 1)
    made = run_kernel(lambda k: finish(k, layers, width, ff), "finish", None, args, outs, s)
    made.o_local, made.o_query, made.o_kv = (
        jnp.swapaxes(array, 1, 2) for array in (made.o_local, made.o_query, made.o_kv)
    )
    made.o_taps = jnp.swapaxes(made.o_taps, 1, 2)
    made.o_gain, made.o_shift = jnp.swapaxes(made.o_gain, 0, 1), jnp.swapaxes(made.o_shift, 0, 1)
    return tuple(vars(made).values())


def with_halo(array, sides, width):
    for axis, dim in sides:
        peers, length = (lax.axis_size(axis), array.shape[dim])
        up = [(i, (i + 1) % peers) for i in range(peers - 1)]
        down = [(j, i) for i, j in up]
        last = lax.slice_in_dim(array, length - width, length, axis=dim)
        first = lax.slice_in_dim(array, 0, width, axis=dim)
        before = lax.ppermute(last, axis, up)
        after = lax.ppermute(first, axis, down)
        array = jnp.concatenate([before, array, after], axis=dim)
    return array


def from_behind(value, axis, steps):
    count = lax.axis_size(axis)
    first, last = (max(0, -steps), min(count, count - steps))
    return lax.ppermute(value, axis, [(source, source + steps) for source in range(first, last)])


def layer_norm(summed, gain, shift_bias):
    centre = summed - jnp.mean(summed, -1, keepdims=True)
    spread = jnp.mean(centre * centre, -1, keepdims=True)
    return centre * lax.rsqrt(spread + EPSILON) * gain + shift_bias


def exact_gelu(value):
    return jax.nn.gelu(value, approximate=False)


def mul_plain(left_rows, right_mat):
    return jnp.dot(left_rows, right_mat, preferred_element_type=jnp.float32)


def mul_last(left_rows, right_mat):
    return lax.dot_general(
        left_rows, right_mat, (((1,), (1,)), ((), ())), preferred_element_type=jnp.float32
    )


def mul_first(left_rows, right_rows):
    return lax.dot_general(
        left_rows, right_rows, (((0,), (0,)), ((), ())), preferred_element_type=jnp.float32
    )


def as_rows(array_in):
    return array_in.reshape(-1, array_in.shape[-1])


def masked_scores(queries, key_rows, allowed):
    factor = queries.shape[-1] ** (-0.5)
    scores = (
        jnp.einsum("nqhe,nkhe->nhqk", queries, key_rows, preferred_element_type=jnp.float32)
        * factor
    )
    return (jnp.where(allowed[:, None], scores, MASKED), factor)


def attend(queries, key_rows, value_rows, allowed):
    scores, factor = masked_scores(queries, key_rows, allowed)
    row_top = jnp.max(scores, -1, keepdims=True)
    raised = jnp.exp(scores - row_top)
    row_total = jnp.sum(raised, -1, keepdims=True)
    soft_weights = (raised / row_total).astype(jnp.bfloat16)
    mixed = jnp.einsum(
        "nhqk,nkhe->nqhe", soft_weights, value_rows, preferred_element_type=jnp.float32
    )
    return (mixed, row_top + jnp.log(row_total))


def attend_back(queries, key_rows, value_rows, allowed, log_total, grad_mixed):
    scores, factor = masked_scores(queries, key_rows, allowed)
    soft_full = jnp.exp(scores - log_total)
    soft_weights = soft_full.astype(jnp.bfloat16)
    grad_values = jnp.einsum(
        "nhqk,nqhe->nkhe", soft_weights, grad_mixed, preferred_element_type=jnp.float32
    )
    grad_soft = jnp.einsum(
        "nqhe,nkhe->nhqk", grad_mixed, value_rows, preferred_element_type=jnp.float32
    )
    row_inner = jnp.sum(soft_full * grad_soft, -1, keepdims=True)
    grad_scores = (soft_full * (grad_soft - row_inner)).astype(jnp.bfloat16)
    grad_queries = (
        jnp.einsum("nhqk,nkhe->nqhe", grad_scores, key_rows, preferred_element_type=jnp.float32)
        * factor
    )
    grad_keys = (
        jnp.einsum("nhqk,nqhe->nkhe", grad_scores, queries, preferred_element_type=jnp.float32)
        * factor
    )
    return (grad_queries, grad_keys, grad_values)


def apply_taps(extended, taps):
    pool_rows = (extended.shape[1] - 2) // 4
    total = extended[:, 0 : 4 * pool_rows : 4] * taps[:, 0]
    for tap_at in range(1, 5):
        total = total + extended[:, tap_at : tap_at + 4 * pool_rows : 4] * taps[:, tap_at]
    return total


def taps_back(extended, taps, grad_pool):
    pool_rows = grad_pool.shape[1]
    grad_ext = jnp.zeros(extended.shape, jnp.float32)
    tap_grads = []
    for tap_at in range(5):
        tap_rows = extended[:, tap_at : tap_at + 4 * pool_rows : 4]
        tap_grads.append(jnp.sum(tap_rows * grad_pool, axis=(0, 1)))
        grad_ext = grad_ext.at[:, tap_at : tap_at + 4 * pool_rows : 4].add(
            grad_pool * taps[:, tap_at]
        )
    return (grad_ext, jnp.stack(tap_grads, 1))


def by_sequence(
    inputs,
    question_count,
    question_at,
    local_proj,
    local_mixer,
    pooled_proj,
    pool_taps,
    pooled_mixer,
    expand_weight,
    reduce_weight,
    norm_gain,
    norm_shift,
    output_grad,
):
    docs_here, tok_here, width = inputs.shape
    layers = local_proj.shape[0]
    heads = width // HD
    half_win = LOCAL_WIN // 2
    seq_count = lax.axis_size("seq")
    seq_at = lax.axis_index("seq")
    length = tok_here * seq_count
    positions = seq_at * tok_here + jnp.arange(tok_here, dtype=jnp.int32)
    slots = jnp.arange(question_at.shape[1], dtype=jnp.int32)
    question = jnp.any(
        (question_at[:, :, None] == positions[None, None, :])
        & (slots[None, :, None] < question_count[:, None, None]),
        axis=1,
    )
    near_cols = seq_at * tok_here - half_win + jnp.arange(tok_here + 2 * half_win, dtype=jnp.int32)
    local_allowed = (
        (jnp.abs(positions[:, None] - near_cols[None, :]) <= half_win)
        & (near_cols[None, :] >= 0)
        & (near_cols[None, :] < length)
    )[None]
    pool_cols = jnp.arange(length // 4, dtype=jnp.int32)
    pool_allowed = (
        jnp.abs(pool_cols[None, None, :] - (positions // 4)[None, :, None]) <= POOL_WIN // 2
    ) | question[:, :, None]
    head_shape = (docs_here, tok_here, heads, HD)
    hidden_now = inputs.astype(jnp.float32)
    saved_all = []
    for layer_at in range(layers):
        in_rows = hidden_now.astype(jnp.bfloat16)
        local_heads = (
            mul_plain(as_rows(in_rows), local_proj[layer_at])
            .astype(jnp.bfloat16)
            .reshape(docs_here, tok_here, 3, heads, HD)
        )
        forward_near_kv = with_halo(local_heads[:, :, 1:], (("seq", 1),), half_win)
        local_result, local_lse = attend(
            local_heads[:, :, 0], forward_near_kv[:, :, 0], forward_near_kv[:, :, 1], local_allowed
        )
        local_mix = local_result.astype(jnp.bfloat16).reshape(docs_here, tok_here, width)
        first_sum = hidden_now + mul_plain(as_rows(local_mix), local_mixer[layer_at]).reshape(
            hidden_now.shape
        )
        first_norm = layer_norm(first_sum, norm_gain[layer_at, 0], norm_shift[layer_at, 0])
        second_in = first_norm.astype(jnp.bfloat16)
        pooled_heads = (
            mul_plain(as_rows(second_in), pooled_proj[layer_at])
            .astype(jnp.bfloat16)
            .reshape(docs_here, tok_here, 3, heads, HD)
        )
        prior_kv = from_behind(pooled_heads[:, tok_here - 2 :, 1:], "seq", 1)
        extended = jnp.concatenate([prior_kv, pooled_heads[:, :, 1:]], 1).astype(jnp.float32)
        forward_taps = pool_taps[layer_at].reshape(2, 5, heads, HD)
        pooled = apply_taps(extended, forward_taps).astype(jnp.bfloat16)
        forward_all_pooled = lax.all_gather(pooled, "seq", axis=1, tiled=True)
        pooled_result, pooled_lse = attend(
            pooled_heads[:, :, 0],
            forward_all_pooled[:, :, 0],
            forward_all_pooled[:, :, 1],
            pool_allowed,
        )
        pooled_mix = pooled_result.astype(jnp.bfloat16).reshape(docs_here, tok_here, width)
        second_sum = first_norm + mul_plain(as_rows(pooled_mix), pooled_mixer[layer_at]).reshape(
            hidden_now.shape
        )
        second_norm = layer_norm(second_sum, norm_gain[layer_at, 1], norm_shift[layer_at, 1])
        ffn_in = second_norm.astype(jnp.bfloat16)
        up_proj = mul_plain(as_rows(ffn_in), expand_weight[layer_at])
        activated = exact_gelu(up_proj).astype(jnp.bfloat16)
        third_sum = second_norm + mul_plain(activated, reduce_weight[layer_at]).reshape(
            hidden_now.shape
        )
        result = layer_norm(third_sum, norm_gain[layer_at, 2], norm_shift[layer_at, 2])
        forward_saved = SimpleNamespace(
            in_rows=in_rows,
            local_heads=local_heads,
            near_kv=forward_near_kv,
            local_lse=local_lse,
            local_mix=local_mix,
            first_sum=first_sum,
            second_in=second_in,
            pooled_heads=pooled_heads,
            extended=extended,
            saved_pool=forward_all_pooled,
            pooled_lse=pooled_lse,
            pooled_mix=pooled_mix,
            second_sum=second_sum,
            ffn_in=ffn_in,
            up_proj=up_proj,
            activated=activated,
            third_sum=third_sum,
        )
        hidden_now = result
        saved_all.append(forward_saved)
    outputs = hidden_now.astype(jnp.bfloat16)
    grad_now = output_grad.astype(jnp.float32)
    grads_list = [None] * layers
    for layer_at in reversed(range(layers)):
        backward_saved = saved_all[layer_at]
        gain_row = norm_gain[layer_at]
        bias_row = norm_shift[layer_at]
        taps = pool_taps[layer_at].reshape(2, 5, heads, HD)
        unused_third, pull_third = jax.vjp(
            layer_norm, backward_saved.third_sum, gain_row[2], bias_row[2]
        )
        grad_third, gain_third, bias_third = pull_third(grad_now)
        grad_down_in = as_rows(grad_third.astype(jnp.bfloat16))
        down_grad = mul_first(backward_saved.activated, grad_down_in)
        grad_act = mul_last(grad_down_in, reduce_weight[layer_at])
        unused_gelu, pull_gelu = jax.vjp(exact_gelu, backward_saved.up_proj)
        grad_up = pull_gelu(grad_act)[0].astype(jnp.bfloat16)
        up_grad = mul_first(as_rows(backward_saved.ffn_in), grad_up)
        grad_second = grad_third + mul_last(grad_up, expand_weight[layer_at]).reshape(
            grad_now.shape
        )
        unused_second, pull_second = jax.vjp(
            layer_norm, backward_saved.second_sum, gain_row[1], bias_row[1]
        )
        grad_mid, gain_second, bias_second = pull_second(grad_second)
        grad_pool_mix = as_rows(grad_mid.astype(jnp.bfloat16))
        out2_grad = mul_first(as_rows(backward_saved.pooled_mix), grad_pool_mix)
        grad_pool_out = (
            mul_last(grad_pool_mix, pooled_mixer[layer_at]).astype(jnp.bfloat16).reshape(head_shape)
        )
        all_pooled = backward_saved.saved_pool
        grad_pool_query, grad_pool_key, grad_pool_value = attend_back(
            backward_saved.pooled_heads[:, :, 0],
            all_pooled[:, :, 0],
            all_pooled[:, :, 1],
            pool_allowed,
            backward_saved.pooled_lse,
            grad_pool_out,
        )
        own_key = lax.psum_scatter(
            grad_pool_key.astype(jnp.bfloat16), "seq", scatter_dimension=1, tiled=True
        ).astype(jnp.float32)
        own_value = lax.psum_scatter(
            grad_pool_value.astype(jnp.bfloat16), "seq", scatter_dimension=1, tiled=True
        ).astype(jnp.float32)
        grad_ext, taps_grad = taps_back(
            backward_saved.extended, taps, jnp.stack([own_key, own_value], 2)
        )
        from_next = from_behind(grad_ext[:, :2].astype(jnp.bfloat16), "seq", -1).astype(jnp.float32)
        grad_kv_second = grad_ext[:, 2:].at[:, tok_here - 2 :].add(from_next)
        grad_heads_two = (
            jnp.concatenate([grad_pool_query[:, :, None], grad_kv_second], 2)
            .astype(jnp.bfloat16)
            .reshape(-1, 3 * width)
        )
        proj2_grad = mul_first(as_rows(backward_saved.second_in), grad_heads_two)
        grad_first = grad_mid + mul_last(grad_heads_two, pooled_proj[layer_at]).reshape(
            grad_now.shape
        )
        unused_first, pull_first = jax.vjp(
            layer_norm, backward_saved.first_sum, gain_row[0], bias_row[0]
        )
        grad_low, gain_first, bias_first = pull_first(grad_first)
        grad_local_mix = as_rows(grad_low.astype(jnp.bfloat16))
        out1_grad = mul_first(as_rows(backward_saved.local_mix), grad_local_mix)
        grad_local_out = (
            mul_last(grad_local_mix, local_mixer[layer_at]).astype(jnp.bfloat16).reshape(head_shape)
        )
        near_kv = backward_saved.near_kv
        grad_local_query, grad_near_key, grad_near_value = attend_back(
            backward_saved.local_heads[:, :, 0],
            near_kv[:, :, 0],
            near_kv[:, :, 1],
            local_allowed,
            backward_saved.local_lse,
            grad_local_out,
        )
        grad_near = jnp.stack([grad_near_key, grad_near_value], 2)
        rim_rows = jnp.concatenate(
            [grad_near[:, :half_win], grad_near[:, tok_here + half_win :]], 1
        )
        came_back = with_halo(rim_rows.astype(jnp.bfloat16), (("seq", 1),), half_win).astype(
            rim_rows.dtype
        )
        grad_kv_first = grad_near[:, half_win : half_win + tok_here]
        grad_kv_first = grad_kv_first.at[:, :half_win].add(came_back[:, :half_win])
        grad_kv_first = grad_kv_first.at[:, tok_here - half_win :].add(came_back[:, 3 * half_win :])
        grad_heads_one = (
            jnp.concatenate([grad_local_query[:, :, None], grad_kv_first], 2)
            .astype(jnp.bfloat16)
            .reshape(-1, 3 * width)
        )
        proj1_grad = mul_first(as_rows(backward_saved.in_rows), grad_heads_one)
        grad_bottom = grad_low + mul_last(grad_heads_one, local_proj[layer_at]).reshape(
            grad_now.shape
        )
        layer_grads = (
            proj1_grad,
            out1_grad,
            proj2_grad[:, :width],
            proj2_grad[:, width:],
            taps_grad.reshape(2, 5, width),
            out2_grad,
            up_grad,
            down_grad,
            jnp.stack([gain_first, gain_second, gain_third]),
            jnp.stack([bias_first, bias_second, bias_third]),
        )
        grad_now, layer_grads = (grad_bottom, layer_grads)
        grads_list[layer_at] = layer_grads
    stacked = [jnp.stack([layer_set[member] for layer_set in grads_list]) for member in range(10)]
    shards_all = (
        lax.psum_scatter(
            stacked[0].astype(jnp.bfloat16), "seq", scatter_dimension=2, tiled=True
        ).astype(jnp.float32),
        lax.psum_scatter(
            stacked[1].astype(jnp.bfloat16), "seq", scatter_dimension=1, tiled=True
        ).astype(jnp.float32),
        lax.psum_scatter(
            stacked[2].astype(jnp.bfloat16), "seq", scatter_dimension=2, tiled=True
        ).astype(jnp.float32),
        lax.psum_scatter(
            stacked[3].astype(jnp.bfloat16), "seq", scatter_dimension=2, tiled=True
        ).astype(jnp.float32),
        lax.psum_scatter(
            stacked[4].astype(jnp.bfloat16), "seq", scatter_dimension=3, tiled=True
        ).astype(jnp.float32),
        lax.psum_scatter(
            stacked[5].astype(jnp.bfloat16), "seq", scatter_dimension=1, tiled=True
        ).astype(jnp.float32),
        lax.psum_scatter(
            stacked[6].astype(jnp.bfloat16), "seq", scatter_dimension=2, tiled=True
        ).astype(jnp.float32),
        lax.psum_scatter(
            stacked[7].astype(jnp.bfloat16), "seq", scatter_dimension=1, tiled=True
        ).astype(jnp.float32),
        lax.psum_scatter(
            stacked[8].astype(jnp.bfloat16), "seq", scatter_dimension=2, tiled=True
        ).astype(jnp.float32),
        lax.psum_scatter(
            stacked[9].astype(jnp.bfloat16), "seq", scatter_dimension=2, tiled=True
        ).astype(jnp.float32),
    )
    stacked = (
        lax.psum(shards_all[0].astype(jnp.bfloat16), "doc").astype(jnp.float32),
        lax.psum(shards_all[1].astype(jnp.bfloat16), "doc").astype(jnp.float32),
        lax.psum(shards_all[2].astype(jnp.bfloat16), "doc").astype(jnp.float32),
        lax.psum(shards_all[3].astype(jnp.bfloat16), "doc").astype(jnp.float32),
        lax.psum(shards_all[4].astype(jnp.bfloat16), "doc").astype(jnp.float32),
        lax.psum(shards_all[5].astype(jnp.bfloat16), "doc").astype(jnp.float32),
        lax.psum(shards_all[6].astype(jnp.bfloat16), "doc").astype(jnp.float32),
        lax.psum(shards_all[7].astype(jnp.bfloat16), "doc").astype(jnp.float32),
        lax.psum(shards_all[8].astype(jnp.bfloat16), "doc").astype(jnp.float32),
        lax.psum(shards_all[9].astype(jnp.bfloat16), "doc").astype(jnp.float32),
    )
    return (
        outputs,
        grad_now,
        stacked[0],
        stacked[1],
        stacked[2],
        stacked[3],
        stacked[4],
        stacked[5],
        stacked[6],
        stacked[7],
        stacked[8],
        stacked[9],
    )


def solution(mesh):
    planes, places = mesh.shape["doc"], mesh.shape["seq"]

    def per_device(inputs, *others):
        docs_here, tok_here, _ = inputs.shape
        whole = docs_here == 4 and 2 * docs_here == places and planes == 4 and tok_here == 128
        return (by_chip if whole else by_sequence)(inputs, *others)

    return jax.shard_map(
        per_device,
        mesh=mesh,
        in_specs=(
            P("doc", "seq", None),
            P("doc"),
            P("doc", None),
            P(),
            P(),
            P(),
            P(),
            P(),
            P(),
            P(),
            P(),
            P(),
            P("doc", "seq", None),
        ),
        out_specs=(
            P("doc", "seq", None),
            P("doc", "seq", None),
            P(None, None, "seq"),
            P(None, "seq", None),
            P(None, None, "seq"),
            P(None, None, "seq"),
            P(None, None, None, "seq"),
            P(None, "seq", None),
            P(None, None, "seq"),
            P(None, "seq", None),
            P(None, None, "seq"),
            P(None, None, "seq"),
        ),
        check_vma=False,
    )
```

```python
from types import SimpleNamespace

import jax
import jax.numpy as jnp
from jax import lax
from jax.experimental import pallas as pl
from jax.experimental.pallas import tpu as pltpu
from jax.sharding import PartitionSpec as P

HD = 64
LOCAL_WIN = 128
POOL_WIN = 512
EPSILON = 1e-05
MASKED = -1e30
F32 = jnp.float32
BF16 = jnp.bfloat16
MESH = pl.DeviceIdType.MESH
ANY = pl.BlockSpec(memory_space=pl.ANY)
VMEM = pl.BlockSpec(memory_space=pltpu.VMEM)
VMEM_LIMIT = 60 * 1024 * 1024


def dot_nn(left, right):
    return jnp.dot(left, right, preferred_element_type=F32)


def dot_nt(left, right):
    return lax.dot_general(left, right, (((1,), (1,)), ((), ())), preferred_element_type=F32)


def dot_tn(left, right):
    return lax.dot_general(left, right, (((0,), (0,)), ((), ())), preferred_element_type=F32)


def loop(count, body):
    def step(i, carry):
        body(i)
        return carry

    lax.fori_loop(0, count, step, 0)


def aligned(index, size):
    return pl.ds(pl.multiple_of(index * size, size), size)


class Copies:
    def __init__(self, sems):
        self.sems = sems
        self.used = 0

    def start(self, source, target):
        copy = pltpu.make_async_copy(source, target, self.sems.at[self.used])
        self.used += 1
        copy.start()
        return copy


class Links:
    def __init__(self, send, recv):
        self.send, self.recv = send, recv
        self.used = 0

    def take(self):
        self.used += 1
        return self.used - 1

    def start(self, source, target, device):
        at = self.take()
        copy = pltpu.make_async_remote_copy(
            src_ref=source,
            dst_ref=target,
            send_sem=self.send.at[at],
            recv_sem=self.recv.at[at],
            device_id=device,
            device_id_type=MESH,
        )
        copy.start()
        return copy


def greet(devices):
    barrier = pltpu.get_barrier_semaphore()
    for device in devices:
        pl.semaphore_signal(barrier, inc=1, device_id=device, device_id_type=MESH)
    pl.semaphore_wait(barrier, len(devices))


class Regroup:
    def __init__(self, copies, links, source, target, gather):
        self.doc, self.me = lax.axis_index("doc"), lax.axis_index("seq")
        self.source, self.target = source, target
        self.gather = gather
        self.copies, self.links = copies, links
        self.local = copies.used
        copies.used += 1
        self.first = links.used
        links.used += 4

    def _to(self, i):
        if self.gather:
            return 2 * i + self.me // 4, self.me % 4
        return 4 * (self.me % 2) + i, self.me // 2

    def _from(self, i):
        if self.gather:
            return 4 * (self.me % 2) + i
        return 2 * i + self.me // 4

    def _remote(self, i, slot, device):
        return pltpu.make_async_remote_copy(
            src_ref=self.source.at[i],
            dst_ref=self.target.at[slot],
            send_sem=self.links.send.at[self.first + i],
            recv_sem=self.links.recv.at[self.first + slot],
            device_id=(self.doc, device),
            device_id_type=MESH,
        )

    def _local(self, i, slot):
        return pltpu.make_async_copy(
            self.source.at[i], self.target.at[slot], self.copies.sems.at[self.local]
        )

    def start(self):
        for i in range(4):
            device, slot = self._to(i)

            @pl.when(device == self.me)
            def _():
                self._local(i, slot).start()

            @pl.when(device != self.me)
            def _():
                self._remote(i, slot, device).start()

    def wait(self):
        for i in range(4):
            device, slot = self._to(i)

            @pl.when(device == self.me)
            def _():
                self._local(i, slot).wait()

            @pl.when(device != self.me)
            def _():
                self._remote(i, slot, device).wait_send()

        for i in range(4):

            @pl.when(self._from(i) != self.me)
            def _():
                self._remote(i, i, self._from(i)).wait_recv()


def regroup_peers():
    me = lax.axis_index("seq")
    return [2 * i + me // 4 for i in range(4)], [4 * (me % 2) + i for i in range(4)]


def greet_regroup(others):
    doc, me = lax.axis_index("doc"), lax.axis_index("seq")
    barrier = pltpu.get_barrier_semaphore()
    to, back = regroup_peers()
    for device in to + back:

        @pl.when(device != me)
        def _():
            pl.semaphore_signal(barrier, inc=1, device_id=(doc, device), device_id_type=MESH)

    for device in others:
        pl.semaphore_signal(barrier, inc=1, device_id=device, device_id_type=MESH)
    inside = me // 4 == me % 2
    pl.semaphore_wait(barrier, len(others) + jnp.where(inside, 6, 8))


def split_masks(width):
    lane = lax.broadcasted_iota(jnp.int32, (1, 2 * HD), 1)
    low = (lane < HD).astype(F32)
    return low, 1.0 - low


def by_head(rows, low, high, factor):
    wide = rows.astype(F32) * factor
    return jnp.concatenate([wide * low, wide * high], 0).astype(BF16)


def from_heads(stacked, low, high):
    rows = stacked.shape[0] // 2
    return stacked[:rows] * low + stacked[rows:] * high


def attend_blocks(queries, key_rows, value_rows, biases):
    low, high = split_masks(2 * HD)
    scores = [
        dot_nt(by_head(query, low, high, HD**-0.5), key) + jnp.concatenate([bias, bias], 0)
        for query, key, bias in zip(queries, key_rows, biases)
    ]
    soft = []
    for score in scores:
        raised = jnp.exp(score - jnp.max(score, -1, keepdims=True))
        soft.append((raised.astype(BF16), 1.0 / jnp.sum(raised, -1, keepdims=True)))
    return [
        from_heads(dot_nn(raised, value) * share, low, high).astype(BF16)
        for (raised, share), value in zip(soft, value_rows)
    ]


def local_bias(at, blocks, length_first, length_last, rows, half):
    shape = (rows, rows + 2 * half)
    query = lax.broadcasted_iota(jnp.int32, shape, 0)
    key = lax.broadcasted_iota(jnp.int32, shape, 1)
    first = jnp.where(length_first & (at == 0), half, 0)
    last = jnp.where(length_last & (at == blocks - 1), rows + half, rows + 2 * half)
    seen = (key >= query) & (key <= query + 2 * half) & (key >= first) & (key < last)
    return jnp.where(seen, 0.0, MASKED).astype(F32)


def norm_rows(summed, gain, shift):
    centre = summed - jnp.mean(summed, -1, keepdims=True)
    spread = jnp.mean(centre * centre, -1, keepdims=True)
    rate = lax.rsqrt(spread + EPSILON)
    plain = centre * rate
    return plain, rate, plain * gain + shift


def gelu_rows(u):
    t = 1.0 / (1.0 + (0.3275911 * 0.5**0.5) * jnp.abs(u))
    series = 0.5307027145 * t - 0.7265760135
    series = series * t + 0.7107068705
    series = series * t - 0.142248368
    series = series * t + 0.127414796
    bell = jnp.exp2((u * u) * -0.7213475204444817)
    tail = series * t * bell
    share = jnp.where(u < 0, tail, 1.0 - tail)
    return u * share, share + (u * 0.3989422804014327) * bell


def vmem(shape, kind=BF16):
    return pltpu.VMEM(shape, kind)


class Scratch:
    def __init__(self):
        self.names, self.shapes = [], []

    def add(self, tag="", **shapes):
        for name, shape in shapes.items():
            self.names.append(tag + name)
            self.shapes.append(shape)

    def plane(self, tag, block):
        first = vmem((2, 2, 4, 2) + block)
        second, total = vmem((2, 2, 4) + block), vmem((2, 4, 2) + block)
        self.add(tag, kept=first, got1=first, got2=second, total=total)

    def line(self, tag, block):
        whole = vmem((2, 2, 2, 2) + block)
        self.add(tag, own=vmem((2, 2) + block), got=vmem((2, 4, 2) + block), whole=whole)

    def core(self, tag, block):
        group = vmem((2, 4, 2, 2, 2) + block)
        self.add(tag, send=group, mine=group, got=group)

    def sems(self, loads, saves, links):
        dma = pltpu.SemaphoreType.DMA
        self.add(load_sems=dma((loads,)), save_sems=dma((saves,)))
        self.add(send_sems=dma((links,)), recv_sems=dma((links,)))

    def bring(self, args, **arrays):
        for name, array in arrays.items():
            args[name] = (array, ANY)
            self.names.append("v_" + name)
            self.shapes.append(pltpu.VMEM(array.shape, array.dtype))


class Kernel:
    def __init__(self, names, refs):
        self.__dict__.update(zip(names, refs))
        assert len(names) == len(refs)
        self.loads = Copies(self.load_sems)
        self.saves = Copies(self.save_sems)
        self.links = Links(self.send_sems, self.recv_sems)
        self.waits = []

    def load(self, source, target):
        return self.loads.start(source, target)

    def load_all(self, names):
        return {name: self.load(getattr(self, name), getattr(self, "v_" + name)) for name in names}

    def save(self, source, target):
        self.waits.append(self.saves.start(source, target))

    def done(self):
        for wait in self.waits:
            wait.wait()


def run_kernel(body, name, collective, args, outs, scratch):
    names = list(args) + list(outs) + scratch.names

    def kernel(*refs):
        k = Kernel(names, refs)
        body(k)
        for used, sems in ((k.loads, k.load_sems), (k.saves, k.save_sems), (k.links, k.send_sems)):
            assert used.used <= sems.shape[0]

    made = pl.pallas_call(
        kernel,
        out_shape=[jax.ShapeDtypeStruct(shape, kind) for shape, kind in outs.values()],
        in_specs=[spec for _, spec in args.values()],
        out_specs=[ANY] * len(outs),
        scratch_shapes=scratch.shapes,
        compiler_params=pltpu.CompilerParams(
            collective_id=collective,
            has_side_effects=collective is not None,
            vmem_limit_bytes=VMEM_LIMIT,
        ),
        name=name,
    )(*(array for array, _ in args.values()))
    return SimpleNamespace(**dict(zip(outs, made)))


def turn(source, target):
    for i in range(0, source.shape[1], 128):
        target[i : i + 128] = source[:, i : i + 128].T


GAIN, SHIFT, TAPS = 0, 3, 6


def small_row(k, layer, row, lane=None, count=None):
    lanes = slice(None) if lane is None else slice(lane, lane + count)
    return k.small[layer, row : row + 1, lanes]


def fill_pooled_bias(k, rows, core):
    doc = lax.axis_index("seq") // 2
    places = k.places[pl.ds(doc, 1)]
    slot = lax.broadcasted_iota(jnp.int32, (128, places.shape[1]), 1)
    column = lax.broadcasted_iota(jnp.int32, (128, rows // 2), 1)
    for i in range(0, rows, 128):
        here = core * rows + i
        position = lax.broadcasted_iota(jnp.int32, (128, places.shape[1]), 0) + here
        hit = (position == places) & (slot < k.counts[doc])
        question = jnp.max(hit.astype(F32), -1, keepdims=True)
        own = (lax.broadcasted_iota(jnp.int32, (128, rows // 2), 0) + here) // 4
        near = jnp.where(jnp.abs(column - own) <= POOL_WIN // 2, 1.0, 0.0)
        bias = jnp.where(near + question > 0.5, 0.0, MASKED).astype(F32)
        k.pbias[i : i + 128] = bias
        k.pbias_t[:, i : i + 128] = bias.T


def forward(k, layer, first, last, rows, width, ff):
    half = LOCAL_WIN // 2
    pool = rows // 4
    blocks = rows // 128
    pairs = width // (2 * HD)
    lanes_of = [slice(2 * HD * pair, 2 * HD * (pair + 1)) for pair in range(pairs)]
    values_of = [slice(width + s.start, width + s.stop) for s in lanes_of]
    core = lax.axis_index("seq") % 2
    sibling = axis_peers()[0]
    links = k.links

    def weight(source, target):
        return k.load(source.at[layer], target)

    got_small = k.load(k.small_in, k.small)
    if not first:
        got_x = k.load(k.x_in, k.xf)
    got = [weight(k.w_local, k.wl)]
    if first:
        greet_regroup([sibling])
        incoming = Regroup(k.loads, links, k.x_in, k.x, True)
        incoming.start()
        background = Regroup(k.loads, links, k.grad_in, k.grad_got, True)
        fill_pooled_bias(k, rows, core)
        k.save(k.pbias, k.o_pbias)
        k.save(k.pbias_t, k.o_pbias_t)
    else:
        greet([sibling])
    for i in range(blocks):
        k.lbias[i] = local_bias(i, blocks, core == 0, core == 1, 128, half)
    k.kvf[:, pl.ds(0, 8)] = jnp.zeros((2 * width // 128, 8, 128), F32)

    if first:
        incoming.wait()
        xrows = k.x.reshape(rows, width)
    else:
        got_x.wait()
        xrows = k.x
        for i in range(0, rows, 128):
            k.x[i : i + 128] = k.xf[i : i + 128].astype(BF16)
    k.save(k.x, k.o_x)
    got += [weight(k.w_mix, k.wm), weight(k.w_pooled, k.wp)]
    if not first:
        got_bias = k.load(k.pbias_in, k.pbias)

    got[0].wait()
    for i in range(0, 2 * width, 256):
        k.kv[half : half + rows, i : i + 256] = dot_nn(
            xrows[...], k.wl[:, width + i : width + i + 256]
        ).astype(BF16)
    rim = links.start(
        k.kv.at[pl.ds(pl.multiple_of(half + (rows - half) * (1 - core), half), half)],
        k.halo,
        sibling,
    )
    for i in range(0, width, 256):
        k.q[:, i : i + 256] = dot_nn(xrows[...], k.wl[:, i : i + 256]).astype(BF16)
    k.save(k.q, k.o_q)
    rim.wait()
    k.kv[pl.ds(pl.multiple_of((rows + half) * (1 - core), half), half)] = k.halo[...]
    k.kv[pl.ds(pl.multiple_of((rows + half) * core, half), half)] = jnp.zeros_like(k.halo)
    k.save(k.kv, k.o_kv)

    def attend_local(i):
        items = [
            (2 * i + j, lanes, values)
            for j in range(2)
            for lanes, values in zip(lanes_of, values_of)
        ]
        seen = [pl.ds(pl.multiple_of(at * 128, 128), 128 + 2 * half) for at, _, _ in items]
        mixed = attend_blocks(
            [k.q[aligned(at, 128), lanes] for at, lanes, _ in items],
            [k.kv[keys, lanes] for keys, (_, lanes, _) in zip(seen, items)],
            [k.kv[keys, values] for keys, (_, _, values) in zip(seen, items)],
            [k.lbias[at] for at, _, _ in items],
        )
        for (at, lanes, _), part in zip(items, mixed):
            k.a[aligned(at, 128), lanes] = part

    loop(blocks // 2, attend_local)
    k.save(k.a, k.o_a)
    got += [weight(k.w_mix2, k.wm2), weight(k.w_up, k.wu), weight(k.w_down, k.wd)]
    if first:
        background.start()
    got_small.wait()

    def mix_norm(at_norm, mixed, weight, residual, plain_ref, rate_ref, full_ref, narrow_ref):
        gain, shift = small_row(k, layer, GAIN + at_norm), small_row(k, layer, SHIFT + at_norm)
        for i in range(0, rows, 128):
            at = slice(i, i + 128)
            update = k.acc[at] if weight is None else dot_nn(mixed[at], weight[...])
            plain, rate, full = norm_rows(residual[at].astype(F32) + update, gain, shift)
            plain_ref[at] = plain.astype(BF16)
            rate_ref[at] = jnp.broadcast_to(rate, (128, 128))
            if full_ref is not None:
                full_ref[at] = full
            if narrow_ref is not None:
                narrow_ref[at] = full.astype(BF16)

    got[1].wait()
    mix_norm(0, k.a, k.wm, xrows if first else k.xf, k.xh, k.rt, k.x1f, k.x1)
    k.save(k.xh, k.o_xh1)
    k.save(k.rt, k.o_r1)
    k.save(k.x1, k.o_x1)

    got[2].wait()
    for i in range(0, 2 * width, 256):
        part = dot_nn(k.x1[...], k.wp[:, width + i : width + i + 256]).astype(BF16)
        k.kv2[:, i : i + 256] = part
        k.kvf[i // 128, 8 : 8 + rows] = part[:, :128].astype(F32)
        k.kvf[i // 128 + 1, 8 : 8 + rows] = part[:, 128:].astype(F32)
    k.save(k.kv2, k.o_kv2)
    for chunk in range(2 * width // 128):
        side, lane = chunk * 128 // width, chunk * 128 % width
        lanes = slice(chunk * 128, chunk * 128 + 128)
        total = jnp.zeros((pool, 128), F32)
        tail = jnp.zeros((1, 128), F32)
        for t in range(5):
            tap = small_row(k, layer, TAPS + 5 * side + t, lane, 128)
            total = total + k.kvf[chunk, pl.ds(6 + t, pool, stride=4)] * tap
            if t < 2:
                tail = tail + k.kvf[chunk, pl.ds(6 + rows + t, 1)] * tap
        k.kp_own[:, lanes] = total.astype(BF16)
        k.aux_own[0:8, lanes] = jnp.broadcast_to(tail, (8, 128))
        k.aux_own[8:16, lanes] = total[:8]
    pooled_out = links.start(k.kp_own, k.kp_got, sibling)
    aux_out = links.start(k.aux_own, k.aux_got, sibling)
    for i in range(0, width, 256):
        k.q2[:, i : i + 256] = dot_nn(k.x1[...], k.wp[:, i : i + 256]).astype(BF16)
    k.save(k.q2, k.o_q2)
    if not first:
        got_bias.wait()
    pooled_out.wait()
    aux_out.wait()
    k.pk[pl.ds(pl.multiple_of(core * pool, pool), pool)] = k.kp_own[...]
    k.pk[pl.ds(pl.multiple_of((1 - core) * pool, pool), pool)] = k.kp_got[...]
    tail = jnp.where(core == 0, k.aux_own[0:1], k.aux_got[0:1])
    head = jnp.where(core == 0, k.aux_got[8:9], k.aux_own[8:9])
    edge = lax.broadcasted_iota(jnp.int32, (16, 1), 0) == 0
    k.pk[pool : pool + 16] = jnp.where(
        edge, jnp.broadcast_to(head + tail, (16, 2 * width)), k.pk[pool : pool + 16].astype(F32)
    ).astype(BF16)
    k.save(k.pk, k.o_pk)

    def attend_pooled(i):
        items = [
            (aligned(2 * i + j, 128), lanes, values)
            for j in range(2)
            for lanes, values in zip(lanes_of, values_of)
        ]
        mixed = attend_blocks(
            [k.q2[here, lanes] for here, lanes, _ in items],
            [k.pk[:, lanes] for _, lanes, _ in items],
            [k.pk[:, values] for _, _, values in items],
            [k.pbias[here] for here, _, _ in items],
        )
        for (here, lanes, _), part in zip(items, mixed):
            k.b[here, lanes] = part

    loop(blocks // 2, attend_pooled)
    k.save(k.b, k.o_b)
    got[3].wait()
    mix_norm(1, k.b, k.wm2, k.x1f, k.xh2, k.rt2, k.x1f, k.x2)
    k.save(k.xh2, k.o_xh2)
    k.save(k.rt2, k.o_r2)
    k.save(k.x2, k.o_x2)

    got[4].wait()
    got[5].wait()
    part, up = 512, (k.up_a, k.up_b)
    count = ff // part

    def expand(i):
        up[i % 2][...] = dot_nn(k.x2[...], k.wu[:, i * part : (i + 1) * part])

    expand(0)
    for i in range(count):
        if i + 1 < count:
            expand(i + 1)
        lanes = slice(i * part, (i + 1) * part)
        full, slope = gelu_rows(up[i % 2][...])
        k.g[:, lanes] = full.astype(BF16)
        k.gp[:, lanes] = slope.astype(BF16)
        k.save(k.g.at[:, lanes], k.o_g.at[:, lanes])
        k.save(k.gp.at[:, lanes], k.o_gp.at[:, lanes])
        product = dot_nn(full.astype(BF16), k.wd[lanes])
        if i == 0:
            k.acc[...] = product
        else:
            k.acc[...] += product
    result = k.out16 if last else k.xf
    mix_norm(
        2, None, None, k.x1f, k.xh3, k.rt3, None if last else result, result if last else None
    )
    k.save(k.xh3, k.o_xh3)
    k.save(k.rt3, k.o_r3)
    k.save(result, k.o_out)
    if first:
        background.wait()
        k.save(k.grad_got, k.o_grad)
    k.done()


def forward_call(layer, first, last, x_in, small, weights, extra):
    width, ff = weights[0].shape[1], weights[4].shape[2]
    rows = x_in.shape[0] * x_in.shape[1] if first else x_in.shape[0]
    half, pool = LOCAL_WIN // 2, rows // 4
    x_shape = (4, rows // 4, width) if first else (rows, width)
    local, mixer, pooled, mixer2, up, down = ((weight, ANY) for weight in weights)
    args = dict(x_in=(x_in, ANY), small_in=(small, ANY), w_local=local, w_mix=mixer)
    args.update(w_pooled=pooled, w_mix2=mixer2, w_up=up, w_down=down)
    wide, kv = ((rows, width), BF16), ((rows + 2 * half, 2 * width), BF16)
    rate, feed, full = ((rows, 128), F32), ((rows, ff), BF16), ((rows, width), F32)
    outs = dict(o_x=(x_shape, BF16), o_q=wide, o_kv=kv, o_a=wide, o_xh1=wide, o_r1=rate)
    outs.update(o_x1=wide, o_q2=wide, o_kv2=((rows, 2 * width), BF16))
    outs.update(o_pk=((2 * pool, 2 * width), BF16), o_b=wide, o_xh2=wide, o_r2=rate)
    outs.update(o_x2=wide, o_g=feed, o_gp=feed, o_xh3=wide, o_r3=rate)
    outs.update(o_out=wide if last else full)
    s = Scratch()
    wl, wm, wp, wm2, wu, wd = (vmem(weight.shape[1:]) for weight in weights)
    s.add(wl=wl, wm=wm, wp=wp, wm2=wm2, wu=wu, wd=wd)
    wide, full, rate, feed = (vmem(*shape) for shape in (wide, full, rate, feed))
    s.add(small=vmem(small.shape, F32), x=vmem(x_shape))
    s.add(q=wide, a=wide, xh=wide, x1=wide, q2=wide, b=wide, xh2=wide, x2=wide, xh3=wide)
    s.add(xf=full, x1f=full, acc=full, rt=rate, rt2=rate, rt3=rate, g=feed, gp=feed)
    part, pooled = vmem((rows, 512), F32), vmem((pool, 2 * width))
    s.add(up_a=part, up_b=part, kv=vmem(*kv), kv2=vmem((rows, 2 * width)))
    s.add(kvf=vmem((2 * width // 128, rows + 16, 128), F32), pk=vmem((2 * pool, 2 * width)))
    aux = vmem((16, 2 * width), F32)
    s.add(halo=vmem((half, 2 * width)), kp_own=pooled, kp_got=pooled, aux_own=aux, aux_got=aux)
    s.add(lbias=vmem((rows // 128, 128, 128 + 2 * half), F32))
    s.add(pbias=vmem((rows, 2 * pool), F32))
    if last:
        s.add(out16=wide)
    if first:
        counts, places, grad_in = extra
        args.update(counts=(counts, pl.BlockSpec(memory_space=pltpu.SMEM)))
        args.update(places=(places, VMEM), grad_in=(grad_in, ANY))
        outs.update(o_grad=(grad_in.shape, BF16))
        outs.update(o_pbias=((rows, 2 * pool), F32), o_pbias_t=((2 * pool, rows), F32))
        s.add(grad_got=vmem(grad_in.shape), pbias_t=vmem((2 * pool, rows), F32))
    else:
        args.update(pbias_in=(extra, ANY))
    s.sems(16, 40, 12)
    return run_kernel(
        lambda k: forward(k, layer, first, last, rows, width, ff),
        "forward_%d" % layer,
        layer,
        args,
        outs,
        s,
    )


def axis_peers():
    doc, me = lax.axis_index("doc"), lax.axis_index("seq")
    core, z = me % 2, me // 2
    along = (z + 1 - 2 * (z % 2), z + 2 - 4 * (z // 2), 3 - z)
    return (
        (doc, me + 1 - 2 * core),
        (doc + 1 - 2 * (doc % 2), me),
        (doc + 2 - 4 * (doc // 2), me),
        [(doc, 2 * other + core) for other in along],
        along,
    )


BOTH = (0, 1)


class CoreSum:
    def __init__(self, k, tag):
        self.links = k.links
        self.send, self.own, self.got = (getattr(k, tag + part) for part in ("send", "mine", "got"))
        self.copy = {}

    def start(self, part):
        self.copy[part] = self.links.start(
            self.send.at[part], self.got.at[part], axis_peers()[0]
        )

    def finish(self, *parts):
        for part in parts or BOTH:
            self.copy[part].wait()

            def add(z):
                self.own[part, z] += self.got[part, z]

            loop(4, add)


class PlaneSum:
    def __init__(self, k, tag, source):
        self.links, self.copies, self.source = k.links, k.loads, source
        self.kept, self.got1, self.got2, self.total = (
            getattr(k, tag + part) for part in ("kept", "got1", "got2", "total")
        )
        doc = lax.axis_index("doc")
        self.x, self.y = doc % 2, doc // 2
        self.copy = {}

    def start(self, *parts):
        _, across, up, _, _ = axis_peers()
        x, y = self.x, self.y
        for part in parts or BOTH:
            source, got = self.source.at[part], self.got1.at[part]
            self.copy[part] = [
                self.links.start(source.at[:, 0, :, 1 - x], got.at[0], across),
                self.links.start(source.at[:, 1, 1 - y], got.at[1], up),
                self.copies.start(source.at[:, 0, :, x], self.kept.at[part, 0]),
                self.copies.start(source.at[:, 1, y], self.kept.at[part, 1]),
            ]

    def middle(self, *parts):
        _, across, up, _, _ = axis_peers()
        for part in parts or BOTH:
            for copy in self.copy[part]:
                copy.wait()

            def add(half):
                self.kept[part, half] += self.got1[part, half]

            loop(2, add)
            kept, got = self.kept.at[part], self.got2.at[part]
            self.copy[part] = [
                self.links.start(kept.at[0, :, 1 - self.y], got.at[0], up),
                self.links.start(kept.at[1, :, 1 - self.x], got.at[1], across),
            ]

    def finish(self, *parts):
        for part in parts or BOTH:
            for copy in self.copy[part]:
                copy.wait()
            for z in range(4):
                self.total[part, z, 0] = self.kept[part, 0, z, self.y] + self.got2[part, 0, z]
                self.total[part, z, 1] = self.kept[part, 1, z, self.x] + self.got2[part, 1, z]


class LineSum:
    def __init__(self, k, tag, source):
        self.links, self.copies, self.source = k.links, k.loads, source
        self.whole = getattr(k, tag + "whole")
        if hasattr(k, tag + "own"):
            self.own, self.got = getattr(k, tag + "own"), getattr(k, tag + "got")
        doc = lax.axis_index("doc")
        self.x, self.y = doc % 2, doc // 2
        self.copy = {}

    def start(self, *parts):
        _, _, _, line, along = axis_peers()
        for part in parts or BOTH:
            source = self.source.at[part]
            self.copy[part] = [
                self.links.start(source.at[other], self.got.at[part, i], device)
                for i, (other, device) in enumerate(zip(along, line))
            ]
            self.copy[part].append(
                self.copies.start(source.at[lax.axis_index("seq") // 2], self.own.at[part])
            )

    def settle(self, *parts):
        for part in parts or BOTH:
            for copy in self.copy[part]:
                copy.wait()
            for half in range(2):
                total = self.own[part, half].astype(F32)
                for i in range(3):
                    total = total + self.got[part, i, half].astype(F32)
                self.whole[part, half, self.y, self.x] = total.astype(BF16)

    def take(self):
        return [
            self.copies.start(self.source.at[part, half], self.whole.at[part, half, self.y, self.x])
            for part in range(2)
            for half in range(2)
        ]

    def give(self, k, target):
        for part in range(2):
            for half in range(2):
                k.save(self.whole.at[part, half, self.y, self.x], target.at[part, half])

    def gather(self, *parts):
        _, across, up, _, _ = axis_peers()
        for part in parts or BOTH:
            first = self.whole.at[part, 0, self.y, self.x]
            second = self.whole.at[part, 1, self.y, self.x]
            self.copy[part] = [
                self.links.start(first, first, across),
                self.links.start(second, second, up),
            ]

    def middle(self, *parts):
        for part in parts or BOTH:
            self.settle(part)
            self.gather(part)

    def spread(self, *parts):
        _, across, up, _, _ = axis_peers()
        for part in parts or BOTH:
            for copy in self.copy[part]:
                copy.wait()
            first = self.whole.at[part, 0, self.y]
            second = self.whole.at[part, 1, :, self.x]
            self.copy[part] = [
                self.links.start(first, first, up),
                self.links.start(second, second, across),
            ]

    def finish(self, *parts):
        for part in parts or BOTH:
            for copy in self.copy[part]:
                copy.wait()


class RelaySum(LineSum):
    def __init__(self, k, tag, source):
        super().__init__(k, tag, source)
        self.doc, me = lax.axis_index("doc"), lax.axis_index("seq")
        self.core, self.z = me % 2, me // 2
        self.near = self.z + 1 - 2 * (self.z % 2)
        self.far = [2 - 2 * (self.z // 2) + i for i in range(2)]
        self.inner = (self.z == 1) | (self.z == 2)
        self.first = {}

    def _send(self, part, source, slot, send, recv, z):
        at = self.first[part]
        return pltpu.make_async_remote_copy(
            src_ref=source,
            dst_ref=self.got.at[part, slot],
            send_sem=self.links.send.at[at + send],
            recv_sem=self.links.recv.at[at + recv],
            device_id=(self.doc, 2 * z + self.core),
            device_id_type=MESH,
        )

    def _beside(self, part):
        return self._send(part, self.source.at[part, self.near], 0, 0, 0, self.near)

    def _past(self, part, i):
        return self._send(part, self.source.at[part, self.far[i]], 2 + i, 1 + i, 1 + i, self.near)

    def _across(self, part, i):
        return self._send(part, self.got.at[part, 2 + i], 1, 3 + i, 3, self.far[i])

    def start(self, *parts):
        for part in parts or BOTH:
            self.first[part] = self.links.used
            self.links.used += 5

            @pl.when(jnp.logical_not(self.inner))
            def _():
                for i in range(2):
                    self._past(part, i).start()

            self._beside(part).start()

    def relay(self, part):
        @pl.when(self.inner)
        def _():
            for i in range(2):
                self._past(part, i).wait_recv()
                self.got[part, 2 + i] += self.source[part, self.far[i]]
                self._across(part, i).start()

    def settle(self, *parts):
        for part in parts or BOTH:
            self._beside(part).wait()
            self._across(part, 0).wait_recv()

            @pl.when(self.inner)
            def _():
                for i in range(2):
                    self._across(part, i).wait_send()

            @pl.when(jnp.logical_not(self.inner))
            def _():
                for i in range(2):
                    self._past(part, i).wait_send()

            for half in range(2):
                total = self.source[part, self.z, half].astype(F32)
                for i in range(2):
                    total = total + self.got[part, i, half].astype(F32)
                self.whole[part, half, self.y, self.x] = total.astype(BF16)


def norm_back(k, rows, incoming, plain_ref, rate_ref, gain, full, narrow, sums, at_sum):
    for i in range(0, rows, 128):
        at = slice(i, i + 128)
        grad = incoming(at)
        plain = plain_ref[at].astype(F32)
        rate = rate_ref[at][:, :1]
        scaled = grad * gain
        even = jnp.mean(scaled, -1, keepdims=True)
        tilt = jnp.mean(scaled * plain, -1, keepdims=True)
        result = rate * (scaled - even - plain * tilt)
        full[at] = result
        narrow[at] = result.astype(BF16)
        for j, part in enumerate((grad * plain, grad)):
            part = jnp.sum(part.reshape(16, 8, -1), 0)
            if i == 0:
                sums[at_sum + j] = part
            else:
                sums[at_sum + j] += part


def attend_back_blocks(queries, key_rows, value_rows, grads_mixed, bias):
    low, high = split_masks(2 * HD)
    wide_bias = jnp.concatenate([bias, bias], 1)
    first = []
    for query, key, value, grad in zip(queries, key_rows, value_rows, grads_mixed):
        stacked, grads = by_head(query, low, high, HD**-0.5), by_head(grad, low, high, 1.0)
        first.append((stacked, grads, dot_nt(key, stacked) + wide_bias, dot_nt(value, grads)))
    second = []
    for _, _, scores, grad_soft in first:
        raised = jnp.exp(scores - jnp.max(scores, 0, keepdims=True))
        soft = raised * (1.0 / jnp.sum(raised, 0, keepdims=True))
        inner = jnp.sum(soft * grad_soft, 0, keepdims=True)
        second.append((soft.astype(BF16), (soft * (grad_soft - inner)).astype(BF16)))
    result = []
    for (stacked, grads, _, _), (soft, grad_scores), key in zip(first, second, key_rows):
        grad_queries = from_heads(dot_tn(grad_scores, key), low, high) * HD**-0.5
        result.append(
            (grad_queries.astype(BF16), dot_nn(grad_scores, stacked), dot_nn(soft, grads))
        )
    return result


def local_bias_turned(at, blocks, length_first, length_last, rows, half):
    shape = (rows + 2 * half, rows)
    key = lax.broadcasted_iota(jnp.int32, shape, 0)
    query = lax.broadcasted_iota(jnp.int32, shape, 1)
    first = jnp.where(length_first & (at == 0), half, 0)
    last = jnp.where(length_last & (at == blocks - 1), rows + half, rows + 2 * half)
    seen = (key >= query) & (key <= query + 2 * half) & (key >= first) & (key < last)
    return jnp.where(seen, 0.0, MASKED).astype(F32)


def place_piece(target, part, z, top, bottom):
    block = target.shape[5:]
    target[part, z, 0] = top[: 4 * block[0]].reshape((2, 2) + block).astype(BF16)
    target[part, z, 1, 0] = top[4 * block[0] :].reshape((2,) + block).astype(BF16)
    target[part, z, 1, 1] = bottom.reshape((2,) + block).astype(BF16)


def whole_piece(target, part, z, value):
    target[part, z] = value.reshape(target.shape[2:]).astype(BF16)


def feed_back(k, layer, rows, width, ff, last):
    core = lax.axis_index("seq") % 2
    sibling, across, up, line_peers, _ = axis_peers()
    shard = ff // 8
    got = k.load_all("dy xh3 r3".split())
    got_small = k.load(k.small_in, k.small)
    if not last:
        greet([sibling, across, up] + line_peers)
        before, line = PlaneSum(k, "x_", k.x_in), LineSum(k, "z_", k.z_in)
        before.start()
        line.start()
    got.update(k.load_all(["g"]))
    for name in ("dy", "xh3", "r3"):
        got[name].wait()
    got_small.wait()
    incoming = k.v_dy.reshape(rows, width) if last else k.v_dy
    norm_back(
        k,
        rows,
        lambda at: incoming[at].astype(F32),
        k.v_xh3,
        k.v_r3,
        small_row(k, layer, GAIN + 2),
        k.res,
        k.dn,
        k.sums,
        0,
    )
    got.update(k.load_all(["gp"]))
    got_down = k.load(k.w_down.at[layer], k.v_down)
    turn(k.dn, k.dn_t)
    got["g"].wait()
    reduced, expanded = CoreSum(k, "r_"), CoreSum(k, "e_")
    middle = width // 2

    def reduce_part(part, which, target):
        rows_of = slice(part * middle, (part + 1) * middle)
        for z in range(4):
            lanes = aligned(2 * z + which, shard)
            whole_piece(target, part, z, dot_nn(k.dn_t[rows_of], k.v_g[:, lanes]))

    def slope_part(first):
        for i in range(first, first + ff // 2, 512):
            k.du[:, i : i + 512] = (
                dot_nt(k.dn[...], k.v_down[i : i + 512]) * k.v_gp[:, i : i + 512].astype(F32)
            ).astype(BF16)

    plane = PlaneSum(k, "r_", k.r_mine)
    reduce_part(0, 1 - core, k.r_send)
    if last:
        greet_regroup([sibling, across, up] + line_peers)
    reduced.start(0)
    if last:
        reduce_part(0, core, k.r_mine)
    reduce_part(1, 1 - core, k.r_send)
    reduced.start(1)
    got.update(k.load_all("x2 xh2 r2".split()))
    got_up = k.load(k.w_up.at[layer], k.v_up)
    if last:
        reduced.finish(0)
        plane.start(0)
        outward = Regroup(k.loads, k.links, k.x3, k.regrouped, False)
        outward.start()
    else:
        reduce_part(0, core, k.r_mine)
    reduce_part(1, core, k.r_mine)
    got["gp"].wait()
    got_down.wait()
    if not last:
        before.middle(0)
    slope_part(0)
    reduced.finish(*((1,) if last else BOTH))
    if not last:
        before.middle(1)
    plane.start(*((1,) if last else BOTH))
    slope_part(ff // 2)
    got["x2"].wait()
    turn(k.v_x2, k.x2_t)

    def expand_part(part, which, target):
        rows_of = slice(part * middle, (part + 1) * middle)
        for z in range(4):
            lanes = aligned(2 * z + which, shard)
            whole_piece(target, part, z, dot_nn(k.x2_t[rows_of], k.du[:, lanes]))

    for part in BOTH:
        expand_part(part, 1 - core, k.e_send)
        expanded.start(part)
    for part in BOTH:
        expand_part(part, core, k.e_mine)
    if not last:
        before.finish()
        late = LineSum(k, "y_", k.x_total)
        late.start()
        line.settle()
        line.give(k, k.o_z)
    else:
        plane.middle(0)
    got_up.wait()
    for i in range(0, width, 256):
        k.res[:, i : i + 256] += dot_nt(k.du[...], k.v_up[i : i + 256])
    got["xh2"].wait()
    got["r2"].wait()
    norm_back(
        k,
        rows,
        lambda at: k.res[at],
        k.v_xh2,
        k.v_r2,
        small_row(k, layer, GAIN + 1),
        k.res,
        k.dn2,
        k.sums,
        2,
    )
    k.save(k.res, k.o_mid)
    k.save(k.dn2, k.o_dy2)
    save_sums(k, 4)
    expanded.finish()
    k.save(k.e_mine, k.o_e)
    plane.middle(*((1,) if last else BOTH))
    if last:
        outward.wait()
        k.save(k.regrouped, k.o_out)
    else:
        late.settle()
        late.give(k, k.o_y)
    plane.finish()
    k.save(k.r_total, k.o_r)
    k.done()


def pooled_back(k, layer, rows, width, last):
    core = lax.axis_index("seq") % 2
    sibling, across, up, line_peers, _ = axis_peers()
    pool = rows // 4
    pairs, blocks = width // (2 * HD), rows // 128
    shard = width // 8
    got = k.load_all(["dy2"])
    got_mix = k.load(k.w_mix2.at[layer], k.v_mix2)
    got_small = k.load(k.small_in, k.small)
    late = [] if last else [LineSum(k, "y_", k.y_in), LineSum(k, "w_", k.w_in)]
    got_late = [copy for each in late for copy in each.take()]
    greet([sibling, across, up] + line_peers)
    plane, line = PlaneSum(k, "x_", k.x_in), LineSum(k, "z_", k.z_in)
    for copy in got_late:
        copy.wait()
    for each in late:
        each.gather()
    plane.start()
    line.start()
    got.update(k.load_all("q2 pk".split()))
    got_bias = k.load(k.pbias, k.v_pbias)
    got["dy2"].wait()
    got_mix.wait()
    got.update(k.load_all("kv2 b".split()))
    for i in range(0, width, 256):
        k.do[:, i : i + 256] = dot_nt(k.v_dy2[...], k.v_mix2[i : i + 256]).astype(BF16)
    for name in ("q2", "pk"):
        got[name].wait()
    k.dkv[...] = jnp.zeros_like(k.dkv)
    got_bias.wait()
    got.update(k.load_all("x1 mid xh1 r1".split()))
    got_proj = k.load(k.w_pooled.at[layer], k.v_pooled)
    lanes_of = [slice(2 * HD * pair, 2 * HD * (pair + 1)) for pair in range(pairs)]
    values_of = [slice(width + part.start, width + part.stop) for part in lanes_of]

    def attend_part(i):
        here = aligned(i, 128)
        parts = attend_back_blocks(
            [k.v_q2[here, lanes] for lanes in lanes_of],
            [k.v_pk[:, lanes] for lanes in lanes_of],
            [k.v_pk[:, lanes] for lanes in values_of],
            [k.do[here, lanes] for lanes in lanes_of],
            k.v_pbias[:, here],
        )
        for lanes, values, (grad_q, grad_k, grad_v) in zip(lanes_of, values_of, parts):
            k.dqkv[here, lanes] = grad_q
            k.dkv[:, lanes] += grad_k
            k.dkv[:, values] += grad_v

    loop(blocks, attend_part)
    k.rim_out[...] = k.dkv[pl.ds(pl.multiple_of((pool - 16) * (1 - core), 16), pool + 16)].astype(
        BF16
    )
    rim = k.links.start(k.rim_out, k.rim_got, sibling)
    got["b"].wait()
    turn(k.v_b, k.b_t)
    got["kv2"].wait()
    for c in range(2 * width // 128):
        k.kvf[c, :rows] = k.v_kv2[:, pl.ds(c * 128, 128)].astype(F32)
    got_small.wait()
    rim.wait()
    k.total[pl.ds(0, pool)] = (
        k.dkv[pl.ds(pl.multiple_of(core * pool, pool), pool)]
        + k.rim_got[pl.ds(pl.multiple_of(core * 16, 16), pool)].astype(F32)
    )
    k.total[pl.ds(pool, 8)] = jnp.where(
        core == 0, k.dkv[pl.ds(pool, 8)] + k.rim_got[pl.ds(pool, 16)].astype(F32)[:8], 0.0
    )

    for c in range(2 * width // 128):
        side, lane = c * 128 // width, c * 128 % width
        lanes = pl.ds(c * 128, 128)
        own, after = k.total[pl.ds(0, pool), lanes], k.total[pl.ds(1, pool), lanes]
        rows_at = [pl.ds(j, pool, stride=4) for j in range(4)]
        kept = [k.kvf[c, at] for at in rows_at]
        taps = [small_row(k, layer, TAPS + 5 * side + t, lane, 128) for t in range(5)]
        pairs_of = ((kept[2], after), (kept[3], after), (kept[0], own), (kept[1], own), (kept[2], own))
        for t, (token, grad) in enumerate(pairs_of):
            k.tap_sums[side, 8 * t : 8 * t + 8, lane : lane + 128] = jnp.sum(
                (token * grad).reshape(pool // 8, 8, 128), 0
            )
        k.kvf[c, rows_at[0]] = own * taps[2]
        k.kvf[c, rows_at[1]] = own * taps[3]
        k.kvf[c, rows_at[2]] = own * taps[4] + after * taps[0]
        k.kvf[c, rows_at[3]] = after * taps[1]
        k.dqkv[:, pl.ds(width + c * 128, 128)] = k.kvf[c, :rows].astype(BF16)
    turn(k.dqkv, k.dqkv_t)
    got["x1"].wait()
    for each in late:
        each.spread()
    line.settle()
    if last:
        line.gather()
    else:
        line.give(k, k.o_z)
    plane.middle()
    summed = CoreSum(k, "p_")
    middle = width // 2

    def grad_part(part, which, target):
        lanes = slice(part * middle, (part + 1) * middle)
        mixers = jnp.concatenate(
            [k.b_t[aligned(2 * z + which, shard)] for z in range(4)], 0
        )
        k.mixed[...] = dot_nn(mixers, k.v_dy2[:, lanes])

        for z in range(4):
            at = 2 * z + which
            mine = jnp.concatenate(
                [
                    k.dqkv_t[aligned(at, shard)],
                    k.dqkv_t[pl.ds(pl.multiple_of(width + at * 2 * shard, 2 * shard), 2 * shard)],
                ],
                0,
            )
            place_piece(
                target, part, z, dot_nn(mine, k.v_x1[:, lanes]), k.mixed[z * shard : (z + 1) * shard]
            )

    for part in BOTH:
        grad_part(part, 1 - core, k.p_send)
        summed.start(part)
    for part in BOTH:
        grad_part(part, core, k.p_mine)
    got["mid"].wait()
    got_proj.wait()

    for i in range(0, width, 256):
        k.v_mid[:, i : i + 256] += dot_nt(k.dqkv[...], k.v_pooled[i : i + 256])
    got["xh1"].wait()
    got["r1"].wait()
    norm_back(
        k,
        rows,
        lambda at: k.v_mid[at],
        k.v_xh1,
        k.v_r1,
        small_row(k, layer, GAIN),
        k.v_mid,
        k.dn,
        k.sums,
        0,
    )
    k.save(k.v_mid, k.o_low)
    k.save(k.dn, k.o_dy1)
    save_sums(k, 2, k.tap_sums)
    if last:
        line.spread()
    plane.finish()
    k.save(k.x_total, k.o_x)
    summed.finish()
    k.save(k.p_mine, k.o_p)
    if last:
        line.finish()
        k.save(k.z_whole, k.o_z)
    else:
        for each, target in zip(late, (k.o_y, k.o_w)):
            each.finish()
            k.save(each.whole, target)
    k.done()


def local_back(k, layer, rows, width, final):
    core = lax.axis_index("seq") % 2
    sibling, across, up, line_peers, _ = axis_peers()
    half = LOCAL_WIN // 2
    pairs, blocks = width // (2 * HD), rows // 128
    shard = width // 8
    got = k.load_all(["dy1"])
    got_mix = k.load(k.w_mix.at[layer], k.v_mix)
    got.update(k.load_all("q kv".split()))
    if final:
        greet_regroup([sibling, across, up] + line_peers)
    else:
        greet([sibling, across, up] + line_peers)
    plane, line = PlaneSum(k, "x_", k.x_in), LineSum(k, "z_", k.z_in)
    plane.start()
    line.start()
    if final:
        small = SmallSum(k)
        small.load()
        early = LineSum(k, "r_", k.r_in)
        got_early = early.take()
    for i in range(blocks):
        k.lbias[i] = local_bias_turned(i, blocks, core == 0, core == 1, 128, half)
    got["dy1"].wait()
    got_mix.wait()
    for i in range(0, width, 256):
        k.do[:, i : i + 256] = dot_nt(k.v_dy1[...], k.v_mix[i : i + 256]).astype(BF16)
    got.update(k.load_all("a x low".split()))
    got_proj = k.load(k.w_local.at[layer], k.v_local)
    for name in ("q", "kv"):
        got[name].wait()
    if final:
        small.step()
    k.dkv[...] = jnp.zeros_like(k.dkv)
    lanes_of = [slice(2 * HD * pair, 2 * HD * (pair + 1)) for pair in range(pairs)]
    values_of = [slice(width + part.start, width + part.stop) for part in lanes_of]

    def attend_part(i):
        here, seen = aligned(i, 128), pl.ds(pl.multiple_of(i * 128, 128), 128 + 2 * half)
        parts = attend_back_blocks(
            [k.v_q[here, lanes] for lanes in lanes_of],
            [k.v_kv[seen, lanes] for lanes in lanes_of],
            [k.v_kv[seen, lanes] for lanes in values_of],
            [k.do[here, lanes] for lanes in lanes_of],
            k.lbias[i],
        )
        for lanes, values, (grad_q, grad_k, grad_v) in zip(lanes_of, values_of, parts):
            k.dqkv[here, lanes] = grad_q
            k.dkv[seen, lanes] += grad_k
            k.dkv[seen, values] += grad_v

    loop(blocks, attend_part)
    k.rim_out[...] = k.dkv[pl.ds(pl.multiple_of((rows + half) * (1 - core), half), half)].astype(
        BF16
    )
    rim = k.links.start(k.rim_out, k.rim_got, sibling)
    got["a"].wait()
    turn(k.v_a, k.a_t)
    rim.wait()
    edge = pl.ds(pl.multiple_of(half + (rows - half) * (1 - core), half), half)
    k.dkv[edge] += k.rim_got[...].astype(F32)
    k.dqkv[:, width:] = k.dkv[half : half + rows].astype(BF16)
    turn(k.dqkv, k.dqkv_t)
    got["x"].wait()
    inputs = k.v_x.reshape(rows, width) if len(k.v_x.shape) == 3 else k.v_x
    summed = CoreSum(k, "l_")
    middle = width // 2

    def grad_part(part, which, target):
        lanes = slice(part * middle, (part + 1) * middle)
        mixers = jnp.concatenate(
            [k.a_t[aligned(2 * z + which, shard)] for z in range(4)], 0
        )
        k.mixed[...] = dot_nn(mixers, k.v_dy1[:, lanes])
        for z in range(4):
            mine = k.dqkv_t[aligned(2 * z + which, 3 * shard)]
            place_piece(
                target, part, z, dot_nn(mine, inputs[:, lanes]), k.mixed[z * shard : (z + 1) * shard]
            )

    def residual():
        got["low"].wait()
        got_proj.wait()
        for i in range(0, width, 256):
            k.v_low[:, i : i + 256] += dot_nt(k.dqkv[...], k.v_local[i : i + 256])

    if not final:
        line.middle()
        plane.middle()
        for part in BOTH:
            grad_part(part, 1 - core, k.l_send)
            summed.start(part)
        for part in BOTH:
            grad_part(part, core, k.l_mine)
        residual()
        k.save(k.v_low, k.o_dx)
        line.spread()
        plane.finish()
        k.save(k.x_total, k.o_x)
        summed.finish()
        k.save(k.l_mine, k.o_l)
        line.finish()
        k.save(k.z_whole, k.o_z)
        k.done()
        return
    small.step()
    residual()
    for i in range(0, rows, 128):
        k.narrow[i // 128] = k.v_low[i : i + 128].astype(BF16)
    outward = Regroup(k.loads, k.links, k.narrow, k.regrouped, False)
    outward.start()
    plane.middle()
    line.settle()
    for part in BOTH:
        grad_part(part, 1 - core, k.l_send)
        summed.start(part)
    small.step()
    last_plane, last_line = PlaneSum(k, "l_", k.l_mine), RelaySum(k, "f_", k.l_total)
    for part in BOTH:
        grad_part(part, core, k.l_mine)
    for part in BOTH:
        summed.finish(part)
        last_plane.start(part)
    plane.finish()
    before = RelaySum(k, "p_", k.x_total)
    before.start()
    small.step()
    last_plane.middle(0)
    for copy in got_early:
        copy.wait()
    last_plane.middle(1)
    before.relay(0)
    before.relay(1)
    line.gather()
    early.gather()
    for part in BOTH:
        last_plane.finish(part)
        last_line.start(part)
    before.settle()
    line.spread()
    early.spread()
    last_line.relay(0)
    before.gather()
    last_line.relay(1)
    small.finish()
    for each, target in ((line, k.o_z), (early, k.o_r)):
        each.finish()
        k.save(each.whole, target)
    before.spread()
    outward.wait()
    k.save(k.regrouped, k.o_dx)
    last_line.middle(0)
    before.finish()
    k.save(k.p_whole, k.o_p)
    last_line.middle(1)
    last_line.spread(0)
    last_line.spread(1)
    last_line.finish()
    k.save(k.f_whole, k.o_f)
    k.done()


class SmallSum:
    def __init__(self, k):
        self.k = k
        sibling, across, up, self.line, self.along = axis_peers()
        self.order = [sibling, across, up]
        self.at = 0

    def load(self):
        k = self.k
        self.copies = []
        for i, (feed, pooled) in enumerate(zip(k.s_feed, k.s_pool)):
            self.copies.append(k.load(feed, k.s_sum.at[24 * i : 24 * i + 8]))
            self.copies.append(k.load(pooled, k.s_sum.at[24 * i + 8 : 24 * i + 24]))

    def window(self, z):
        return pl.ds(pl.multiple_of(3 * z // 2 * 128, 128), 256)

    def step(self):
        k = self.k
        for copy in self.copies:
            copy.wait()
        if self.at > 0:
            k.s_sum[...] += k.s_got[self.at - 1].astype(F32)
        k.s_out[...] = k.s_sum[...].astype(BF16)
        if self.at < len(self.order):
            self.copies = [k.links.start(k.s_out, k.s_got.at[self.at], self.order[self.at])]
        else:
            self.copies = [
                k.links.start(k.s_out.at[:, self.window(z)], k.s_line.at[i], device)
                for i, (z, device) in enumerate(zip(self.along, self.line))
            ]
        self.at += 1

    def finish(self):
        k = self.k
        for copy in self.copies:
            copy.wait()
        mine = self.window(lax.axis_index("seq") // 2)
        total = k.s_sum[:, mine]
        for i in range(3):
            total = total + k.s_line[i].astype(F32)
        k.s_sum[:, mine] = total
        k.save(k.s_sum, k.o_small)


def save_sums(k, count, taps=None):
    for i in range(count):
        k.row_sums[i : i + 1] = jnp.sum(k.sums[i], 0, keepdims=True)
    at = count
    if taps is not None:
        for side in range(2):
            for t in range(5):
                k.row_sums[at : at + 1] = jnp.sum(
                    taps[side, 8 * t : 8 * t + 8], 0, keepdims=True
                )
                at += 1
    k.row_sums[at:] = jnp.zeros((k.row_sums.shape[0] - at, k.row_sums.shape[1]), F32)
    k.save(k.row_sums, k.o_sums)


def block_of(width):
    return (width // 16, width // 2)


def group_shape(block):
    return (2, 4, 2, 2, 2) + block


def total_shape(block):
    return (2, 4, 2) + block


def whole_shape(block):
    return (2, 2, 2, 2) + block


def feed_back_call(layer, last, dy, small, kept, w_down, w_up, x_in, z_in, outputs):
    rows, width = kept.o_xh3.shape
    ff = kept.o_g.shape[1]
    block = block_of(width)
    full, wide = (rows, width), vmem((rows, width))
    s = Scratch()
    args = dict(small_in=(small, ANY), w_down=(w_down, ANY), w_up=(w_up, ANY))
    s.bring(args, dy=dy, xh3=kept.o_xh3, r3=kept.o_r3, g=kept.o_g, gp=kept.o_gp)
    s.bring(args, x2=kept.o_x2, xh2=kept.o_xh2, r2=kept.o_r2)
    outs = dict(o_mid=(full, F32), o_dy2=(full, BF16), o_sums=((8, width), F32))
    outs.update(o_r=(total_shape(block), BF16), o_e=(group_shape(block), BF16))
    s.add(small=vmem(small.shape, F32), sums=vmem((4, 8, width), F32))
    s.add(v_down=vmem(w_down.shape[1:]), v_up=vmem(w_up.shape[1:]))
    s.add(row_sums=vmem((8, width), F32), res=vmem(full, F32), dn=wide, dn2=wide)
    s.add(dn_t=vmem((width, rows)), x2_t=vmem((width, rows)), du=vmem((rows, ff)))
    s.core("r_", block)
    s.core("e_", block)
    s.plane("r_", block)
    if last:
        by_doc = (4, rows // 4, width)
        args.update(x3=(outputs.reshape(by_doc), ANY))
        outs.update(o_out=(by_doc, BF16))
        s.add(regrouped=vmem(by_doc))
    else:
        args.update(x_in=(x_in, ANY), z_in=(z_in, ANY))
        outs.update(o_y=((2, 2) + block, BF16), o_z=((2, 2) + block, BF16))
        s.plane("x_", block)
        s.line("y_", block)
        s.line("z_", block)
    s.sems(40, 16, 48)
    return run_kernel(
        lambda k: feed_back(k, layer, rows, width, ff, last),
        "feed_back_%d" % layer,
        2 + layer,
        args,
        outs,
        s,
    )


def pooled_back_call(
    layer, last, mid, dy2, small, pbias, kept, w_mix2, w_pooled, x_in, z_in, y_in, w_in
):
    rows, width = mid.shape
    pool = rows // 4
    block = block_of(width)
    full, wide = (rows, width), vmem((rows, width))
    s = Scratch()
    args = dict(small_in=(small, ANY), w_mix2=(w_mix2, ANY), w_pooled=(w_pooled, ANY))
    args.update(x_in=(x_in, ANY), z_in=(z_in, ANY))
    s.bring(args, mid=mid, dy2=dy2, b=kept.o_b, q2=kept.o_q2, kv2=kept.o_kv2, pk=kept.o_pk)
    s.bring(args, x1=kept.o_x1, xh1=kept.o_xh1, r1=kept.o_r1, pbias=pbias)
    outs = dict(o_low=(full, F32), o_dy1=(full, BF16), o_sums=((16, width), F32))
    outs.update(o_p=(group_shape(block), BF16), o_x=(total_shape(block), BF16))
    outs.update(o_z=(whole_shape(block) if last else (2, 2) + block, BF16))
    s.add(small=vmem(small.shape, F32), v_mix2=vmem(w_mix2.shape[1:]))
    s.add(v_pooled=vmem(w_pooled.shape[1:]), sums=vmem((2, 8, width), F32))
    s.add(row_sums=vmem((16, width), F32), tap_sums=vmem((2, 40, width), F32), do=wide, dn=wide)
    rim, turned = vmem((pool + 16, 2 * width)), vmem((width, rows))
    s.add(dkv=vmem((2 * pool, 2 * width), F32), rim_out=rim, rim_got=rim)
    s.add(total=vmem((pool + 8, 2 * width), F32), kvf=vmem((2 * width // 128, rows + 8, 128), F32))
    s.add(dqkv=vmem((rows, 3 * width)), dqkv_t=vmem((3 * width, rows)), b_t=turned)
    s.add(mixed=vmem((width // 2, width // 2), F32))
    s.core("p_", block)
    s.plane("x_", block)
    s.line("z_", block)
    if not last:
        args.update(y_in=(y_in, ANY), w_in=(w_in, ANY))
        whole = whole_shape(block)
        outs.update(o_y=(whole, BF16), o_w=(whole, BF16))
        s.add(y_whole=vmem(whole), w_whole=vmem(whole))
    s.sems(40, 16, 48)
    return run_kernel(
        lambda k: pooled_back(k, layer, rows, width, last),
        "pooled_back_%d" % layer,
        4 + layer,
        args,
        outs,
        s,
    )


def local_back_call(layer, final, low, dy1, kept, w_mix, w_local, x_in, z_in, r_in, sums):
    rows, width = low.shape
    half = LOCAL_WIN // 2
    block = block_of(width)
    s = Scratch()
    args = dict(w_mix=(w_mix, ANY), w_local=(w_local, ANY), x_in=(x_in, ANY), z_in=(z_in, ANY))
    s.bring(args, low=low, dy1=dy1, a=kept.o_a, q=kept.o_q, kv=kept.o_kv, x=kept.o_x)
    outs = dict(o_z=(whole_shape(block), BF16))
    by_doc, total = (4, rows // 4, width), (len(sums) * 24, width)
    if final:
        whole = (whole_shape(block), BF16)
        for i, (feed, pooled) in enumerate(sums):
            args["s_feed%d" % i], args["s_pool%d" % i] = (feed, ANY), (pooled, ANY)
        args.update(r_in=(r_in, ANY))
        outs.update(o_dx=(by_doc, BF16), o_p=whole, o_f=whole, o_r=whole, o_small=(total, F32))
        s.add(r_whole=vmem(whole_shape(block)))
    else:
        outs.update(o_dx=((rows, width), F32), o_l=(group_shape(block), BF16))
        outs.update(o_x=(total_shape(block), BF16))
    s.add(v_mix=vmem(w_mix.shape[1:]), v_local=vmem(w_local.shape[1:]))
    s.add(lbias=vmem((rows // 128, 128 + 2 * half, 128), F32), do=vmem((rows, width)))
    s.add(dkv=vmem((rows + 2 * half, 2 * width), F32))
    s.add(rim_out=vmem((half, 2 * width)), rim_got=vmem((half, 2 * width)))
    s.add(dqkv=vmem((rows, 3 * width)), dqkv_t=vmem((3 * width, rows)))
    s.add(a_t=vmem((width, rows)), mixed=vmem((width // 2, width // 2), F32))
    s.core("l_", block)
    s.plane("x_", block)
    s.line("z_", block)
    if final:
        s.add(narrow=vmem(by_doc), regrouped=vmem(by_doc))
        s.add(s_sum=vmem(total, F32), s_out=vmem(total), s_got=vmem((3,) + total))
        s.add(s_line=vmem((3, len(sums) * 24, 256)))
        s.plane("l_", block)
        s.line("p_", block)
        s.line("f_", block)
    s.sems(48, 16, 96)

    def body(k):
        if final:
            k.s_feed = [getattr(k, "s_feed%d" % i) for i in range(len(sums))]
            k.s_pool = [getattr(k, "s_pool%d" % i) for i in range(len(sums))]
        local_back(k, layer, rows, width, final)

    return run_kernel(
        body,
        "local_back_%d" % layer,
        6 + layer,
        args,
        outs,
        s,
    )


def by_chip(
    inputs,
    question_count,
    question_at,
    local_proj,
    local_mixer,
    pooled_proj,
    pool_taps,
    pooled_mixer,
    expand_weight,
    reduce_weight,
    norm_gain,
    norm_shift,
    output_grad,
):
    docs_here, tok_here, width = inputs.shape
    layers, ff = local_proj.shape[0], expand_weight.shape[2]
    small = jnp.concatenate([norm_gain, norm_shift, pool_taps.reshape(layers, 10, width)], 1)
    weights = (local_proj, local_mixer, pooled_proj, pooled_mixer, expand_weight, reduce_weight)
    hidden, kept, bias = inputs, [], None
    for layer in range(layers):
        first, last = layer == 0, layer == layers - 1
        extra = (question_count, question_at, output_grad) if first else bias
        made = forward_call(layer, first, last, hidden, small, weights, extra)
        if first:
            grad, bias, bias_t = made.o_grad, made.o_pbias, made.o_pbias_t
        kept.append(made)
        hidden = made.o_out
    x_in = z_in = None
    reduced, expanded, pooled_sums, local_sums, sums = {}, {}, {}, {}, []
    for layer in reversed(range(layers)):
        last = layer == layers - 1
        saved = kept[layer]
        fed = feed_back_call(
            layer, last, grad, small, saved, reduce_weight, expand_weight, x_in, z_in, hidden
        )
        if last:
            outputs = fed.o_out
        pooled = pooled_back_call(
            layer,
            last,
            fed.o_mid,
            fed.o_dy2,
            small,
            bias_t,
            saved,
            pooled_mixer,
            pooled_proj,
            fed.o_e,
            fed.o_r,
            None if last else fed.o_y,
            None if last else fed.o_z,
        )
        if not last:
            local_sums[layer + 1], pooled_sums[layer + 1] = pooled.o_y, pooled.o_w
        sums.insert(0, (fed.o_sums, pooled.o_sums))
        local = local_back_call(
            layer,
            layer == 0,
            pooled.o_low,
            pooled.o_dy1,
            saved,
            local_mixer,
            local_proj,
            pooled.o_p,
            pooled.o_x,
            None if last else pooled.o_z,
            sums,
        )
        reduced[layer] = pooled.o_z if last else local.o_r
        expanded[layer] = local.o_z
        if layer > 0:
            grad, x_in, z_in = local.o_dx, local.o_l, local.o_x
    pooled_sums[0], local_sums[0] = local.o_p, local.o_f
    groups = [[group[i] for i in range(layers)] for group in (reduced, expanded, local_sums, pooled_sums)]
    return finish_call(outputs, local.o_dx, local.o_small, groups, layers, width, ff)


def finish(k, layers, width, ff):
    part, feed = width // 8, ff // 8
    me = lax.axis_index("seq")
    order = list(reversed(range(layers)))
    names = ["g%d" % i for i in range(4 * layers)]
    got = [k.load(getattr(k, name), getattr(k, "v_" + name)) for name in names]
    got_dx, got_small = k.load(k.dx, k.v_dx), k.load(k.small_sum, k.v_small_sum)
    got_out = k.load(k.outputs, k.v_outputs)

    def whole(group, layer, axis):
        got[group * layers + layer].wait()
        block = getattr(k, "v_" + names[group * layers + layer])
        parts = [block[i].reshape(-1, block.shape[-1]).astype(F32) for i in BOTH]
        return jnp.concatenate(parts, axis)

    def put(layer, source, target, value):
        source[layer] = value
        k.save(source.at[layer], target.at[layer])

    for layer in order:
        put(layer, k.v_down, k.o_down, whole(0, layer, 0).T)
        put(layer, k.v_up, k.o_up, whole(1, layer, 0))
    got_out.wait()
    k.save(k.v_outputs, k.o_outputs)
    got_dx.wait()
    for i in range(4):
        k.v_dx32[i] = k.v_dx[i].astype(F32)
    k.save(k.v_dx32, k.o_dx)
    for layer in order:
        local = whole(2, layer, 1)
        put(layer, k.v_local, k.o_local, local[: 3 * part])
        put(layer, k.v_mix, k.o_mix, local[3 * part :])
        pooled = whole(3, layer, 1)
        put(layer, k.v_query, k.o_query, pooled[:part])
        put(layer, k.v_kv, k.o_kv, pooled[part : 3 * part])
        put(layer, k.v_mix2, k.o_mix2, pooled[3 * part :])
    got_small.wait()
    small = k.v_small_sum[...]
    mine = jnp.zeros((small.shape[0], part), F32)
    for i in range(8):
        mine = jnp.where(me == i, small[:, i * part : (i + 1) * part], mine)
    for layer in range(layers):
        rows = mine[24 * layer : 24 * layer + 24]
        for i, (gain, shift) in enumerate(((8, 9), (2, 3), (0, 1))):
            k.v_gain[i, layer : layer + 1] = rows[gain : gain + 1]
            k.v_shift[i, layer : layer + 1] = rows[shift : shift + 1]
        for side in range(2):
            for t in range(5):
                at = 10 + 5 * side + t
                k.v_taps[layer, t, side : side + 1] = rows[at : at + 1]
    k.save(k.v_gain, k.o_gain)
    k.save(k.v_shift, k.o_shift)
    k.save(k.v_taps, k.o_taps)
    k.done()


def finish_call(outputs, dx, small_sum, groups, layers, width, ff):
    part, feed = width // 8, ff // 8
    args = {}
    s = Scratch()
    s.bring(args, outputs=outputs, dx=dx, small_sum=small_sum)
    s.add(v_dx32=vmem(dx.shape, F32))
    for i, array in enumerate(array for group in groups for array in group):
        s.bring(args, **{"g%d" % i: array})
    mixer, few = (layers, part, width), (3, layers, part)
    shapes = dict(local=(layers, 3 * part, width), mix=mixer, query=mixer)
    shapes.update(kv=(layers, 2 * part, width), taps=(layers, 5, 2, part), mix2=mixer)
    shapes.update(up=(layers, width, feed), down=(layers, feed, width), gain=few, shift=few)
    outs = dict(o_outputs=(outputs.shape, BF16), o_dx=(dx.shape, F32))
    for name, shape in shapes.items():
        outs["o_" + name] = (shape, F32)
        s.add("v_", **{name: vmem(shape, F32)})
    s.sems(16, 32, 1)
    made = run_kernel(lambda k: finish(k, layers, width, ff), "finish", None, args, outs, s)
    made.o_local, made.o_query, made.o_kv = (
        jnp.swapaxes(array, 1, 2) for array in (made.o_local, made.o_query, made.o_kv)
    )
    made.o_taps = jnp.swapaxes(made.o_taps, 1, 2)
    made.o_gain, made.o_shift = jnp.swapaxes(made.o_gain, 0, 1), jnp.swapaxes(made.o_shift, 0, 1)
    return tuple(vars(made).values())


def with_halo(array, sides, width):
    for axis, dim in sides:
        peers, length = (lax.axis_size(axis), array.shape[dim])
        up = [(i, (i + 1) % peers) for i in range(peers - 1)]
        down = [(j, i) for i, j in up]
        last = lax.slice_in_dim(array, length - width, length, axis=dim)
        first = lax.slice_in_dim(array, 0, width, axis=dim)
        before = lax.ppermute(last, axis, up)
        after = lax.ppermute(first, axis, down)
        array = jnp.concatenate([before, array, after], axis=dim)
    return array


def from_behind(value, axis, steps):
    count = lax.axis_size(axis)
    first, last = (max(0, -steps), min(count, count - steps))
    return lax.ppermute(value, axis, [(source, source + steps) for source in range(first, last)])


def layer_norm(summed, gain, shift_bias):
    centre = summed - jnp.mean(summed, -1, keepdims=True)
    spread = jnp.mean(centre * centre, -1, keepdims=True)
    return centre * lax.rsqrt(spread + EPSILON) * gain + shift_bias


def exact_gelu(value):
    return jax.nn.gelu(value, approximate=False)


def mul_plain(left_rows, right_mat):
    return jnp.dot(left_rows, right_mat, preferred_element_type=jnp.float32)


def mul_last(left_rows, right_mat):
    return lax.dot_general(
        left_rows, right_mat, (((1,), (1,)), ((), ())), preferred_element_type=jnp.float32
    )


def mul_first(left_rows, right_rows):
    return lax.dot_general(
        left_rows, right_rows, (((0,), (0,)), ((), ())), preferred_element_type=jnp.float32
    )


def as_rows(array_in):
    return array_in.reshape(-1, array_in.shape[-1])


def masked_scores(queries, key_rows, allowed):
    factor = queries.shape[-1] ** (-0.5)
    scores = (
        jnp.einsum("nqhe,nkhe->nhqk", queries, key_rows, preferred_element_type=jnp.float32)
        * factor
    )
    return (jnp.where(allowed[:, None], scores, MASKED), factor)


def attend(queries, key_rows, value_rows, allowed):
    scores, factor = masked_scores(queries, key_rows, allowed)
    row_top = jnp.max(scores, -1, keepdims=True)
    raised = jnp.exp(scores - row_top)
    row_total = jnp.sum(raised, -1, keepdims=True)
    soft_weights = (raised / row_total).astype(jnp.bfloat16)
    mixed = jnp.einsum(
        "nhqk,nkhe->nqhe", soft_weights, value_rows, preferred_element_type=jnp.float32
    )
    return (mixed, row_top + jnp.log(row_total))


def attend_back(queries, key_rows, value_rows, allowed, log_total, grad_mixed):
    scores, factor = masked_scores(queries, key_rows, allowed)
    soft_full = jnp.exp(scores - log_total)
    soft_weights = soft_full.astype(jnp.bfloat16)
    grad_values = jnp.einsum(
        "nhqk,nqhe->nkhe", soft_weights, grad_mixed, preferred_element_type=jnp.float32
    )
    grad_soft = jnp.einsum(
        "nqhe,nkhe->nhqk", grad_mixed, value_rows, preferred_element_type=jnp.float32
    )
    row_inner = jnp.sum(soft_full * grad_soft, -1, keepdims=True)
    grad_scores = (soft_full * (grad_soft - row_inner)).astype(jnp.bfloat16)
    grad_queries = (
        jnp.einsum("nhqk,nkhe->nqhe", grad_scores, key_rows, preferred_element_type=jnp.float32)
        * factor
    )
    grad_keys = (
        jnp.einsum("nhqk,nqhe->nkhe", grad_scores, queries, preferred_element_type=jnp.float32)
        * factor
    )
    return (grad_queries, grad_keys, grad_values)


def apply_taps(extended, taps):
    pool_rows = (extended.shape[1] - 2) // 4
    total = extended[:, 0 : 4 * pool_rows : 4] * taps[:, 0]
    for tap_at in range(1, 5):
        total = total + extended[:, tap_at : tap_at + 4 * pool_rows : 4] * taps[:, tap_at]
    return total


def taps_back(extended, taps, grad_pool):
    pool_rows = grad_pool.shape[1]
    grad_ext = jnp.zeros(extended.shape, jnp.float32)
    tap_grads = []
    for tap_at in range(5):
        tap_rows = extended[:, tap_at : tap_at + 4 * pool_rows : 4]
        tap_grads.append(jnp.sum(tap_rows * grad_pool, axis=(0, 1)))
        grad_ext = grad_ext.at[:, tap_at : tap_at + 4 * pool_rows : 4].add(
            grad_pool * taps[:, tap_at]
        )
    return (grad_ext, jnp.stack(tap_grads, 1))


def by_sequence(
    inputs,
    question_count,
    question_at,
    local_proj,
    local_mixer,
    pooled_proj,
    pool_taps,
    pooled_mixer,
    expand_weight,
    reduce_weight,
    norm_gain,
    norm_shift,
    output_grad,
):
    docs_here, tok_here, width = inputs.shape
    layers = local_proj.shape[0]
    heads = width // HD
    half_win = LOCAL_WIN // 2
    seq_count = lax.axis_size("seq")
    seq_at = lax.axis_index("seq")
    length = tok_here * seq_count
    positions = seq_at * tok_here + jnp.arange(tok_here, dtype=jnp.int32)
    slots = jnp.arange(question_at.shape[1], dtype=jnp.int32)
    question = jnp.any(
        (question_at[:, :, None] == positions[None, None, :])
        & (slots[None, :, None] < question_count[:, None, None]),
        axis=1,
    )
    near_cols = seq_at * tok_here - half_win + jnp.arange(tok_here + 2 * half_win, dtype=jnp.int32)
    local_allowed = (
        (jnp.abs(positions[:, None] - near_cols[None, :]) <= half_win)
        & (near_cols[None, :] >= 0)
        & (near_cols[None, :] < length)
    )[None]
    pool_cols = jnp.arange(length // 4, dtype=jnp.int32)
    pool_allowed = (
        jnp.abs(pool_cols[None, None, :] - (positions // 4)[None, :, None]) <= POOL_WIN // 2
    ) | question[:, :, None]
    head_shape = (docs_here, tok_here, heads, HD)
    hidden_now = inputs.astype(jnp.float32)
    saved_all = []
    for layer_at in range(layers):
        in_rows = hidden_now.astype(jnp.bfloat16)
        local_heads = (
            mul_plain(as_rows(in_rows), local_proj[layer_at])
            .astype(jnp.bfloat16)
            .reshape(docs_here, tok_here, 3, heads, HD)
        )
        forward_near_kv = with_halo(local_heads[:, :, 1:], (("seq", 1),), half_win)
        local_result, local_lse = attend(
            local_heads[:, :, 0], forward_near_kv[:, :, 0], forward_near_kv[:, :, 1], local_allowed
        )
        local_mix = local_result.astype(jnp.bfloat16).reshape(docs_here, tok_here, width)
        first_sum = hidden_now + mul_plain(as_rows(local_mix), local_mixer[layer_at]).reshape(
            hidden_now.shape
        )
        first_norm = layer_norm(first_sum, norm_gain[layer_at, 0], norm_shift[layer_at, 0])
        second_in = first_norm.astype(jnp.bfloat16)
        pooled_heads = (
            mul_plain(as_rows(second_in), pooled_proj[layer_at])
            .astype(jnp.bfloat16)
            .reshape(docs_here, tok_here, 3, heads, HD)
        )
        prior_kv = from_behind(pooled_heads[:, tok_here - 2 :, 1:], "seq", 1)
        extended = jnp.concatenate([prior_kv, pooled_heads[:, :, 1:]], 1).astype(jnp.float32)
        forward_taps = pool_taps[layer_at].reshape(2, 5, heads, HD)
        pooled = apply_taps(extended, forward_taps).astype(jnp.bfloat16)
        forward_all_pooled = lax.all_gather(pooled, "seq", axis=1, tiled=True)
        pooled_result, pooled_lse = attend(
            pooled_heads[:, :, 0],
            forward_all_pooled[:, :, 0],
            forward_all_pooled[:, :, 1],
            pool_allowed,
        )
        pooled_mix = pooled_result.astype(jnp.bfloat16).reshape(docs_here, tok_here, width)
        second_sum = first_norm + mul_plain(as_rows(pooled_mix), pooled_mixer[layer_at]).reshape(
            hidden_now.shape
        )
        second_norm = layer_norm(second_sum, norm_gain[layer_at, 1], norm_shift[layer_at, 1])
        ffn_in = second_norm.astype(jnp.bfloat16)
        up_proj = mul_plain(as_rows(ffn_in), expand_weight[layer_at])
        activated = exact_gelu(up_proj).astype(jnp.bfloat16)
        third_sum = second_norm + mul_plain(activated, reduce_weight[layer_at]).reshape(
            hidden_now.shape
        )
        result = layer_norm(third_sum, norm_gain[layer_at, 2], norm_shift[layer_at, 2])
        forward_saved = SimpleNamespace(
            in_rows=in_rows,
            local_heads=local_heads,
            near_kv=forward_near_kv,
            local_lse=local_lse,
            local_mix=local_mix,
            first_sum=first_sum,
            second_in=second_in,
            pooled_heads=pooled_heads,
            extended=extended,
            saved_pool=forward_all_pooled,
            pooled_lse=pooled_lse,
            pooled_mix=pooled_mix,
            second_sum=second_sum,
            ffn_in=ffn_in,
            up_proj=up_proj,
            activated=activated,
            third_sum=third_sum,
        )
        hidden_now = result
        saved_all.append(forward_saved)
    outputs = hidden_now.astype(jnp.bfloat16)
    grad_now = output_grad.astype(jnp.float32)
    grads_list = [None] * layers
    for layer_at in reversed(range(layers)):
        backward_saved = saved_all[layer_at]
        gain_row = norm_gain[layer_at]
        bias_row = norm_shift[layer_at]
        taps = pool_taps[layer_at].reshape(2, 5, heads, HD)
        unused_third, pull_third = jax.vjp(
            layer_norm, backward_saved.third_sum, gain_row[2], bias_row[2]
        )
        grad_third, gain_third, bias_third = pull_third(grad_now)
        grad_down_in = as_rows(grad_third.astype(jnp.bfloat16))
        down_grad = mul_first(backward_saved.activated, grad_down_in)
        grad_act = mul_last(grad_down_in, reduce_weight[layer_at])
        unused_gelu, pull_gelu = jax.vjp(exact_gelu, backward_saved.up_proj)
        grad_up = pull_gelu(grad_act)[0].astype(jnp.bfloat16)
        up_grad = mul_first(as_rows(backward_saved.ffn_in), grad_up)
        grad_second = grad_third + mul_last(grad_up, expand_weight[layer_at]).reshape(
            grad_now.shape
        )
        unused_second, pull_second = jax.vjp(
            layer_norm, backward_saved.second_sum, gain_row[1], bias_row[1]
        )
        grad_mid, gain_second, bias_second = pull_second(grad_second)
        grad_pool_mix = as_rows(grad_mid.astype(jnp.bfloat16))
        out2_grad = mul_first(as_rows(backward_saved.pooled_mix), grad_pool_mix)
        grad_pool_out = (
            mul_last(grad_pool_mix, pooled_mixer[layer_at]).astype(jnp.bfloat16).reshape(head_shape)
        )
        all_pooled = backward_saved.saved_pool
        grad_pool_query, grad_pool_key, grad_pool_value = attend_back(
            backward_saved.pooled_heads[:, :, 0],
            all_pooled[:, :, 0],
            all_pooled[:, :, 1],
            pool_allowed,
            backward_saved.pooled_lse,
            grad_pool_out,
        )
        own_key = lax.psum_scatter(
            grad_pool_key.astype(jnp.bfloat16), "seq", scatter_dimension=1, tiled=True
        ).astype(jnp.float32)
        own_value = lax.psum_scatter(
            grad_pool_value.astype(jnp.bfloat16), "seq", scatter_dimension=1, tiled=True
        ).astype(jnp.float32)
        grad_ext, taps_grad = taps_back(
            backward_saved.extended, taps, jnp.stack([own_key, own_value], 2)
        )
        from_next = from_behind(grad_ext[:, :2].astype(jnp.bfloat16), "seq", -1).astype(jnp.float32)
        grad_kv_second = grad_ext[:, 2:].at[:, tok_here - 2 :].add(from_next)
        grad_heads_two = (
            jnp.concatenate([grad_pool_query[:, :, None], grad_kv_second], 2)
            .astype(jnp.bfloat16)
            .reshape(-1, 3 * width)
        )
        proj2_grad = mul_first(as_rows(backward_saved.second_in), grad_heads_two)
        grad_first = grad_mid + mul_last(grad_heads_two, pooled_proj[layer_at]).reshape(
            grad_now.shape
        )
        unused_first, pull_first = jax.vjp(
            layer_norm, backward_saved.first_sum, gain_row[0], bias_row[0]
        )
        grad_low, gain_first, bias_first = pull_first(grad_first)
        grad_local_mix = as_rows(grad_low.astype(jnp.bfloat16))
        out1_grad = mul_first(as_rows(backward_saved.local_mix), grad_local_mix)
        grad_local_out = (
            mul_last(grad_local_mix, local_mixer[layer_at]).astype(jnp.bfloat16).reshape(head_shape)
        )
        near_kv = backward_saved.near_kv
        grad_local_query, grad_near_key, grad_near_value = attend_back(
            backward_saved.local_heads[:, :, 0],
            near_kv[:, :, 0],
            near_kv[:, :, 1],
            local_allowed,
            backward_saved.local_lse,
            grad_local_out,
        )
        grad_near = jnp.stack([grad_near_key, grad_near_value], 2)
        rim_rows = jnp.concatenate(
            [grad_near[:, :half_win], grad_near[:, tok_here + half_win :]], 1
        )
        came_back = with_halo(rim_rows.astype(jnp.bfloat16), (("seq", 1),), half_win).astype(
            rim_rows.dtype
        )
        grad_kv_first = grad_near[:, half_win : half_win + tok_here]
        grad_kv_first = grad_kv_first.at[:, :half_win].add(came_back[:, :half_win])
        grad_kv_first = grad_kv_first.at[:, tok_here - half_win :].add(came_back[:, 3 * half_win :])
        grad_heads_one = (
            jnp.concatenate([grad_local_query[:, :, None], grad_kv_first], 2)
            .astype(jnp.bfloat16)
            .reshape(-1, 3 * width)
        )
        proj1_grad = mul_first(as_rows(backward_saved.in_rows), grad_heads_one)
        grad_bottom = grad_low + mul_last(grad_heads_one, local_proj[layer_at]).reshape(
            grad_now.shape
        )
        layer_grads = (
            proj1_grad,
            out1_grad,
            proj2_grad[:, :width],
            proj2_grad[:, width:],
            taps_grad.reshape(2, 5, width),
            out2_grad,
            up_grad,
            down_grad,
            jnp.stack([gain_first, gain_second, gain_third]),
            jnp.stack([bias_first, bias_second, bias_third]),
        )
        grad_now, layer_grads = (grad_bottom, layer_grads)
        grads_list[layer_at] = layer_grads
    stacked = [jnp.stack([layer_set[member] for layer_set in grads_list]) for member in range(10)]
    shards_all = (
        lax.psum_scatter(
            stacked[0].astype(jnp.bfloat16), "seq", scatter_dimension=2, tiled=True
        ).astype(jnp.float32),
        lax.psum_scatter(
            stacked[1].astype(jnp.bfloat16), "seq", scatter_dimension=1, tiled=True
        ).astype(jnp.float32),
        lax.psum_scatter(
            stacked[2].astype(jnp.bfloat16), "seq", scatter_dimension=2, tiled=True
        ).astype(jnp.float32),
        lax.psum_scatter(
            stacked[3].astype(jnp.bfloat16), "seq", scatter_dimension=2, tiled=True
        ).astype(jnp.float32),
        lax.psum_scatter(
            stacked[4].astype(jnp.bfloat16), "seq", scatter_dimension=3, tiled=True
        ).astype(jnp.float32),
        lax.psum_scatter(
            stacked[5].astype(jnp.bfloat16), "seq", scatter_dimension=1, tiled=True
        ).astype(jnp.float32),
        lax.psum_scatter(
            stacked[6].astype(jnp.bfloat16), "seq", scatter_dimension=2, tiled=True
        ).astype(jnp.float32),
        lax.psum_scatter(
            stacked[7].astype(jnp.bfloat16), "seq", scatter_dimension=1, tiled=True
        ).astype(jnp.float32),
        lax.psum_scatter(
            stacked[8].astype(jnp.bfloat16), "seq", scatter_dimension=2, tiled=True
        ).astype(jnp.float32),
        lax.psum_scatter(
            stacked[9].astype(jnp.bfloat16), "seq", scatter_dimension=2, tiled=True
        ).astype(jnp.float32),
    )
    stacked = (
        lax.psum(shards_all[0].astype(jnp.bfloat16), "doc").astype(jnp.float32),
        lax.psum(shards_all[1].astype(jnp.bfloat16), "doc").astype(jnp.float32),
        lax.psum(shards_all[2].astype(jnp.bfloat16), "doc").astype(jnp.float32),
        lax.psum(shards_all[3].astype(jnp.bfloat16), "doc").astype(jnp.float32),
        lax.psum(shards_all[4].astype(jnp.bfloat16), "doc").astype(jnp.float32),
        lax.psum(shards_all[5].astype(jnp.bfloat16), "doc").astype(jnp.float32),
        lax.psum(shards_all[6].astype(jnp.bfloat16), "doc").astype(jnp.float32),
        lax.psum(shards_all[7].astype(jnp.bfloat16), "doc").astype(jnp.float32),
        lax.psum(shards_all[8].astype(jnp.bfloat16), "doc").astype(jnp.float32),
        lax.psum(shards_all[9].astype(jnp.bfloat16), "doc").astype(jnp.float32),
    )
    return (
        outputs,
        grad_now,
        stacked[0],
        stacked[1],
        stacked[2],
        stacked[3],
        stacked[4],
        stacked[5],
        stacked[6],
        stacked[7],
        stacked[8],
        stacked[9],
    )


def solution(mesh):
    planes, places = mesh.shape["doc"], mesh.shape["seq"]

    def per_device(inputs, *others):
        docs_here, tok_here, _ = inputs.shape
        whole = docs_here == 4 and 2 * docs_here == places and planes == 4 and tok_here == 128
        return (by_chip if whole else by_sequence)(inputs, *others)

    return jax.shard_map(
        per_device,
        mesh=mesh,
        in_specs=(
            P("doc", "seq", None),
            P("doc"),
            P("doc", None),
            P(),
            P(),
            P(),
            P(),
            P(),
            P(),
            P(),
            P(),
            P(),
            P("doc", "seq", None),
        ),
        out_specs=(
            P("doc", "seq", None),
            P("doc", "seq", None),
            P(None, None, "seq"),
            P(None, "seq", None),
            P(None, None, "seq"),
            P(None, None, "seq"),
            P(None, None, None, "seq"),
            P(None, "seq", None),
            P(None, None, "seq"),
            P(None, "seq", None),
            P(None, None, "seq"),
            P(None, None, "seq"),
        ),
        check_vma=False,
    )
```
